32 devices in a mesh: dp: 16 (over z, y, x), tensor: 2 (over core).
Axes of the slice: x: 2, y: 2, z: 4, core: 2. Of those that a mesh axis runs over, the one named last changes fastest.
Arguments:
- tokens: bfloat16 [25216, 768], P(('dp', 'tensor')), may hold values from -6 to 6
- cotangent: bfloat16 [25216, 768], P(('dp', 'tensor')), may hold values from -6 to 6
- norm1_gain: bfloat16 [768], P(('dp', 'tensor')), may hold values from 0.25 to 1.75
- norm1_shift: bfloat16 [768], P(('dp', 'tensor')), may hold values from -3 to 3
- qkv_weight: bfloat16 [3, 768, 768], P(None, 'dp', 'tensor'), may hold values from -16 to 16
- qv_bias: bfloat16 [2, 2, 384], P(None, 'tensor', 'dp'), may hold values from -3 to 3
- out_weight: bfloat16 [768, 768], P('tensor', 'dp'), may hold values from -1.75 to 1.75
- out_bias: bfloat16 [768], P(('dp', 'tensor')), may hold values from -3 to 3
- norm2_gain: bfloat16 [768], P(('dp', 'tensor')), may hold values from 0.25 to 1.75
- norm2_shift: bfloat16 [768], P(('dp', 'tensor')), may hold values from -3 to 3
- up_weight: bfloat16 [768, 3072], P('dp', 'tensor'), may hold values from -0.21875 to 0.21875
- up_bias: bfloat16 [2, 1536], P('tensor', 'dp'), may hold values from -3 to 3
- down_weight: bfloat16 [3072, 768], P('tensor', 'dp'), may hold values from -0.15625 to 0.15625
- down_bias: bfloat16 [768], P(('dp', 'tensor')), may hold values from -3 to 3
Outputs:
- layer_out: bfloat16 [25216, 768], P(('dp', 'tensor'))
- input_grad: float32 [25216, 768], P(('dp', 'tensor'))
- grad_norm1_gain: float32 [768], P(('dp', 'tensor'))
- grad_norm1_shift: float32 [768], P(('dp', 'tensor'))
- grad_qkv_weight: float32 [3, 768, 768], P(None, 'dp', 'tensor')
- grad_qv_bias: float32 [2, 2, 384], P(None, 'tensor', 'dp')
- grad_out_weight: float32 [768, 768], P('tensor', 'dp')
- grad_out_bias: float32 [768], P(('dp', 'tensor'))
- grad_norm2_gain: float32 [768], P(('dp', 'tensor'))
- grad_norm2_shift: float32 [768], P(('dp', 'tensor'))
- grad_up_weight: float32 [768, 3072], P('dp', 'tensor')
- grad_up_bias: float32 [2, 1536], P('tensor', 'dp')
- grad_down_weight: float32 [3072, 768], P('tensor', 'dp')
- grad_down_bias: float32 [768], P(('dp', 'tensor'))
The draws below stay inside these ranges and needn't reach their ends.
All inputs are finite; a program needn't handle non-finite values.
Results may differ from the reference program's by a relative error of at most 0.018.
Values may be sent and summed in bfloat16 or wider, within the bound.
A program may use at most 128 MiB of HBM per device.

```python
import jax
import jax.numpy as jnp
from jax import lax

D = 768
H = 12
HD = 64
FF = 3072
SEQ = 197
IMAGES = 128
TOKENS = 25216
DT = 384
FT = 1536
N_TENSOR = 2


def draw_qkv_weight(key, part):
    base_key = jax.random.fold_in(jax.random.fold_in(key, 7), 0)
    base = jax.random.normal(base_key, (3, D, D), jnp.float32) * D ** (-0.5)
    return jnp.clip(base, -16.0, 16.0).astype(jnp.bfloat16)


def raised(values, stream_key, source, target, parts, factor):
    owner, partner = [(jnp.arange(values.shape[dim]) // (values.shape[dim] // parts)).reshape([-1 if axis == dim else 1 for axis in range(values.ndim)]) for dim in (source, target)]
    chosen = jax.random.permutation(stream_key, parts)[partner]
    strong = (owner == chosen) | (owner == (partner + parts // 2) % parts)
    return jnp.where(strong, factor * values, values)


def block_levels(rng, shape, cuts, least, top_value):
    gain = 1.0
    for axis_at, parts in cuts:
        heights = jax.random.uniform(jax.random.fold_in(jax.random.fold_in(rng, 6), axis_at), (parts,), jnp.float32, least / len(cuts), top_value / len(cuts))
        gain = gain * jnp.repeat(jnp.exp(heights), shape[axis_at] // parts).reshape((-1,) + (1,) * (len(shape) - 1 - axis_at))
    return gain


def scatter_about(rng, extent, scale, most, pieces=(), kind=jnp.bfloat16):
    values = jax.random.normal(rng, extent, jnp.float32) * scale
    if len(pieces) > 0:
        values = block_levels(rng, extent, pieces, -0.22, 0.18) * values
    return jnp.clip(values, min=-most, max=most).astype(kind)


def bell_draw_with(stream_key, dims, scale, bound, cuts, heavy, held_as=jnp.bfloat16):
    values = scale * jax.random.normal(stream_key, dims, jnp.float32)
    if cuts:
        values = values * block_levels(stream_key, dims, cuts, -0.22, 0.18)
    return jnp.clip(raised(values, jax.random.fold_in(stream_key, 3), *heavy), -bound, bound).astype(held_as)


def setup_inputs(seed: int = 0) -> dict:
    streams_of = jax.random.split(jax.random.key(seed), 15)
    return {
        "tokens": scatter_about(streams_of[0], (TOKENS, D), 1.0, 6.0, ((0, 32),)),
        "cotangent": bell_draw_with(streams_of[1], (TOKENS, D), 1.0, 6.0, ((0, 32),), (0, 1, 32, 2.75)),
        "norm1_gain": jnp.clip(1.0 + 0.15 * jax.random.normal(streams_of[2], (D,), jnp.float32), 0.25, 1.75).astype(jnp.bfloat16),
        "norm1_shift": scatter_about(streams_of[3], (D,), 0.5, 3.0, ((0, 32),)),
        "qkv_weight": draw_qkv_weight(jax.random.fold_in(streams_of[14], 71), 0),
        "qv_bias": scatter_about(streams_of[5], (2, N_TENSOR, DT), 0.5, 3.0, ((1, 2), (2, 16))),
        "out_weight": scatter_about(streams_of[6], (D, D), (D // 64) ** -0.5, 1.75, ((0, 2), (1, 16))),
        "out_bias": scatter_about(streams_of[7], (D,), 0.5, 3.0, ((0, 32),)),
        "norm2_gain": jnp.clip(1.0 + 0.15 * jax.random.normal(streams_of[8], (D,), jnp.float32), 0.25, 1.75).astype(jnp.bfloat16),
        "norm2_shift": scatter_about(streams_of[9], (D,), 0.5, 3.0, ((0, 32),)),
        "up_weight": scatter_about(streams_of[10], (D, FF), D ** -0.5, 0.21875, ((0, 16), (1, 2))),
        "up_bias": scatter_about(streams_of[11], (N_TENSOR, FT), 0.5, 3.0, ((0, 2), (1, 16))),
        "down_weight": scatter_about(streams_of[12], (FF, D), (FF // 2) ** -0.5, 0.15625, ((0, 2), (1, 16))),
        "down_bias": scatter_about(streams_of[13], (D,), 0.5, 3.0, ((0, 32),)),
    }


@jax.custom_vjp
def low(v):
    return lax.optimization_barrier(v.astype(jnp.bfloat16)).astype(jnp.float32)

@jax.custom_vjp
def low_back(v):
    return v

def low_keep(v):
    return (low(v), None)

def low_pass(kept, grad):
    return (grad,)

def back_keep(v):
    return (v, None)

def back_low(kept, grad):
    return (low(grad),)
low.defvjp(low_keep, low_pass)
low_back.defvjp(back_keep, back_low)

def normalize(values):
    centered = values - lax.optimization_barrier(jnp.mean(values, axis=-1, keepdims=True))
    inverse = lax.rsqrt(lax.optimization_barrier(jnp.mean(centered * centered, axis=-1, keepdims=True)) + 1e-06)
    return centered * inverse

def project(rows, matrix):
    return jnp.einsum('isd,de->ise', rows, matrix, precision=lax.Precision.HIGHEST)

def layer(block, params):
    gain_one, shift_one, qkv_mat, qv_vec, out_mat, out_vec, gain_two, shift_two, up_mat, up_vec, down_mat, down_vec = params
    images = block.shape[0]
    highest = lax.Precision.HIGHEST
    factor = HD ** (-0.5)
    h_one = low(normalize(block) * gain_one + shift_one)
    qv_rows = qv_vec.reshape(2, D)
    queries = low_back(low(project(h_one, qkv_mat[0]) + qv_rows[0]))
    keys = low_back(low(project(h_one, qkv_mat[1])))
    values = low_back(low(project(h_one, qkv_mat[2]) + qv_rows[1]))
    q_heads = queries.reshape(images, SEQ, H, HD)
    k_heads = keys.reshape(images, SEQ, H, HD)
    v_heads = values.reshape(images, SEQ, H, HD)
    scores = low_back(jnp.einsum('iqhd,ikhd->ihqk', q_heads, k_heads, precision=highest) * factor)
    probs = low(jax.nn.softmax(scores, axis=-1))
    attended = jnp.einsum('ihqk,ikhd->iqhd', probs, v_heads, precision=highest)
    attended = low_back(low(attended.reshape(images, SEQ, D)))
    branch_one = low_back(project(attended, out_mat) + out_vec)
    middle = block + branch_one
    h_two = low(normalize(middle) * gain_two + shift_two)
    pre_act = low_back(project(h_two, up_mat) + up_vec.reshape(FF))
    hidden = low(jax.nn.gelu(pre_act, approximate=False))
    branch_two = low_back(project(hidden, down_mat) + down_vec)
    return middle + branch_two

def reference(tokens, cotangent, norm1_gain, norm1_shift, qkv_weight, qv_bias, out_weight, out_bias, norm2_gain, norm2_shift, up_weight, up_bias, down_weight, down_bias):
    params = tuple((item.astype(jnp.float32) for item in (norm1_gain, norm1_shift, qkv_weight, qv_bias, out_weight, out_bias, norm2_gain, norm2_shift, up_weight, up_bias, down_weight, down_bias)))
    inputs = tokens.astype(jnp.float32)

    def forward(rows, weights):
        groups = rows.reshape(IMAGES // 16, 16, SEQ, D)
        run_block = jax.checkpoint(lambda block: layer(block, weights))
        return lax.map(run_block, groups).reshape(TOKENS, D)
    result, pull = jax.vjp(forward, inputs, params)
    grad_rows, grads = pull(cotangent.astype(jnp.float32))
    return (result.astype(jnp.bfloat16), grad_rows, grads[0], grads[1], grads[2], grads[3], grads[4], grads[5], grads[6], grads[7], grads[8], grads[9], grads[10], grads[11])
```

```python
import functools
from functools import partial
import jax
import jax.numpy as jnp
from jax import lax
from jax.experimental import pallas as pl
from jax.experimental.pallas import tpu as pltpu
from jax.sharding import PartitionSpec as P

MESH = pl.DeviceIdType.MESH
BF = jnp.bfloat16
F32 = jnp.float32
DMA = pltpu.SemaphoreType.DMA
HD = 64
SEQ = 197
SP = 208
QUAD = 256
EPS = 1e-06
X = Y = 2
ALL = slice(None)


def dot(a, b, ca=1, cb=0):
    return lax.dot_general(a, b, (((ca,), (cb,)), ((), ())), preferred_element_type=F32)


def remote(src, dst, send, recv, dev):
    return pltpu.make_async_remote_copy(
        src_ref=src, dst_ref=dst, send_sem=send, recv_sem=recv, device_id=dev, device_id_type=MESH
    )


def by_core(c, make, op):
    for core in range(2):

        @pl.when(c == core)
        def _(core=core):
            getattr(make(core), op)()


def center(x):
    d = x - jnp.mean(x, axis=-1, keepdims=True)
    r = lax.rsqrt(jnp.mean(d * d, axis=-1, keepdims=True) + EPS)
    return d * r, r


class Place:
    def __init__(self, zs):
        dp = lax.axis_index("dp")
        self.c = lax.axis_index("tensor")
        self.zs = zs
        self.z = dp // (X * Y)
        self.y = (dp // X) % Y
        self.x = dp % X
        self.dp = dp

    def dev(self, z, y, x, c):
        return {"dp": (z * Y + y) * X + x, "tensor": c}

    def zdev(self, k):
        return self.dev(lax.rem(self.z + k, self.zs), self.y, self.x, self.c)

    def xdev(self):
        return self.dev(self.z, self.y, 1 - self.x, self.c)

    def ydev(self):
        return self.dev(self.z, 1 - self.y, self.x, self.c)

    def cdev(self):
        return self.dev(self.z, self.y, self.x, 1 - self.c)

    def greet(self):
        barrier = pltpu.get_barrier_semaphore()
        peers = [self.xdev(), self.ydev(), self.cdev()] + [self.zdev(k) for k in range(1, self.zs)]
        for peer in peers:
            pl.semaphore_signal(barrier, inc=1, device_id=peer, device_id_type=MESH)
        pl.semaphore_wait(barrier, len(peers))


PIECES = (
    ("s", 0, 0, 128),
    ("a", 0, 0, 384),
    ("a", 1, 0, 384),
    ("a", 2, 0, 384),
    ("a", 3, 0, 384),
    ("b", 0, 0, 768),
    ("b", 0, 768, 768),
    ("b", 1, 0, 768),
    ("b", 1, 768, 768),
)
NP = len(PIECES)
HALF = {"a": 384, "b": 1536}


class Gather:
    def __init__(self, place, shards, fulls, sems):
        self.place, self.shards, self.fulls = place, shards, fulls
        self.zs, self.zr, self.fs, self.fr, self.gs, self.gr, self.ps, self.pr, self.ls = sems

    def full(self, p, idx):
        name, m, col, width = PIECES[p]
        ref = self.fulls[name]
        c = self.place.c
        if name == "s":
            return ref.at[(c,) + idx]
        cols = pl.ds(pl.multiple_of(c * HALF[name] + col, 128), width)
        return ref.at[(m,) + idx + (ALL, cols)]

    def own(self, p):
        name, m, col, width = PIECES[p]
        if name == "s":
            return self.shards[name]
        return self.shards[name].at[m, :, pl.ds(col, width)]

    def zcopy(self, p, k):
        pp = self.place
        return remote(
            self.own(p), self.full(p, (pp.z, pp.y, pp.x)), self.zs.at[p, k - 1], self.zr.at[p, k - 1], pp.zdev(k)
        )

    def local(self, p):
        pp = self.place
        return pltpu.make_async_copy(self.own(p), self.full(p, (pp.z, pp.y, pp.x)), self.ls.at[p])

    def first(self, p, core):
        pp = self.place
        s = self.full(p, (ALL, pp.y, pp.x))
        return remote(s, s, self.fs.at[p], self.fr.at[p], pp.xdev() if core == 0 else pp.ydev())

    def second(self, p, core):
        pp = self.place
        s = self.full(p, (ALL, pp.y, ALL) if core == 0 else (ALL, ALL, pp.x))
        return remote(s, s, self.gs.at[p], self.gr.at[p], pp.ydev() if core == 0 else pp.xdev())

    def pair(self, p):
        s = self.full(p, (ALL, ALL, ALL))
        return remote(s, s, self.ps.at[p], self.pr.at[p], self.place.cdev())

    def start_z(self, p):
        self.local(p).start()
        for k in range(1, self.place.zs):
            self.zcopy(p, k).start()

    def tick(self, t, ahead=2):
        c = self.place.c
        if t < NP:
            self.local(t).wait()
            for k in range(1, self.place.zs):
                self.zcopy(t, k).wait_recv()
            if t + ahead < NP:
                self.start_z(t + ahead)
            by_core(c, functools.partial(self.first, t), "start")
        if 0 <= t - 1 < NP:
            by_core(c, functools.partial(self.first, t - 1), "wait_recv")
            by_core(c, functools.partial(self.second, t - 1), "start")
        if 0 <= t - 2 < NP:
            by_core(c, functools.partial(self.second, t - 2), "wait_recv")
            self.pair(t - 2).start()
        if 0 <= t - 3 < NP:
            self.pair(t - 3).wait_recv()

    def finish(self):
        c = self.place.c
        for p in range(NP):
            for k in range(1, self.place.zs):
                self.zcopy(p, k).wait_send()
            by_core(c, functools.partial(self.first, p), "wait_send")
            by_core(c, functools.partial(self.second, p), "wait_send")
            self.pair(p).wait_send()


def forward_kernel(zs, images, *refs):
    (a_sh, b_sh, s_sh, tok) = refs[:4]
    outs = refs[4:17]
    (wa_o, wb_o, h1_o, qkv_o, p_o, att_o, mid_o, h2_o, hid_o, gp_o, lo_o, vec_o, upb_o) = outs
    (wa, wb, sv, h1, qkv, pbuf, att, mid, h2, hid, gp, lo, acc, psem, osem) = refs[17:32]
    sems = refs[32:]
    rows = images * SP
    place = Place(zs)
    n = zs * Y * X
    place.greet()
    g = Gather(place, {"a": a_sh, "b": b_sh, "s": s_sh}, {"a": wa, "b": wb, "s": sv}, sems)
    for p in range(2):
        g.start_z(p)
    for t in range(4):
        g.tick(t)

    cell = 768 // (2 * n)
    flat = sv[...].reshape(2 * n * 16, 128)
    lane = lax.broadcasted_iota(jnp.int32, (128, 768), 0)
    col = lax.broadcasted_iota(jnp.int32, (128, 768), 1)
    spread = dot(flat, (lax.rem(col, cell) == lane).astype(BF)).reshape(2 * n, 16, 768)
    who = lax.broadcasted_iota(jnp.int32, (2 * n, 16, 768), 0)
    kind = lax.broadcasted_iota(jnp.int32, (2 * n, 16, 768), 1)
    spot = lax.broadcasted_iota(jnp.int32, (2 * n, 16, 768), 2) // cell
    r_of, c_of = lax.rem(who, n), who // n
    mine = jnp.where(kind < 6, 2 * r_of + c_of, n * c_of + r_of)
    vec_o[...] = jnp.sum(jnp.where(mine == spot, spread, 0.0), axis=0)
    cell_up = 1536 // n
    pick_r = lax.broadcasted_iota(jnp.int32, (2 * n, 2 * n * 16), 0)
    pick_c = lax.broadcasted_iota(jnp.int32, (2 * n, 2 * n * 16), 1)
    up_rows = dot((pick_c == pick_r * 16 + 8).astype(BF), flat).astype(BF)
    lane = lax.broadcasted_iota(jnp.int32, (128, 3072), 0)
    col = lax.broadcasted_iota(jnp.int32, (128, 3072), 1)
    spread = dot(up_rows, (lax.rem(col, cell_up) == lane).astype(BF))
    who = lax.broadcasted_iota(jnp.int32, (2 * n, 3072), 0)
    spot = lax.broadcasted_iota(jnp.int32, (2 * n, 3072), 1) // cell_up
    upb_o[...] = jnp.sum(jnp.where(who == spot, spread, 0.0), axis=0, keepdims=True)

    def rows_of(i):
        return pl.ds(pl.multiple_of(i * SP, 16), SP)

    @pl.loop(0, images)
    def _(i):
        v, _r = center(tok[rows_of(i), :].astype(F32))
        h1[rows_of(i), :] = (v * vec_o[0:1, :] + vec_o[1:2, :]).astype(BF)

    def save(src, dst, k):
        pltpu.make_async_copy(src, dst, osem.at[k]).start()

    save(h1, h1_o, 0)

    def project(t):
        @pl.loop(0, 3)
        def _(j):
            cols = pl.ds(pl.multiple_of(j * 256, 256), 256)
            w = wa[t, :, :, :, :, cols].reshape(768, 256)
            r = dot(h1[...], w)
            if t == 0:
                r = (r + vec_o[6:7, cols]).astype(BF) * jnp.asarray(HD**-0.5, BF)
            elif t == 2:
                r = r + vec_o[7:8, cols]
            qkv[t, :, cols] = r.astype(BF)

    for t in range(3):
        g.tick(4 + t)
        project(t)
    save(qkv, qkv_o, 1)

    def attention(i):
        @pl.loop(0, 3)
        def _(j):
            cols = pl.ds(pl.multiple_of(j * QUAD, QUAD), QUAD)
            step = i * 3 + j
            slot = lax.rem(step, 2)
            head = lax.broadcasted_iota(jnp.int32, (SP, QUAD), 1) // HD
            q = qkv[0, rows_of(i), cols]
            zero = jnp.zeros_like(q)
            q4 = jnp.concatenate([jnp.where(head == h, q, zero) for h in range(4)], axis=0)
            s = dot(q4, qkv[1, rows_of(i), cols], 1, 1)
            key = lax.broadcasted_iota(jnp.int32, (4 * SP, SP), 1)
            s = jnp.where(key < SEQ, s, -1e30)
            e = jnp.exp(s - jnp.max(s, axis=-1, keepdims=True))
            p = (e * (1.0 / jnp.sum(e, axis=-1, keepdims=True))).astype(BF)

            @pl.when(step >= 2)
            def _():
                pltpu.make_async_copy(pbuf.at[slot], p_o.at[step - 2], psem.at[slot]).wait()

            pbuf[slot] = p
            pltpu.make_async_copy(pbuf.at[slot], p_o.at[step], psem.at[slot]).start()
            o4 = dot(p, qkv[2, rows_of(i), cols])
            o = jnp.zeros((SP, QUAD), F32)
            for h in range(4):
                o = jnp.where(head == h, o4[h * SP : (h + 1) * SP], o)
            att[rows_of(i), cols] = o.astype(BF)

    done = 7
    for i in range(images):
        attention(i)
        if i % 2 == 1 and done < 8:
            g.tick(done)
            done += 1
    while done < 8:
        g.tick(done)
        done += 1
    steps = images * 3
    for k in (steps - 2, steps - 1):
        pltpu.make_async_copy(pbuf.at[k % 2], p_o.at[k], psem.at[k % 2]).wait()
    save(att, att_o, 2)
    save(wa, wa_o, 3)

    for j in range(3):
        w = wa[3].reshape(768, 768)[j * 256 : (j + 1) * 256, :]
        cols = slice(j * 256, (j + 1) * 256)
        mid[:, cols] = tok[:, cols].astype(F32) + (dot(att[...], w, 1, 1) + vec_o[2:3, cols])

    @pl.loop(0, images)
    def _(i):
        v, _r = center(mid[rows_of(i), :])
        h2[rows_of(i), :] = (v * vec_o[3:4, :] + vec_o[4:5, :]).astype(BF)

    save(mid, mid_o, 4)
    save(h2, h2_o, 5)

    def expand(col0):
        @pl.loop(0, 6)
        def _(j):
            start = (j // 3) * 1536 + col0 + (j % 3) * 256
            cols = pl.ds(pl.multiple_of(start, 256), 256)
            w = wb[0, :, :, :, :, cols].reshape(768, 256)

            @pl.loop(0, images)
            def _(i):
                pre = dot(h2[rows_of(i), :], w) + upb_o[:, cols]
                cdf = 0.5 + 0.5 * lax.erf(pre * (0.5**0.5))
                pdf = jnp.exp(pre * pre * -0.5) * 0.3989422804014327
                hid[rows_of(i), cols] = (pre * cdf).astype(BF)
                gp[rows_of(i), cols] = (cdf + pre * pdf).astype(BF)

    g.tick(8)
    expand(0)
    g.tick(9)
    expand(768)
    save(hid, hid_o, 6)
    save(gp, gp_o, 7)

    def contract(col0, last):
        for j in range(3):
            cols = slice(j * 256, (j + 1) * 256)
            total = mid[:, cols] + vec_o[5:6, cols] if col0 == 0 else acc[:, cols]
            for half in range(2):
                fc = slice(half * 1536 + col0, half * 1536 + col0 + 768)
                w = wb[1, :, :, :, :, fc].reshape(768, 768)[j * 256 : (j + 1) * 256, :]
                total = total + dot(hid[:, fc], w, 1, 1)
            if last:
                lo[:, cols] = total.astype(BF)
            else:
                acc[:, cols] = total

    g.tick(10)
    contract(0, False)
    g.tick(11)
    save(wb, wb_o, 8)
    contract(768, True)
    save(lo, lo_o, 9)
    g.finish()
    pairs = (
        (h1, h1_o), (qkv, qkv_o), (att, att_o), (wa, wa_o), (mid, mid_o),
        (h2, h2_o), (hid, hid_o), (gp, gp_o), (wb, wb_o), (lo, lo_o),
    )
    for k, (src, dst) in enumerate(pairs):
        pltpu.make_async_copy(src, dst, osem.at[k]).wait()


def forward(a_sh, b_sh, s_sh, tok, zs, images):
    rows = images * SP
    n = zs * Y * X
    S = jax.ShapeDtypeStruct
    V = pltpu.VMEM
    outs = (
        S((4, zs, Y, X, 48, 768), BF), S((2, zs, Y, X, 48, 3072), BF), S((rows, 768), BF), S((3, rows, 768), BF),
        S((images * 3, 4 * SP, SP), BF), S((rows, 768), BF), S((rows, 768), F32), S((rows, 768), BF),
        S((rows, 3072), BF), S((rows, 3072), BF), S((rows, 768), BF), S((16, 768), F32), S((1, 3072), F32),
    )
    anys = pl.BlockSpec(memory_space=pl.ANY)
    vm = pl.BlockSpec(memory_space=pltpu.VMEM)
    return pl.pallas_call(
        functools.partial(forward_kernel, zs, images),
        out_shape=outs,
        in_specs=[vm] * 4,
        out_specs=[anys] * 11 + [vm] * 2,
        scratch_shapes=[
            V((4, zs, Y, X, 48, 768), BF), V((2, zs, Y, X, 48, 3072), BF), V((2, zs, Y, X, 16, 128), BF),
            V((rows, 768), BF), V((3, rows, 768), BF), V((2, 4 * SP, SP), BF), V((rows, 768), BF), V((rows, 768), F32),
            V((rows, 768), BF), V((rows, 3072), BF), V((rows, 3072), BF), V((rows, 768), BF), V((rows, 768), F32),
            DMA((2,)), DMA((10,)),
            DMA((NP, zs - 1)), DMA((NP, zs - 1)), DMA((NP,)), DMA((NP,)), DMA((NP,)), DMA((NP,)), DMA((NP,)), DMA((NP,)), DMA((NP,)),
        ],
        compiler_params=pltpu.CompilerParams(collective_id=1, has_side_effects=True, vmem_limit_bytes=60 * 2**20),
        name="gather_forward",
    )(a_sh, b_sh, s_sh, tok)


def pack_small(n1g, n1s, ob, n2g, n2s, db, qv, upb):
    cells = [n1g, n1s, ob, n2g, n2s, db, qv[0, 0], qv[1, 0]]
    parts = [jnp.pad(v, (0, 128 - v.shape[0])) for v in cells] + [jnp.pad(upb[0], (0, 128 - upb.shape[1]))]
    return jnp.pad(jnp.stack(parts), ((0, 7), (0, 0)))


def pad_rows(v, images):
    return jnp.pad(v.reshape(images, SEQ, v.shape[1]), ((0, 0), (0, SP - SEQ), (0, 0))).reshape(images * SP, v.shape[1])


PLAN = {
    "dn10": [(0, 1)],
    "pre0": [(1, 1)],
    "pre2": [(0, 2)],
    "up00": [(0, 3)],
    "up01": [(2, 1)],
    "up11": [(3, 1)],
    "dh20": [(1, 2)],
    "dh21": [(0, 4)],
    "dh22": [(1, 3)],
    "out": [(2, 2), (1, 4)],
    "datt": [(4, 1), (2, 3)],
    "attn0": [(3, 2), (2, 4)],
    "attn1": [(3, 3), (4, 2)],
    "attn2": [(3, 4), (4, 3)],
    "attn3": [(4, 4)],
    "qkv1": [(5, 1)],
    "qkv2": [(6, 1)],
    "dh10": [(7, 1), (5, 2)],
    "dh11": [(6, 2), (5, 3)],
    "dh12": [(7, 2), (5, 4), (6, 3)],
    "small": [(8, 1), (6, 4), (7, 3), (8, 2), (7, 4), (8, 3), (8, 4)],
}


SPIECES = (
    ("b", 1, 0, 768),
    ("b", 1, 768, 768),
    ("b", 0, 0, 768),
    ("b", 0, 768, 768),
    ("a", 3, 0, 384),
    ("a", 0, 0, 384),
    ("a", 1, 0, 384),
    ("a", 2, 0, 384),
    ("s", 0, 0, 128),
)
NS = len(SPIECES)


class Scatter:
    def __init__(self, place, gdn, gout, gs, wb, pb, pa, psm, rb, ra, rs, outs, sems):
        self.place = place
        self.gdn, self.gout, self.gs_, self.wb = gdn, gout, gs, wb
        self.pbuf = {"b": pb, "a": pa, "s": psm}
        self.rbuf = {"b": rb, "a": ra, "s": rs}
        self.outs = outs
        self.s_send, self.s_recv, self.z_send, self.z_recv = sems

    def index(self, p):
        return p if p < 4 else (p - 4 if p < 8 else 0)

    def part(self, p, own):
        if p < 2:
            return self.gdn.at[p, own]
        if p < 4:
            cols = pl.ds(pl.multiple_of((p - 2) * 1536 + own * 768, 128), 768)
            return self.wb.at[1, :, :, :, :, cols]
        if p == 4:
            return self.gout.at[own]
        if p < 8:
            k = p - 5
            return self.gdn.at[k // 2, own, :, :, :, :, pl.ds((k % 2) * 384, 384)]
        return self.gs_.at[own]

    def precv(self, p):
        return self.pbuf[SPIECES[p][0]].at[self.index(p)]

    def recv(self, p, k):
        return self.rbuf[SPIECES[p][0]][k].at[self.index(p)]

    def pair(self, p):
        return remote(self.part(p, 0), self.precv(p), self.s_send.at[p, 0], self.s_recv.at[p, 0], self.place.cdev())

    def one(self, p, core):
        pp, s = self.place, self.part(p, 1)
        src = s.at[:, 1 - pp.y, :] if core == 0 else s.at[:, :, 1 - pp.x]
        return remote(src, self.recv(p, 0), self.s_send.at[p, 1], self.s_recv.at[p, 1], pp.ydev() if core == 0 else pp.xdev())

    def two(self, p, core):
        pp, s = self.place, self.part(p, 1)
        src = s.at[:, pp.y, 1 - pp.x] if core == 0 else s.at[:, 1 - pp.y, pp.x]
        return remote(src, self.recv(p, 1), self.s_send.at[p, 2], self.s_recv.at[p, 2], pp.xdev() if core == 0 else pp.ydev())

    def three(self, p, k):
        pp, s = self.place, self.part(p, 1)
        to = lax.rem(pp.z + k, pp.zs)
        return remote(
            s.at[to, pp.y, pp.x], self.recv(p, 2).at[k - 1], self.z_send.at[p, k - 1], self.z_recv.at[p, k - 1], pp.zdev(k)
        )

    def stage(self, p, k):
        pp = self.place
        c = pp.c
        zs = pp.zs
        kind = F32 if p == 8 else BF
        s = self.part(p, 1)
        if k == 0:
            self.pair(p).start()
        elif k == 1:
            self.pair(p).wait_recv()
            r = self.precv(p)
            for zz in range(zs):
                s[zz] = (s[zz].astype(F32) + r[zz].astype(F32)).astype(kind)
            by_core(c, functools.partial(self.one, p), "start")
        elif k == 2:
            by_core(c, functools.partial(self.one, p), "wait_recv")
            r = self.recv(p, 0)
            for zz in range(zs):
                for j in range(2):
                    yi, xi = jnp.where(c == 0, pp.y, j), jnp.where(c == 0, j, pp.x)
                    s[zz, yi, xi] = (s[zz, yi, xi].astype(F32) + r[zz, j].astype(F32)).astype(kind)
            by_core(c, functools.partial(self.two, p), "start")
        elif k == 3:
            by_core(c, functools.partial(self.two, p), "wait_recv")
            r = self.recv(p, 1)
            for zz in range(zs):
                s[zz, pp.y, pp.x] = (s[zz, pp.y, pp.x].astype(F32) + r[zz].astype(F32)).astype(kind)
            for k in range(1, zs):
                self.three(p, k).start()
        else:
            r = self.recv(p, 2)
            total = s[pp.z, pp.y, pp.x].astype(F32)
            for k in range(1, zs):
                self.three(p, k).wait_recv()
                total = total + r[k - 1].astype(F32)
            name, m, col, width = SPIECES[p]
            if name == "s":
                self.outs[name][...] = total
            else:
                self.outs[name][m, :, pl.ds(col, width)] = total
            self.pair(p).wait_send()
            by_core(c, functools.partial(self.one, p), "wait_send")
            by_core(c, functools.partial(self.two, p), "wait_send")
            for k in range(1, zs):
                self.three(p, k).wait_send()


def backward_kernel(zs, images, plan, *refs):
    (wa_i, wb_i, h1_i, qkv_i, p_i, att_i, mid_i, h2_i, hid_i, gp_i, tok_i, cot_i, vec) = refs[:13]
    dx_o, ga_o, gb_o, gs_o = refs[13:17]
    (wa, wb, cot, h2, qkv, att, mid, dh, dpre, db, hidt, pt, xt, yt, vg, ug, gdn, gout, gs) = refs[17:36]
    pb, pa, psm = refs[36:39]
    rb, ra, rs = refs[39:42], refs[42:45], refs[45:48]
    lsem, hsem, psem = refs[48:51]
    sems = refs[51:]
    n = zs * Y * X
    rows = images * SP
    place = Place(zs)
    c = place.c
    sc = Scatter(place, gdn, gout, gs, wb, pb, pa, psm, rb, ra, rs, {"a": ga_o, "b": gb_o, "s": gs_o}, sems)

    loads = {
        "cot": (cot_i, cot), "dn": (wb_i.at[1], wb.at[1]), "gp": (gp_i, dpre), "h2": (h2_i, h2), "up": (wb_i.at[0], wb.at[0]),
        "mid": (mid_i, mid), "att": (att_i, att), "wa": (wa_i, wa), "qkv": (qkv_i, qkv), "h1": (h1_i, cot), "tok": (tok_i, h2),
    }
    names = list(loads)

    def load(name):
        src, dst = loads[name]
        return pltpu.make_async_copy(src, dst, lsem.at[names.index(name)])

    def hcols(step):
        own = (step // 3) % 2
        half = jnp.where(own == 1, c, 1 - c)
        return pl.ds(pl.multiple_of(half * 1536 + (step // 6) * 768 + (step % 3) * 256, 256), 256)

    def htile(step):
        slot = step % 3
        return pltpu.make_async_copy(hid_i.at[:, hcols(step)], hidt.at[slot], hsem.at[slot])

    load("cot").start()
    for k in range(2):
        htile(k).start()
    for name in ("dn", "gp", "h2", "up", "mid", "att", "wa", "qkv"):
        load(name).start()
    place.greet()

    def after(key):
        for p, k in plan.get(key, ()):
            sc.stage(p, k)

    def rows_of(i):
        return pl.ds(pl.multiple_of(i * SP, 16), SP)

    def cut(v):
        return v.reshape(zs, Y, X, 48, v.shape[1])

    vg[...] = jnp.zeros_like(vg)
    load("cot").wait()
    xt[...] = cot[...].T
    vg[5:6, :] = jnp.sum(cot[...].astype(F32), axis=0, keepdims=True)

    for piece in range(2):
        for own in range(2):

            @pl.loop(0, 3)
            def _(j, piece=piece, own=own):
                step = piece * 6 + own * 3 + j
                htile(step).wait()

                @pl.when(step + 2 < 12)
                def _():
                    htile(step + 2).start()

                gdn[piece, own, :, :, :, :, pl.ds(pl.multiple_of(j * 256, 256), 256)] = cut(
                    dot(xt[...], hidt[step % 3]).astype(BF)
                )

            if own == 0:
                sc.stage(piece, 0)
            after(f"dn{piece}{own}")

    load("dn").wait()
    load("gp").wait()
    for part in range(4):

        @pl.loop(0, 3)
        def _(j, part=part):
            cols = pl.ds(pl.multiple_of(part * 768 + j * 256, 256), 256)
            w = wb[1, :, :, :, :, cols].reshape(768, 256)
            d = (dot(cot[...], w) * dpre[:, cols].astype(F32)).astype(BF)
            dpre[:, cols] = d
            ug[:, cols] = jnp.sum(d.astype(F32), axis=0, keepdims=True)

        after(f"pre{part}")
    load("h2").wait()
    yt[...] = h2[...].T
    load("tok").start()
    for piece in range(2):
        for own in range(2):

            @pl.loop(0, 3)
            def _(j, piece=piece, own=own):
                half = c if own == 1 else 1 - c
                cols = pl.ds(pl.multiple_of(half * 1536 + piece * 768 + j * 256, 256), 256)
                dest = pl.ds(pl.multiple_of(piece * 1536 + own * 768 + j * 256, 256), 256)
                wb[1, :, :, :, :, dest] = cut(dot(yt[...], dpre[:, cols]).astype(BF))

            if own == 0:
                sc.stage(2 + piece, 0)
            after(f"up{piece}{own}")

    load("up").wait()
    for j in range(3):
        w = wb[0].reshape(768, 3072)[j * 256 : (j + 1) * 256, :]
        dh[:, j * 256 : (j + 1) * 256] = dot(dpre[...], w, 1, 1)
        after(f"dh2{j}")
    load("mid").wait()

    @pl.loop(0, images)
    def _(i):
        v, r = center(mid[rows_of(i), :])
        g = dh[rows_of(i), :]
        vg[3:4, :] += jnp.sum(g * v, axis=0, keepdims=True)
        vg[4:5, :] += jnp.sum(g, axis=0, keepdims=True)
        dn = g * vec[3:4, :]
        d = cot[rows_of(i), :].astype(F32) + r * (
            dn - jnp.mean(dn, axis=-1, keepdims=True) - v * jnp.mean(dn * v, axis=-1, keepdims=True)
        )
        dh[rows_of(i), :] = d
        low = d.astype(BF)
        db[rows_of(i), :] = low
        vg[2:3, :] += jnp.sum(low.astype(F32), axis=0, keepdims=True)

    load("h1").start()
    after("norm2")
    xt[...] = db[...].T
    load("att").wait()
    for h in range(2):
        own = jnp.where(c == h, 1, 0)
        gout[own] = cut(dot(xt[...], att[:, h * 384 : (h + 1) * 384]).astype(BF))
    sc.stage(4, 0)
    after("out")
    load("wa").wait()

    @pl.loop(0, 3)
    def _(j):
        cols = pl.ds(pl.multiple_of(j * 256, 256), 256)
        att[:, cols] = dot(db[...], wa[3, :, :, :, :, cols].reshape(768, 256)).astype(BF)

    after("datt")
    load("qkv").wait()

    def ptile(step):
        return pltpu.make_async_copy(p_i.at[step], pt.at[step % 2], psem.at[step % 2])

    ptile(0).start()
    total = images * 3
    for i in range(images):

        @pl.loop(0, 3)
        def _(j, i=i):
            cols = pl.ds(pl.multiple_of(j * QUAD, QUAD), QUAD)
            step = i * 3 + j
            ptile(step).wait()

            @pl.when(step + 1 < total)
            def _():
                ptile(step + 1).start()

            head = lax.broadcasted_iota(jnp.int32, (SP, QUAD), 1) // HD
            q, k, v, do = qkv[0, rows_of(i), cols], qkv[1, rows_of(i), cols], qkv[2, rows_of(i), cols], att[rows_of(i), cols]
            zero = jnp.zeros_like(q)
            q4 = jnp.concatenate([jnp.where(head == h, q, zero) for h in range(4)], axis=0)
            do4 = jnp.concatenate([jnp.where(head == h, do, zero) for h in range(4)], axis=0)
            p = pt[step % 2]
            dp = dot(do4, v, 1, 1)
            dv = dot(p, do4, 0, 0)
            pf = p.astype(F32)
            ds = (pf * (dp - jnp.sum(pf * dp, axis=-1, keepdims=True))).astype(BF)
            dq4 = dot(ds, k)
            dk = dot(ds, q4, 0, 0)
            dq = jnp.zeros((SP, QUAD), F32)
            for h in range(4):
                dq = jnp.where(head == h, dq4[h * SP : (h + 1) * SP], dq)
            qkv[0, rows_of(i), cols] = (dq * HD**-0.5).astype(BF)
            qkv[1, rows_of(i), cols] = dk.astype(BF)
            qkv[2, rows_of(i), cols] = dv.astype(BF)

        after(f"attn{i}")

    load("h1").wait()
    yt[...] = cot[...].T
    vg[6:7, :] = jnp.sum(qkv[0].astype(F32), axis=0, keepdims=True)
    vg[7:8, :] = jnp.sum(qkv[2].astype(F32), axis=0, keepdims=True)
    for t in range(3):
        for h in range(2):
            own = jnp.where(c == h, 1, 0)
            gdn[t // 2, own, :, :, :, :, (t % 2) * 384 : (t % 2) * 384 + 384] = cut(
                dot(yt[...], qkv[t, :, h * 384 : (h + 1) * 384]).astype(BF)
            )
        sc.stage(5 + t, 0)
        after(f"qkv{t}")

    for j in range(3):
        cols = slice(j * 256, (j + 1) * 256)
        sum_ = None
        for t in range(3):
            w = wa[t].reshape(768, 768)[cols, :]
            r = dot(qkv[t], w, 1, 1)
            sum_ = r if sum_ is None else sum_ + r
        mid[:, cols] = sum_
        after(f"dh1{j}")
    load("tok").wait()

    @pl.loop(0, images)
    def _(i):
        v, r = center(h2[rows_of(i), :].astype(F32))
        g = mid[rows_of(i), :]
        vg[0:1, :] += jnp.sum(g * v, axis=0, keepdims=True)
        vg[1:2, :] += jnp.sum(g, axis=0, keepdims=True)
        dn = g * vec[0:1, :]
        mid[rows_of(i), :] = dh[rows_of(i), :] + r * (
            dn - jnp.mean(dn, axis=-1, keepdims=True) - v * jnp.mean(dn * v, axis=-1, keepdims=True)
        )

    done = pltpu.make_async_copy(mid, dx_o, lsem.at[len(names)])
    done.start()

    def two_parts(v):
        hi = v.astype(BF)
        return hi, (v - hi.astype(F32)).astype(BF)

    cell = 768 // (2 * n)
    who = lax.broadcasted_iota(jnp.int32, (2 * n, 16, 768), 0)
    kind = lax.broadcasted_iota(jnp.int32, (2 * n, 16, 768), 1)
    spot = lax.broadcasted_iota(jnp.int32, (2 * n, 16, 768), 2) // cell
    r_of, c_of = lax.rem(who, n), who // n
    mine = jnp.where(kind < 6, 2 * r_of + c_of, n * c_of + r_of)
    mixed = jnp.where(mine == spot, vg[...][None], 0.0).reshape(2 * n * 16, 768)
    pick = (lax.rem(lax.broadcasted_iota(jnp.int32, (768, 128), 0), cell) == lax.broadcasted_iota(jnp.int32, (768, 128), 1)).astype(BF)
    small = sum(dot(part, pick) for part in two_parts(mixed)).reshape(2 * n, 16, 128)
    cell_up = 1536 // n
    who = lax.broadcasted_iota(jnp.int32, (2 * n, 3072), 0)
    spot = lax.broadcasted_iota(jnp.int32, (2 * n, 3072), 1) // cell_up
    mixed = jnp.where(who == spot, ug[...], 0.0)
    pick = (lax.rem(lax.broadcasted_iota(jnp.int32, (3072, 128), 0), cell_up) == lax.broadcasted_iota(jnp.int32, (3072, 128), 1)).astype(BF)
    up_part = sum(dot(part, pick) for part in two_parts(mixed)).reshape(2 * n, 1, 128)
    kind = lax.broadcasted_iota(jnp.int32, (2 * n, 16, 128), 1)
    small = jnp.where(kind == 8, up_part, small).reshape(2, zs, Y, X, 16, 128)
    for h in range(2):
        gs[jnp.where(c == h, 1, 0)] = small[h]
    sc.stage(8, 0)
    after("small")
    done.wait()


def backward(saved, tok, cot, vec, zs, images, plan):
    rows = images * SP
    S = jax.ShapeDtypeStruct
    V = pltpu.VMEM
    dims = (zs, Y, X)
    anys = pl.BlockSpec(memory_space=pl.ANY)
    vm = pl.BlockSpec(memory_space=pltpu.VMEM)
    return pl.pallas_call(
        functools.partial(backward_kernel, zs, images, plan),
        out_shape=(S((rows, 768), F32), S((4, 48, 384), F32), S((2, 48, 1536), F32), S((16, 128), F32)),
        in_specs=[anys] * 12 + [vm],
        out_specs=[anys] + [vm] * 3,
        scratch_shapes=[
            V((4,) + dims + (48, 768), BF), V((2,) + dims + (48, 3072), BF), V((rows, 768), BF), V((rows, 768), BF),
            V((3, rows, 768), BF), V((rows, 768), BF), V((rows, 768), F32), V((rows, 768), F32), V((rows, 3072), BF),
            V((rows, 768), BF), V((3, rows, 256), BF), V((2, 4 * SP, SP), BF), V((768, rows), BF), V((768, rows), BF),
            V((16, 768), F32), V((1, 3072), F32),
            V((2, 2) + dims + (48, 768), BF), V((2,) + dims + (48, 384), BF), V((2,) + dims + (16, 128), F32),
            V((4,) + dims + (48, 768), BF), V((4,) + dims + (48, 384), BF), V((1,) + dims + (16, 128), F32),
            V((4, zs, 2, 48, 768), BF), V((4, zs, 48, 768), BF), V((4, zs - 1, 48, 768), BF),
            V((4, zs, 2, 48, 384), BF), V((4, zs, 48, 384), BF), V((4, zs - 1, 48, 384), BF),
            V((1, zs, 2, 16, 128), F32), V((1, zs, 16, 128), F32), V((1, zs - 1, 16, 128), F32),
            DMA((12,)), DMA((3,)), DMA((2,)),
            DMA((NS, 3)), DMA((NS, 3)), DMA((NS, zs - 1)), DMA((NS, zs - 1)),
        ],
        compiler_params=pltpu.CompilerParams(collective_id=2, has_side_effects=True, vmem_limit_bytes=60 * 2**20),
        name="backward_scatter",
    )(*saved, tok, cot, vec)


def normalize(values):
    centered = values - jnp.mean(values, axis=-1, keepdims=True)
    inverse = lax.rsqrt(jnp.mean(centered * centered, axis=-1, keepdims=True) + EPS)
    return (centered * inverse, inverse)


def norm_back(grad_out, normed, inverse, gain):
    d_normed = grad_out * gain
    grad_in = inverse * (
        d_normed
        - jnp.mean(d_normed, axis=-1, keepdims=True)
        - normed * jnp.mean(d_normed * normed, axis=-1, keepdims=True)
    )
    return (grad_in, jnp.sum(grad_out * normed, axis=0), jnp.sum(grad_out, axis=0))


def gather_rows(rows):
    return lax.all_gather(rows, "tensor", axis=0, tiled=True)


def sum_rows(terms):
    return lax.psum_scatter(
        terms.astype(jnp.bfloat16), "tensor", scatter_dimension=0, tiled=True
    ).astype(jnp.float32)


def gather_grads(rows):
    return lax.all_gather(rows, "tensor", axis=0, tiled=True)


def sum_grads(terms):
    return lax.psum_scatter(
        terms.astype(jnp.bfloat16), "tensor", scatter_dimension=0, tiled=True
    ).astype(jnp.float32)


def split_heads(matrix):
    return matrix.reshape(matrix.shape[0] // SEQ, SEQ, matrix.shape[1] // HD, HD)


def attend(queries, keys, values):
    scores = jnp.einsum(
        "iqhd,ikhd->ihqk", queries, keys, preferred_element_type=jnp.float32
    ) * HD ** (-0.5)
    row_top = jnp.max(scores, axis=-1, keepdims=True)
    shifted = jnp.exp(scores - row_top)
    row_total = jnp.sum(shifted, axis=-1, keepdims=True)
    probs = (shifted / row_total).astype(jnp.bfloat16)
    attended = jnp.einsum("ihqk,ikhd->iqhd", probs, values, preferred_element_type=jnp.float32)
    return (attended.astype(jnp.bfloat16), row_top + jnp.log(row_total))


def attend_back(queries, keys, values, log_total, d_attended):
    factor = HD ** (-0.5)
    scores = (
        jnp.einsum("iqhd,ikhd->ihqk", queries, keys, preferred_element_type=jnp.float32) * factor
    )
    probs = jnp.exp(scores - log_total)
    probs_low = probs.astype(jnp.bfloat16)
    grad_values = jnp.einsum(
        "ihqk,iqhd->ikhd", probs_low, d_attended, preferred_element_type=jnp.float32
    ).astype(jnp.bfloat16)
    d_probs = jnp.einsum("iqhd,ikhd->ihqk", d_attended, values, preferred_element_type=jnp.float32)
    d_scores = (probs * (d_probs - jnp.sum(probs * d_probs, axis=-1, keepdims=True))).astype(
        jnp.bfloat16
    )
    grad_queries = (
        jnp.einsum("ihqk,ikhd->iqhd", d_scores, keys, preferred_element_type=jnp.float32) * factor
    ).astype(jnp.bfloat16)
    grad_keys = (
        jnp.einsum("ihqk,iqhd->ikhd", d_scores, queries, preferred_element_type=jnp.float32)
        * factor
    ).astype(jnp.bfloat16)
    return (grad_queries, grad_keys, grad_values)


def local(
    tokens,
    cotangent,
    norm1_gain,
    norm1_shift,
    qkv_weight,
    qv_bias,
    out_weight,
    out_bias,
    norm2_gain,
    norm2_shift,
    up_weight,
    up_bias,
    down_weight,
    down_bias,
):
    small_full = (
        lax.all_gather(norm1_gain, ("dp", "tensor"), axis=0, tiled=True),
        lax.all_gather(norm1_shift, ("dp", "tensor"), axis=0, tiled=True),
        lax.all_gather(out_bias, ("dp", "tensor"), axis=0, tiled=True),
        lax.all_gather(norm2_gain, ("dp", "tensor"), axis=0, tiled=True),
        lax.all_gather(norm2_shift, ("dp", "tensor"), axis=0, tiled=True),
        lax.all_gather(down_bias, ("dp", "tensor"), axis=0, tiled=True),
    )
    gain_one, shift_one, out_vec, gain_two, shift_two, down_vec = [
        item.astype(jnp.float32) for item in small_full
    ]
    qkv_full, qv_full, out_full = (
        lax.all_gather(qkv_weight, "dp", axis=1, tiled=True),
        lax.all_gather(qv_bias, "dp", axis=2, tiled=True),
        lax.all_gather(out_weight, "dp", axis=1, tiled=True),
    )
    inputs = tokens.astype(jnp.float32)
    normed_one, inverse_one = normalize(inputs)
    h_one = gather_rows((normed_one * gain_one + shift_one).astype(jnp.bfloat16))
    projected = jnp.einsum("gd,tde->tge", h_one, qkv_full, preferred_element_type=jnp.float32)
    qv_rows = qv_full.astype(jnp.float32)
    queries = split_heads((projected[0] + qv_rows[0, 0]).astype(jnp.bfloat16))
    keys = split_heads(projected[1].astype(jnp.bfloat16))
    values = split_heads((projected[2] + qv_rows[1, 0]).astype(jnp.bfloat16))
    attended_heads, log_total = attend(queries, keys, values)
    group_rows = h_one.shape[0]
    attended = attended_heads.reshape(group_rows, qkv_full.shape[2])
    branch_one = sum_rows(jnp.dot(attended, out_full, preferred_element_type=jnp.float32)) + out_vec
    middle = inputs + branch_one
    up_full, up_vec, down_full = (
        lax.all_gather(up_weight, "dp", axis=0, tiled=True),
        lax.all_gather(up_bias, "dp", axis=1, tiled=True),
        lax.all_gather(down_weight, "dp", axis=1, tiled=True),
    )
    normed_two, inverse_two = normalize(middle)
    h_two = gather_rows((normed_two * gain_two + shift_two).astype(jnp.bfloat16))
    pre_act = jnp.dot(h_two, up_full, preferred_element_type=jnp.float32) + up_vec[0].astype(
        jnp.float32
    )
    hidden = jax.nn.gelu(pre_act, approximate=False).astype(jnp.bfloat16)
    branch_two = sum_rows(jnp.dot(hidden, down_full, preferred_element_type=jnp.float32)) + down_vec
    layer_out = (middle + branch_two).astype(jnp.bfloat16)
    grad_rows = cotangent.astype(jnp.float32)
    grad_down_bias = jnp.sum(grad_rows, axis=0)
    cot_all = gather_grads(cotangent)
    grad_down = jnp.einsum("gf,gd->fd", hidden, cot_all, preferred_element_type=jnp.float32)
    d_hidden = jnp.einsum("gd,fd->gf", cot_all, down_full, preferred_element_type=jnp.float32)
    gelu_out, gelu_back = jax.vjp(partial(jax.nn.gelu, approximate=False), pre_act)
    d_pre = gelu_back(d_hidden)[0].astype(jnp.bfloat16)
    grad_up_bias = jnp.sum(d_pre.astype(jnp.float32), axis=0)[None, :]
    grad_up = jnp.einsum("gd,gf->df", h_two, d_pre, preferred_element_type=jnp.float32)
    d_h_two = sum_grads(jnp.einsum("gf,df->gd", d_pre, up_full, preferred_element_type=jnp.float32))
    d_middle, grad_gain_two, grad_shift_two = norm_back(d_h_two, normed_two, inverse_two, gain_two)
    d_middle = d_middle + grad_rows
    d_branch = d_middle.astype(jnp.bfloat16)
    grad_out_bias = jnp.sum(d_branch.astype(jnp.float32), axis=0)
    branch_all = gather_grads(d_branch)
    grad_out = jnp.einsum("ge,gd->ed", attended, branch_all, preferred_element_type=jnp.float32)
    d_attended = jnp.einsum(
        "gd,ed->ge", branch_all, out_full, preferred_element_type=jnp.float32
    ).astype(jnp.bfloat16)
    grad_queries, grad_keys, grad_values = attend_back(
        queries, keys, values, log_total, split_heads(d_attended)
    )
    width = qkv_full.shape[2]
    grad_stack = jnp.stack(
        [
            grad_queries.reshape(group_rows, width),
            grad_keys.reshape(group_rows, width),
            grad_values.reshape(group_rows, width),
        ]
    )
    grad_qv = jnp.stack(
        [
            jnp.sum(grad_stack[0].astype(jnp.float32), axis=0),
            jnp.sum(grad_stack[2].astype(jnp.float32), axis=0),
        ]
    )[:, None, :]
    grad_qkv = jnp.einsum("gd,tge->tde", h_one, grad_stack, preferred_element_type=jnp.float32)
    d_h_one = sum_grads(
        jnp.einsum("tge,tde->gd", grad_stack, qkv_full, preferred_element_type=jnp.float32)
    )
    share_qkv, share_qv, share_out, share_up, share_up_bias, share_down = (
        lax.psum_scatter(grad_qkv, "dp", scatter_dimension=1, tiled=True),
        lax.psum_scatter(grad_qv, "dp", scatter_dimension=2, tiled=True),
        lax.psum_scatter(grad_out, "dp", scatter_dimension=1, tiled=True),
        lax.psum_scatter(grad_up, "dp", scatter_dimension=0, tiled=True),
        lax.psum_scatter(grad_up_bias, "dp", scatter_dimension=1, tiled=True),
        lax.psum_scatter(grad_down, "dp", scatter_dimension=1, tiled=True),
    )
    d_input, grad_gain_one, grad_shift_one = norm_back(d_h_one, normed_one, inverse_one, gain_one)
    input_grad = d_middle + d_input
    small_shares = (
        lax.psum_scatter(grad_gain_one, ("dp", "tensor"), scatter_dimension=0, tiled=True),
        lax.psum_scatter(grad_shift_one, ("dp", "tensor"), scatter_dimension=0, tiled=True),
        lax.psum_scatter(grad_out_bias, ("dp", "tensor"), scatter_dimension=0, tiled=True),
        lax.psum_scatter(grad_gain_two, ("dp", "tensor"), scatter_dimension=0, tiled=True),
        lax.psum_scatter(grad_shift_two, ("dp", "tensor"), scatter_dimension=0, tiled=True),
        lax.psum_scatter(grad_down_bias, ("dp", "tensor"), scatter_dimension=0, tiled=True),
    )
    return (
        layer_out,
        input_grad,
        small_shares[0],
        small_shares[1],
        share_qkv,
        share_qv,
        share_out,
        small_shares[2],
        small_shares[3],
        small_shares[4],
        share_up,
        share_up_bias,
        share_down,
        small_shares[5],
    )


def local_fused(zs, tokens, cotangent, norm1_gain, norm1_shift, qkv_weight, qv_bias, out_weight, out_bias,
                norm2_gain, norm2_shift, up_weight, up_bias, down_weight, down_bias):
    images = tokens.shape[0] // SEQ
    a = jnp.concatenate([qkv_weight, out_weight.T[None]], 0)
    b = jnp.stack([up_weight, down_weight.T])
    s = pack_small(norm1_gain, norm1_shift, out_bias, norm2_gain, norm2_shift, down_bias, qv_bias, up_bias)
    tok = pad_rows(tokens, images)
    o = forward(a, b, s, tok, zs, images)
    dx, ga, gb, gs = backward(o[:10], tok, pad_rows(cotangent, images), o[11], zs, images, PLAN)
    cell = norm1_gain.shape[0]

    def unpad(v):
        return v.reshape(images, SP, -1)[:, :SEQ].reshape(images * SEQ, -1)

    return (
        unpad(o[10]), unpad(dx), gs[0, :cell], gs[1, :cell], ga[:3], gs[6:8, None, :cell], ga[3].T, gs[2, :cell],
        gs[3, :cell], gs[4, :cell], gb[0], gs[8:9, : up_bias.shape[1]], gb[1].T, gs[5, :cell],
    )


def solution(mesh):
    size = mesh.shape["dp"]
    zs = size // (X * Y)
    fused = size == zs * X * Y and mesh.shape["tensor"] == 2 and 768 // size == 48
    placed = (
        P(("dp", "tensor"), None),
        P(("dp", "tensor"), None),
        P(("dp", "tensor")),
        P(("dp", "tensor")),
        P(None, "dp", "tensor"),
        P(None, "tensor", "dp"),
        P("tensor", "dp"),
        P(("dp", "tensor")),
        P(("dp", "tensor")),
        P(("dp", "tensor")),
        P("dp", "tensor"),
        P("tensor", "dp"),
        P("tensor", "dp"),
        P(("dp", "tensor")),
    )
    return jax.shard_map(
        partial(local_fused, zs) if fused else local,
        mesh=mesh,
        in_specs=placed,
        out_specs=(
            P(("dp", "tensor"), None),
            P(("dp", "tensor"), None),
            P(("dp", "tensor")),
            P(("dp", "tensor")),
            P(None, "dp", "tensor"),
            P(None, "tensor", "dp"),
            P("tensor", "dp"),
            P(("dp", "tensor")),
            P(("dp", "tensor")),
            P(("dp", "tensor")),
            P("dp", "tensor"),
            P("tensor", "dp"),
            P("tensor", "dp"),
            P(("dp", "tensor")),
        ),
        check_vma=False,
    )
```

```python
import functools
from functools import partial
import jax
import jax.numpy as jnp
from jax import lax
from jax.experimental import pallas as pl
from jax.experimental.pallas import tpu as pltpu
from jax.sharding import PartitionSpec as P

MESH = pl.DeviceIdType.MESH
BF = jnp.bfloat16
F32 = jnp.float32
DMA = pltpu.SemaphoreType.DMA
HD = 64
SEQ = 197
SP = 208
QUAD = 256
EPS = 1e-06
X = Y = 2
ALL = slice(None)


def dot(a, b, ca=1, cb=0):
    return lax.dot_general(a, b, (((ca,), (cb,)), ((), ())), preferred_element_type=F32)


def remote(src, dst, send, recv, dev):
    return pltpu.make_async_remote_copy(
        src_ref=src, dst_ref=dst, send_sem=send, recv_sem=recv, device_id=dev, device_id_type=MESH
    )


def center(x):
    d = x - jnp.mean(x, axis=-1, keepdims=True)
    r = lax.rsqrt(jnp.mean(d * d, axis=-1, keepdims=True) + EPS)
    return d * r, r


def padded(v, images):
    gap = jnp.zeros((SP - SEQ, v.shape[1]), v.dtype)
    parts = []
    for i in range(images):
        parts += [v[i * SEQ : (i + 1) * SEQ], gap]
    return jnp.concatenate(parts, axis=0)


def unpadded(v, images):
    return jnp.concatenate([v[i * SP : i * SP + SEQ] for i in range(images)], axis=0)


class Place:
    def __init__(self, zs):
        dp = lax.axis_index("dp")
        self.c = c = lax.axis_index("tensor")
        self.zs = zs
        self.z = z = dp // (X * Y)
        self.y = y = (dp // X) % Y
        self.x = x = dp % X
        self.one_y, self.one_x = y + c * (1 - 2 * y), x + (1 - c) * (1 - 2 * x)
        self.two_y, self.two_x = y + (1 - c) * (1 - 2 * y), x + c * (1 - 2 * x)
        self.one = self.dev(z, self.one_y, self.one_x, c)
        self.two = self.dev(z, self.two_y, self.two_x, c)
        self.pair = self.dev(z, y, x, 1 - c)

    def dev(self, z, y, x, c):
        return {"dp": (z * Y + y) * X + x, "tensor": c}

    def zdev(self, k):
        return self.dev(lax.rem(self.z + k, self.zs), self.y, self.x, self.c)

    def greet(self):
        barrier = pltpu.get_barrier_semaphore()
        peers = [self.one, self.two, self.pair] + [self.zdev(k) for k in range(1, self.zs)]
        for peer in peers:
            pl.semaphore_signal(barrier, inc=1, device_id=peer, device_id_type=MESH)
        pl.semaphore_wait(barrier, len(peers))


PIECES = (
    ("s", 0, 0, 128),
    ("a", 0, 0, 384),
    ("a", 1, 0, 384),
    ("a", 2, 0, 384),
    ("a", 3, 0, 384),
    ("b", 0, 0, 768),
    ("b", 0, 768, 768),
    ("b", 1, 0, 768),
    ("b", 1, 768, 768),
)
NP = len(PIECES)
HALF = {"a": 384, "b": 1536}


class Gather:
    def __init__(self, place, shards, fulls, sems):
        self.place, self.shards, self.fulls = place, shards, fulls
        self.send, self.recv, self.zs, self.zr, self.ls = sems

    def full(self, p, idx):
        name, m, col, width = PIECES[p]
        ref = self.fulls[name]
        c = self.place.c
        if name == "s":
            return ref.at[(c,) + idx]
        cols = pl.ds(pl.multiple_of(c * HALF[name] + col, 128), width)
        return ref.at[(m,) + idx + (ALL, cols)]

    def own(self, p):
        name, m, col, width = PIECES[p]
        return self.shards[name, m].at[:, pl.ds(col, width)]

    def zcopy(self, p, k):
        pp = self.place
        return remote(
            self.own(p), self.full(p, (pp.z, pp.y, pp.x)), self.zs.at[p, k - 1], self.zr.at[p, k - 1], pp.zdev(k)
        )

    def local(self, p):
        pp = self.place
        return pltpu.make_async_copy(self.own(p), self.full(p, (pp.z, pp.y, pp.x)), self.ls.at[p])

    def hop(self, p, k):
        pp = self.place
        idx = ((ALL, pp.y, pp.x), (ALL, pp.y, pp.x), (ALL, pp.one_y, pp.one_x), (ALL, ALL, ALL))[k]
        s = self.full(p, idx)
        return remote(s, s, self.send.at[p, k], self.recv.at[p, k], (pp.one, pp.two, pp.two, pp.pair)[k])

    def stage(self, p, k):
        zs = self.place.zs
        if k == 0:
            for j in range(1, zs):
                self.zcopy(p, j).start()
            self.local(p).start()
        elif k == 1:
            self.local(p).wait()
            for j in range(1, zs):
                self.zcopy(p, j).wait_recv()
            self.hop(p, 0).start()
            self.hop(p, 1).start()
        elif k == 2:
            self.hop(p, 0).wait_recv()
            self.hop(p, 2).start()
        elif k == 3:
            self.hop(p, 1).wait_recv()
            self.hop(p, 2).wait_recv()
            self.hop(p, 3).start()
        else:
            self.hop(p, 3).wait_recv()

    def finish(self):
        for p in range(NP):
            for k in range(1, self.place.zs):
                self.zcopy(p, k).wait_send()
            for k in range(4):
                self.hop(p, k).wait_send()


def forward_kernel(zs, images, plan, *refs):
    (qkv_w, out_w, up_w, dn_w, tok_r, cot_r), tiny = refs[:6], refs[6:14]
    (lo_o, vec, upb_o, wa_o, wb_o, h1t_o, qkv_o, p_o, att_o, mid_o, h2t_o, gp_o, tok_o, cot_o, gdn_o) = refs[14:29]
    (wa, wb, sv, s_sh, s_wide, h1, qkv, pbuf, att, mid, h2, hid, gp, acc, tok, cot, cott, h1t, gdn, psem, osem) = refs[29:50]
    sems = refs[50:]
    place = Place(zs)
    c = place.c
    n = zs * Y * X
    saves = []
    early = pltpu.make_async_copy(h1t, h1t_o, osem.at[15])

    def save(src, dst):
        copy = pltpu.make_async_copy(src, dst, osem.at[len(saves)])
        copy.start()
        saves.append(copy)

    s_wide[...] = jnp.zeros_like(s_wide)
    row = 0
    for ref in tiny:
        value = ref[...].astype(F32)
        s_wide[row : row + value.shape[0], 0 : value.shape[1]] = value
        row += value.shape[0]
    s_sh[...] = s_wide[...].astype(BF)
    place.greet()
    shards = {("s", 0): s_sh, ("b", 0): up_w, ("b", 1): dn_w, ("a", 3): out_w}
    for t in range(3):
        shards["a", t] = qkv_w.at[t]
    g = Gather(place, shards, {"a": wa, "b": wb, "s": sv}, sems)

    def rows_of(i):
        return pl.ds(pl.multiple_of(i * SP, 16), SP)

    def cut(v):
        return v.reshape(zs, Y, X, 48, v.shape[1])

    def pad():
        tok[...] = padded(tok_r[...].astype(F32), images).astype(BF)
        cot_f = cot_r[...].astype(F32)
        cot[...] = padded(cot_f, images).astype(BF)
        vec[16:17, :] = jnp.sum(cot_f, axis=0, keepdims=True)
        save(tok, tok_o)
        save(cot, cot_o)

    def ct():
        cott[...] = cot[...].T

    def prep():
        flat = sv[...].reshape(2 * n * 16, 128)
        cell, cell_up = 768 // (2 * n), 1536 // n
        lane = lax.broadcasted_iota(jnp.int32, (128, 768), 0)
        col = lax.rem(lax.broadcasted_iota(jnp.int32, (128, 768), 1), cell)
        spread = dot(flat, (col == lane).astype(BF)).reshape(2 * n, 16, 768)
        who = lax.broadcasted_iota(jnp.int32, (2 * n, 16, 768), 0)
        kind = lax.broadcasted_iota(jnp.int32, (2 * n, 16, 768), 1)
        spot = lax.broadcasted_iota(jnp.int32, (2 * n, 16, 768), 2) // cell
        r_of, c_of = lax.rem(who, n), who // n
        mine = jnp.where(kind < 6, 2 * r_of + c_of, n * c_of + r_of)
        vec[0:16, :] = jnp.sum(jnp.where(mine == spot, spread, 0.0), axis=0)
        row = lax.broadcasted_iota(jnp.int32, (2 * n, 2 * n * 16), 0)
        col = lax.broadcasted_iota(jnp.int32, (2 * n, 2 * n * 16), 1)
        up_rows = dot((col == row * 16 + 8).astype(BF), flat).astype(BF)
        lane = lax.broadcasted_iota(jnp.int32, (128, 3072), 0)
        col = lax.rem(lax.broadcasted_iota(jnp.int32, (128, 3072), 1), cell_up)
        spread = dot(up_rows, (col == lane).astype(BF))
        who = lax.broadcasted_iota(jnp.int32, (2 * n, 3072), 0)
        spot = lax.broadcasted_iota(jnp.int32, (2 * n, 3072), 1) // cell_up
        upb_o[...] = jnp.sum(jnp.where(who == spot, spread, 0.0), axis=0, keepdims=True)

        @pl.loop(0, images)
        def _(i):
            v, _r = center(tok[rows_of(i), :].astype(F32))
            h1[rows_of(i), :] = (v * vec[0:1, :] + vec[1:2, :]).astype(BF)

    def project(t):
        @pl.loop(0, 3)
        def _(j):
            cols = pl.ds(pl.multiple_of(j * 256, 256), 256)
            w = wa[t, :, :, :, :, cols].reshape(768, 256)
            r = dot(h1[...], w)
            if t == 0:
                r = (r + vec[6:7, cols]).astype(BF) * jnp.asarray(HD**-0.5, BF)
            elif t == 2:
                r = r + vec[7:8, cols]
            qkv[t, :, cols] = r.astype(BF)

        if t == 2:
            save(qkv, qkv_o)
            h1t[...] = h1[...].T
            early.start()

    def attention(i):
        @pl.loop(0, 3)
        def _(j):
            cols = pl.ds(pl.multiple_of(j * QUAD, QUAD), QUAD)
            step = i * 3 + j
            slot = lax.rem(step, 2)
            head = lax.broadcasted_iota(jnp.int32, (SP, QUAD), 1) // HD
            q = qkv[0, rows_of(i), cols]
            zero = jnp.zeros_like(q)
            q4 = jnp.concatenate([jnp.where(head == h, q, zero) for h in range(4)], axis=0)
            s = dot(q4, qkv[1, rows_of(i), cols], 1, 1)
            key = lax.broadcasted_iota(jnp.int32, (4 * SP, SP), 1)
            s = jnp.where(key < SEQ, s, -1e30)
            e = jnp.exp(s - jnp.max(s, axis=-1, keepdims=True))
            p = (e * (1.0 / jnp.sum(e, axis=-1, keepdims=True))).astype(BF)

            @pl.when(step >= 2)
            def _():
                pltpu.make_async_copy(pbuf.at[slot], p_o.at[step - 2], psem.at[slot]).wait()

            pbuf[slot] = p
            pltpu.make_async_copy(pbuf.at[slot], p_o.at[step], psem.at[slot]).start()
            o4 = dot(p, qkv[2, rows_of(i), cols])
            o = jnp.zeros((SP, QUAD), F32)
            for h in range(4):
                o = jnp.where(head == h, o4[h * SP : (h + 1) * SP], o)
            att[rows_of(i), cols] = o.astype(BF)

        if i == images - 1:
            for k in (images * 3 - 2, images * 3 - 1):
                pltpu.make_async_copy(pbuf.at[k % 2], p_o.at[k], psem.at[k % 2]).wait()

    def out():
        save(att, att_o)
        for j in range(3):
            w = wa[3].reshape(768, 768)[j * 256 : (j + 1) * 256, :]
            cols = slice(j * 256, (j + 1) * 256)
            mid[:, cols] = tok[:, cols].astype(F32) + (dot(att[...], w, 1, 1) + vec[2:3, cols])

        @pl.loop(0, images)
        def _(i):
            v, _r = center(mid[rows_of(i), :])
            h2[rows_of(i), :] = (v * vec[3:4, :] + vec[4:5, :]).astype(BF)

        save(mid, mid_o)
        save(wa, wa_o)

    def expand(piece, half):
        @pl.loop(0, 3)
        def _(j):
            cols = pl.ds(pl.multiple_of(half * 1536 + piece * 768 + j * 256, 256), 256)
            w = wb[0, :, :, :, :, cols].reshape(768, 256)

            @pl.loop(0, images)
            def _(i):
                pre = dot(h2[rows_of(i), :], w) + upb_o[:, cols]
                cdf = 0.5 + 0.5 * lax.erf(pre * (0.5**0.5))
                pdf = jnp.exp(pre * pre * -0.5) * 0.3989422804014327
                hid[rows_of(i), cols] = (pre * cdf).astype(BF)
                gp[rows_of(i), cols] = (cdf + pre * pdf).astype(BF)

        if piece == 1 and half == 1:
            save(wb.at[0], wb_o.at[0])
            save(gp, gp_o)

    def grad_down(piece, own):
        half = c if own else 1 - c

        @pl.loop(0, 3)
        def _(j):
            cols = pl.ds(pl.multiple_of(half * 1536 + piece * 768 + j * 256, 256), 256)
            gdn[piece, own, :, :, :, :, pl.ds(pl.multiple_of(j * 256, 256), 256)] = cut(
                dot(cott[...], hid[:, cols]).astype(BF)
            )

        save(gdn.at[piece, own], gdn_o.at[piece, own])

    def contract(piece):
        for j in range(3):
            cols = slice(j * 256, (j + 1) * 256)
            total = mid[:, cols] + vec[5:6, cols] if piece == 0 else acc[:, cols]
            for half in range(2):
                fc = slice(half * 1536 + piece * 768, half * 1536 + piece * 768 + 768)
                w = wb[1, :, :, :, :, fc].reshape(768, 768)[j * 256 : (j + 1) * 256, :]
                total = total + dot(hid[:, fc], w, 1, 1)
            if piece == 0:
                acc[:, cols] = total
            else:
                lo_o[:, cols] = unpadded(total, images).astype(BF)
        if piece == 0:
            early.wait()
            h1t[...] = h2[...].T
            save(h1t, h2t_o)

    tasks = {"pad": pad, "ct": ct, "prep": prep, "out": out}
    for t in range(3):
        tasks["qkv"[t]] = functools.partial(project, t)
    for i in range(images):
        tasks[f"at{i}"] = functools.partial(attention, i)
    for k in range(2):
        for h in range(2):
            tasks[f"ex{k}" + "ab"[h]] = functools.partial(expand, k, h)
            tasks[f"gd{k}" + "ow"[h]] = functools.partial(grad_down, k, h)
        tasks[f"ct{k}"] = functools.partial(contract, k)
    for item in plan:
        if isinstance(item, str):
            tasks[item]()
        else:
            g.stage(*item)
            if item == (8, 4):
                save(wb.at[1], wb_o.at[1])
    g.finish()
    for copy in saves:
        copy.wait()


def forward(qkv_w, out_w, up_w, dn_w, tok, cot, tiny, zs, images, plan):
    rows = images * SP
    S = jax.ShapeDtypeStruct
    V = pltpu.VMEM
    dims = (zs, Y, X)
    outs = (
        S((images * SEQ, 768), BF), S((24, 768), F32), S((1, 3072), F32),
        S((4,) + dims + (48, 768), BF), S((2,) + dims + (48, 3072), BF), S((768, rows), BF), S((3, rows, 768), BF),
        S((images * 3, 4 * SP, SP), BF), S((rows, 768), BF), S((rows, 768), F32), S((768, rows), BF),
        S((rows, 3072), BF), S((rows, 768), BF), S((rows, 768), BF), S((2, 2) + dims + (48, 768), BF),
    )
    anys = pl.BlockSpec(memory_space=pl.ANY)
    vm = pl.BlockSpec(memory_space=pltpu.VMEM)
    return pl.pallas_call(
        functools.partial(forward_kernel, zs, images, plan),
        out_shape=outs,
        in_specs=[vm] * 14,
        out_specs=[vm] * 3 + [anys] * 12,
        scratch_shapes=[
            V((4,) + dims + (48, 768), BF), V((2,) + dims + (48, 3072), BF), V((2,) + dims + (16, 128), BF), V((16, 128), BF), V((16, 128), F32),
            V((rows, 768), BF), V((3, rows, 768), BF), V((2, 4 * SP, SP), BF), V((rows, 768), BF), V((rows, 768), F32),
            V((rows, 768), BF), V((rows, 3072), BF), V((rows, 3072), BF), V((rows, 768), F32),
            V((rows, 768), BF), V((rows, 768), BF), V((768, rows), BF), V((768, rows), BF), V((2, 2) + dims + (48, 768), BF),
            DMA((2,)), DMA((16,)),
            DMA((NP, 4)), DMA((NP, 4)), DMA((NP, zs - 1)), DMA((NP, zs - 1)), DMA((NP,)),
        ],
        compiler_params=pltpu.CompilerParams(collective_id=1, has_side_effects=True, vmem_limit_bytes=60 * 2**20),
        name="gather_forward",
    )(qkv_w, out_w, up_w, dn_w, tok, cot, *tiny)


FORWARD = (
    (0, 0), (1, 0), (2, 0), "pad", "ct", (0, 1), (3, 0), (1, 1), (4, 0), (0, 2), (2, 1), (5, 0), (1, 2), (0, 3),
    (3, 1), (6, 0), (0, 4), "prep", (2, 2), (4, 1), (7, 0), (3, 2), (1, 3), (1, 4), "q", (4, 2), (5, 1), (8, 0),
    (2, 3), (2, 4), "k", (3, 3), (6, 1), (5, 2), (3, 4), "v", (4, 3), "at0", (4, 4), "at1", (6, 2), (7, 1), "at2",
    "at3", (8, 1), "out", (7, 2), (5, 3), (5, 4), "ex0a", (6, 3), (8, 2), "ex0b", (6, 4), "ex1a", "ex1b", (7, 3),
    "gd0o", (8, 3), "gd0w", "gd1o", (7, 4), "gd1w", (8, 4), "ct0", "ct1",
)

BACKWARD = (
    "down", (0, 0), (1, 0), "pr0", "pr2", "pr1", (0, 1), (1, 1), "pr3", "u0o", (2, 0), "u0w", (0, 2), "u1o", (2, 1),
    (3, 0), "u1w", "dh0", (3, 1), (1, 2), (0, 3), "dh1", "dh2", "nm2", "og", (0, 4), (1, 3), (2, 2), (4, 0), "da",
    "at0", (3, 2), (4, 1), "at1", (1, 4), (2, 3), "at2", (4, 2), "at3", (3, 3), (4, 3), "gq", (2, 4), (5, 0), "gk",
    (6, 0), "gv", (5, 1), (7, 0), "di0", (6, 1), "di1", (3, 4), (5, 2), (7, 1), "di2", (4, 4), "nm1", (6, 2), "sm",
    (8, 0), "fin", (5, 3), (8, 1), (7, 2), (6, 3), (5, 4), (8, 2), (7, 3), (8, 3), (6, 4), (7, 4), (8, 4),
)


SPIECES = (
    ("b", 1, 0, 768),
    ("b", 1, 768, 768),
    ("b", 0, 0, 768),
    ("b", 0, 768, 768),
    ("a", 3, 0, 384),
    ("a", 0, 0, 384),
    ("a", 1, 0, 384),
    ("a", 2, 0, 384),
    ("s", 0, 0, 128),
)
NS = len(SPIECES)


class Scatter:
    def __init__(self, place, gdn, gout, gs, wb, pb, pa, psm, rb, ra, rs, outs, sems):
        self.place = place
        self.gdn, self.gout, self.gs_, self.wb = gdn, gout, gs, wb
        self.pbuf = {"b": pb, "a": pa, "s": psm}
        self.rbuf = {"b": rb, "a": ra, "s": rs}
        self.outs = outs
        self.send, self.recv_, self.z_send, self.z_recv = sems

    def index(self, p):
        return p if p < 4 else (p - 4 if p < 8 else 0)

    def part(self, p, own):
        if p < 2:
            return self.gdn.at[p, own]
        if p < 4:
            cols = pl.ds(pl.multiple_of((p - 2) * 1536 + own * 768, 128), 768)
            return self.wb.at[1, :, :, :, :, cols]
        if p == 4:
            return self.gout.at[own]
        if p < 8:
            k = p - 5
            return self.gdn.at[k // 2, own, :, :, :, :, pl.ds((k % 2) * 384, 384)]
        return self.gs_.at[own]

    def precv(self, p):
        return self.pbuf[SPIECES[p][0]].at[self.index(p)]

    def recv(self, p, k):
        return self.rbuf[SPIECES[p][0]][k].at[self.index(p)]

    def pair(self, p):
        return remote(self.part(p, 0), self.precv(p), self.send.at[p, 0], self.recv_.at[p, 0], self.place.pair)

    def hop(self, p, k):
        pp, s = self.place, self.part(p, 1)
        y, x = ((1 - pp.y, 1 - pp.x), (pp.two_y, pp.two_x), (pp.one_y, pp.one_x))[k - 1]
        return remote(
            s.at[:, y, x], self.recv(p, k - 1), self.send.at[p, k], self.recv_.at[p, k], pp.one if k == 3 else pp.two
        )

    def three(self, p, k):
        pp, s = self.place, self.part(p, 1)
        to = lax.rem(pp.z + k, pp.zs)
        return remote(
            s.at[to, pp.y, pp.x], self.recv(p, 3).at[k - 1], self.z_send.at[p, k - 1], self.z_recv.at[p, k - 1], pp.zdev(k)
        )

    def stage(self, p, k):
        pp = self.place
        zs = pp.zs
        kind = F32 if p == 8 else BF
        s = self.part(p, 1)
        if k == 0:
            self.pair(p).start()
        elif k == 1:
            self.pair(p).wait_recv()
            r = self.precv(p)
            for zz in range(zs):
                s[zz] = (s[zz].astype(F32) + r[zz].astype(F32)).astype(kind)
            self.hop(p, 1).start()
            self.hop(p, 2).start()
        elif k == 2:
            self.hop(p, 1).wait_recv()
            r = self.recv(p, 0)
            for zz in range(zs):
                at = (zz, pp.one_y, pp.one_x)
                s[at] = (s[at].astype(F32) + r[zz].astype(F32)).astype(kind)
            self.hop(p, 3).start()
        elif k == 3:
            self.hop(p, 2).wait_recv()
            self.hop(p, 3).wait_recv()
            ra, rb = self.recv(p, 1), self.recv(p, 2)
            for zz in range(zs):
                at = (zz, pp.y, pp.x)
                s[at] = (s[at].astype(F32) + ra[zz].astype(F32) + rb[zz].astype(F32)).astype(kind)
            for k in range(1, zs):
                self.three(p, k).start()
        else:
            r = self.recv(p, 3)
            total = s[pp.z, pp.y, pp.x].astype(F32)
            for k in range(1, zs):
                self.three(p, k).wait_recv()
                total = total + r[k - 1].astype(F32)
            name, m, col, width = SPIECES[p]
            self.outs[name, m][:, pl.ds(col, width)] = total
            self.pair(p).wait_send()
            for k in range(1, 4):
                self.hop(p, k).wait_send()
            for k in range(1, zs):
                self.three(p, k).wait_send()


def backward_kernel(zs, images, plan, *refs):
    (vec, wa_i, wb_i, h1t_i, qkv_i, p_i, att_i, mid_i, h2t_i, gp_i, tok_i, cot_i, gdn_i) = refs[:13]
    dx_o, gq_o, go_o, gu_o, gd_o, gs_o = refs[13:19]
    (wa, wb, cot, qkv, att, mid, dh, dpre, db, pt, xt, yt, vg, ug, gdn, gout, gs) = refs[19:36]
    pb, pa, psm = refs[36:39]
    rb, ra, rs = refs[39:43], refs[43:47], refs[47:51]
    lsem, psem = refs[51:53]
    sems = refs[53:]
    n = zs * Y * X
    place = Place(zs)
    c = place.c
    outs = {("b", 0): gu_o, ("b", 1): gd_o, ("a", 3): go_o, ("s", 0): gs_o}
    for t in range(3):
        outs["a", t] = gq_o.at[t]
    sc = Scatter(place, gdn, gout, gs, wb, pb, pa, psm, rb, ra, rs, outs, sems)

    loads = {
        "gdn": (gdn_i, gdn), "cot": (cot_i, cot), "dn": (wb_i.at[1], wb.at[1]), "gp": (gp_i, dpre), "h2t": (h2t_i, yt),
        "up": (wb_i.at[0], wb.at[0]), "mid": (mid_i, mid), "att": (att_i, att), "wa": (wa_i, wa), "qkv": (qkv_i, qkv),
        "tok": (tok_i, cot), "h1t": (h1t_i, yt),
    }
    names = list(loads)

    def load(name):
        src, dst = loads[name]
        return pltpu.make_async_copy(src, dst, lsem.at[names.index(name)])

    for name in names[:-2]:
        load(name).start()
    place.greet()

    def rows_of(i):
        return pl.ds(pl.multiple_of(i * SP, 16), SP)

    def cut(v):
        return v.reshape(zs, Y, X, 48, v.shape[1])

    def ptile(step):
        return pltpu.make_async_copy(p_i.at[step], pt.at[step % 2], psem.at[step % 2])

    ptile(0).start()
    vg[...] = jnp.zeros_like(vg)
    vg[5:6, :] = vec[16:17, :]

    def down():
        load("gdn").wait()

    def pre(part):
        if part == 0:
            load("cot").wait()
            load("dn").wait()
            load("gp").wait()

        @pl.loop(0, 3)
        def _(j):
            cols = pl.ds(pl.multiple_of(part * 768 + j * 256, 256), 256)
            w = wb[1, :, :, :, :, cols].reshape(768, 256)
            d = (dot(cot[...], w) * dpre[:, cols].astype(F32)).astype(BF)
            dpre[:, cols] = d
            ug[:, cols] = jnp.sum(d.astype(F32), axis=0, keepdims=True)

        if part == 3:
            load("h2t").wait()

    def grad_up(piece, own):
        half = c if own == 1 else 1 - c

        @pl.loop(0, 3)
        def _(j):
            cols = pl.ds(pl.multiple_of(half * 1536 + piece * 768 + j * 256, 256), 256)
            dest = pl.ds(pl.multiple_of(piece * 1536 + own * 768 + j * 256, 256), 256)
            wb[1, :, :, :, :, dest] = cut(dot(yt[...], dpre[:, cols]).astype(BF))

        if piece == 1 and own == 1:
            load("h1t").start()

    def d_h2(j):
        if j == 0:
            load("up").wait()
        w = wb[0].reshape(768, 3072)[j * 256 : (j + 1) * 256, :]
        dh[:, j * 256 : (j + 1) * 256] = dot(dpre[...], w, 1, 1)

    def norm2():
        load("mid").wait()

        @pl.loop(0, images)
        def _(i):
            v, r = center(mid[rows_of(i), :])
            g = dh[rows_of(i), :]
            vg[3:4, :] += jnp.sum(g * v, axis=0, keepdims=True)
            vg[4:5, :] += jnp.sum(g, axis=0, keepdims=True)
            dn = g * vec[3:4, :]
            d = cot[rows_of(i), :].astype(F32) + r * (
                dn - jnp.mean(dn, axis=-1, keepdims=True) - v * jnp.mean(dn * v, axis=-1, keepdims=True)
            )
            dh[rows_of(i), :] = d
            low = d.astype(BF)
            db[rows_of(i), :] = low
            vg[2:3, :] += jnp.sum(low.astype(F32), axis=0, keepdims=True)

        load("tok").start()

    def grad_out():
        xt[...] = db[...].T
        load("att").wait()
        for h in range(2):
            own = 1 - h - c + 2 * h * c
            gout[own] = cut(dot(xt[...], att[:, h * 384 : (h + 1) * 384]).astype(BF))

    def d_att():
        load("wa").wait()

        @pl.loop(0, 3)
        def _(j):
            cols = pl.ds(pl.multiple_of(j * 256, 256), 256)
            att[:, cols] = dot(db[...], wa[3, :, :, :, :, cols].reshape(768, 256)).astype(BF)

    total = images * 3

    def attention(i):
        if i == 0:
            load("qkv").wait()

        @pl.loop(0, 3)
        def _(j):
            cols = pl.ds(pl.multiple_of(j * QUAD, QUAD), QUAD)
            step = i * 3 + j
            ptile(step).wait()

            @pl.when(step + 1 < total)
            def _():
                ptile(step + 1).start()

            head = lax.broadcasted_iota(jnp.int32, (SP, QUAD), 1) // HD
            q, k, v, do = qkv[0, rows_of(i), cols], qkv[1, rows_of(i), cols], qkv[2, rows_of(i), cols], att[rows_of(i), cols]
            zero = jnp.zeros_like(q)
            q4 = jnp.concatenate([jnp.where(head == h, q, zero) for h in range(4)], axis=0)
            do4 = jnp.concatenate([jnp.where(head == h, do, zero) for h in range(4)], axis=0)
            p = pt[step % 2]
            dp = dot(do4, v, 1, 1)
            dv = dot(p, do4, 0, 0)
            pf = p.astype(F32)
            ds = (pf * (dp - jnp.sum(pf * dp, axis=-1, keepdims=True))).astype(BF)
            dq4 = dot(ds, k)
            dk = dot(ds, q4, 0, 0)
            dq = jnp.zeros((SP, QUAD), F32)
            for h in range(4):
                dq = jnp.where(head == h, dq4[h * SP : (h + 1) * SP], dq)
            qkv[0, rows_of(i), cols] = (dq * HD**-0.5).astype(BF)
            qkv[1, rows_of(i), cols] = dk.astype(BF)
            qkv[2, rows_of(i), cols] = dv.astype(BF)

    def grad_qkv(t):
        if t == 0:
            load("h1t").wait()
        for h in range(2):
            own = 1 - h - c + 2 * h * c
            gdn[t // 2, own, :, :, :, :, (t % 2) * 384 : (t % 2) * 384 + 384] = cut(
                dot(yt[...], qkv[t, :, h * 384 : (h + 1) * 384]).astype(BF)
            )
        if t != 1:
            vg[6 + t // 2 : 7 + t // 2, :] = jnp.sum(qkv[t].astype(F32), axis=0, keepdims=True)

    def d_h1(j):
        cols = slice(j * 256, (j + 1) * 256)
        sum_ = None
        for t in range(3):
            w = wa[t].reshape(768, 768)[cols, :]
            r = dot(qkv[t], w, 1, 1)
            sum_ = r if sum_ is None else sum_ + r
        mid[:, cols] = sum_

    def norm1():
        load("tok").wait()

        @pl.loop(0, images)
        def _(i):
            v, r = center(cot[rows_of(i), :].astype(F32))
            g = mid[rows_of(i), :]
            vg[0:1, :] += jnp.sum(g * v, axis=0, keepdims=True)
            vg[1:2, :] += jnp.sum(g, axis=0, keepdims=True)
            dn = g * vec[0:1, :]
            mid[rows_of(i), :] = dh[rows_of(i), :] + r * (
                dn - jnp.mean(dn, axis=-1, keepdims=True) - v * jnp.mean(dn * v, axis=-1, keepdims=True)
            )

    def two_parts(v):
        hi = v.astype(BF)
        return hi, (v - hi.astype(F32)).astype(BF)

    def small_blocks():
        cell, cell_up = 768 // (2 * n), 1536 // n
        who = lax.broadcasted_iota(jnp.int32, (2 * n, 16, 768), 0)
        kind = lax.broadcasted_iota(jnp.int32, (2 * n, 16, 768), 1)
        spot = lax.broadcasted_iota(jnp.int32, (2 * n, 16, 768), 2) // cell
        r_of, c_of = lax.rem(who, n), who // n
        mine = jnp.where(kind < 6, 2 * r_of + c_of, n * c_of + r_of)
        mixed = jnp.where(mine == spot, vg[...][None], 0.0).reshape(2 * n * 16, 768)
        col = lax.rem(lax.broadcasted_iota(jnp.int32, (768, 128), 0), cell)
        pick = (col == lax.broadcasted_iota(jnp.int32, (768, 128), 1)).astype(BF)
        small = sum(dot(part, pick) for part in two_parts(mixed)).reshape(2 * n, 16, 128)
        who = lax.broadcasted_iota(jnp.int32, (2 * n, 3072), 0)
        spot = lax.broadcasted_iota(jnp.int32, (2 * n, 3072), 1) // cell_up
        mixed = jnp.where(who == spot, ug[...], 0.0)
        col = lax.rem(lax.broadcasted_iota(jnp.int32, (3072, 128), 0), cell_up)
        pick = (col == lax.broadcasted_iota(jnp.int32, (3072, 128), 1)).astype(BF)
        up_part = sum(dot(part, pick) for part in two_parts(mixed)).reshape(2 * n, 1, 128)
        kind = lax.broadcasted_iota(jnp.int32, (2 * n, 16, 128), 1)
        small = jnp.where(kind == 8, up_part, small).reshape(2, zs, Y, X, 16, 128)
        for h in range(2):
            gs[1 - h - c + 2 * h * c] = small[h]

    def finish():
        dx_o[...] = unpadded(mid[...], images)

    tasks = {
        "down": down, "nm2": norm2, "og": grad_out, "da": d_att, "nm1": norm1, "sm": small_blocks, "fin": finish,
    }
    for k in range(4):
        tasks[f"pr{k}"] = functools.partial(pre, k)
    for k in range(2):
        for h in range(2):
            tasks[f"u{k}" + "ow"[h]] = functools.partial(grad_up, k, h)
    for j in range(3):
        tasks[f"dh{j}"] = functools.partial(d_h2, j)
        tasks["g" + "qkv"[j]] = functools.partial(grad_qkv, j)
        tasks[f"di{j}"] = functools.partial(d_h1, j)
    for i in range(images):
        tasks[f"at{i}"] = functools.partial(attention, i)
    for item in plan:
        if isinstance(item, str):
            tasks[item]()
        else:
            sc.stage(*item)


def backward(saved, zs, images, plan):
    rows = images * SP
    S = jax.ShapeDtypeStruct
    V = pltpu.VMEM
    dims = (zs, Y, X)
    anys = pl.BlockSpec(memory_space=pl.ANY)
    vm = pl.BlockSpec(memory_space=pltpu.VMEM)

    def inbox(count, rows_, width, kind):
        return [V((count, zs, rows_, width), kind)] * 3 + [V((count, zs - 1, rows_, width), kind)]

    return pl.pallas_call(
        functools.partial(backward_kernel, zs, images, plan),
        out_shape=(
            S((images * SEQ, 768), F32), S((3, 48, 384), F32), S((48, 384), F32), S((48, 1536), F32), S((48, 1536), F32), S((16, 128), F32),
        ),
        in_specs=[vm] + [anys] * 12,
        out_specs=[vm] * 6,
        scratch_shapes=[
            V((4,) + dims + (48, 768), BF), V((2,) + dims + (48, 3072), BF), V((rows, 768), BF),
            V((3, rows, 768), BF), V((rows, 768), BF), V((rows, 768), F32), V((rows, 768), F32), V((rows, 3072), BF),
            V((rows, 768), BF), V((2, 4 * SP, SP), BF), V((768, rows), BF), V((768, rows), BF),
            V((16, 768), F32), V((1, 3072), F32),
            V((2, 2) + dims + (48, 768), BF), V((2,) + dims + (48, 384), BF), V((2,) + dims + (16, 128), F32),
            V((4,) + dims + (48, 768), BF), V((4,) + dims + (48, 384), BF), V((1,) + dims + (16, 128), F32),
        ]
        + inbox(4, 48, 768, BF)
        + inbox(4, 48, 384, BF)
        + inbox(1, 16, 128, F32)
        + [
            DMA((12,)), DMA((2,)),
            DMA((NS, 4)), DMA((NS, 4)), DMA((NS, zs - 1)), DMA((NS, zs - 1)),
        ],
        compiler_params=pltpu.CompilerParams(collective_id=2, has_side_effects=True, vmem_limit_bytes=60 * 2**20),
        name="backward_scatter",
    )(*saved)


def normalize(values):
    centered = values - jnp.mean(values, axis=-1, keepdims=True)
    inverse = lax.rsqrt(jnp.mean(centered * centered, axis=-1, keepdims=True) + EPS)
    return (centered * inverse, inverse)


def norm_back(grad_out, normed, inverse, gain):
    d_normed = grad_out * gain
    grad_in = inverse * (
        d_normed
        - jnp.mean(d_normed, axis=-1, keepdims=True)
        - normed * jnp.mean(d_normed * normed, axis=-1, keepdims=True)
    )
    return (grad_in, jnp.sum(grad_out * normed, axis=0), jnp.sum(grad_out, axis=0))


def gather_rows(rows):
    return lax.all_gather(rows, "tensor", axis=0, tiled=True)


def sum_rows(terms):
    return lax.psum_scatter(
        terms.astype(jnp.bfloat16), "tensor", scatter_dimension=0, tiled=True
    ).astype(jnp.float32)


def gather_grads(rows):
    return lax.all_gather(rows, "tensor", axis=0, tiled=True)


def sum_grads(terms):
    return lax.psum_scatter(
        terms.astype(jnp.bfloat16), "tensor", scatter_dimension=0, tiled=True
    ).astype(jnp.float32)


def split_heads(matrix):
    return matrix.reshape(matrix.shape[0] // SEQ, SEQ, matrix.shape[1] // HD, HD)


def attend(queries, keys, values):
    scores = jnp.einsum(
        "iqhd,ikhd->ihqk", queries, keys, preferred_element_type=jnp.float32
    ) * HD ** (-0.5)
    row_top = jnp.max(scores, axis=-1, keepdims=True)
    shifted = jnp.exp(scores - row_top)
    row_total = jnp.sum(shifted, axis=-1, keepdims=True)
    probs = (shifted / row_total).astype(jnp.bfloat16)
    attended = jnp.einsum("ihqk,ikhd->iqhd", probs, values, preferred_element_type=jnp.float32)
    return (attended.astype(jnp.bfloat16), row_top + jnp.log(row_total))


def attend_back(queries, keys, values, log_total, d_attended):
    factor = HD ** (-0.5)
    scores = (
        jnp.einsum("iqhd,ikhd->ihqk", queries, keys, preferred_element_type=jnp.float32) * factor
    )
    probs = jnp.exp(scores - log_total)
    probs_low = probs.astype(jnp.bfloat16)
    grad_values = jnp.einsum(
        "ihqk,iqhd->ikhd", probs_low, d_attended, preferred_element_type=jnp.float32
    ).astype(jnp.bfloat16)
    d_probs = jnp.einsum("iqhd,ikhd->ihqk", d_attended, values, preferred_element_type=jnp.float32)
    d_scores = (probs * (d_probs - jnp.sum(probs * d_probs, axis=-1, keepdims=True))).astype(
        jnp.bfloat16
    )
    grad_queries = (
        jnp.einsum("ihqk,ikhd->iqhd", d_scores, keys, preferred_element_type=jnp.float32) * factor
    ).astype(jnp.bfloat16)
    grad_keys = (
        jnp.einsum("ihqk,iqhd->ikhd", d_scores, queries, preferred_element_type=jnp.float32)
        * factor
    ).astype(jnp.bfloat16)
    return (grad_queries, grad_keys, grad_values)


def local(
    tokens,
    cotangent,
    norm1_gain,
    norm1_shift,
    qkv_weight,
    qv_bias,
    out_weight,
    out_bias,
    norm2_gain,
    norm2_shift,
    up_weight,
    up_bias,
    down_weight,
    down_bias,
):
    small_full = (
        lax.all_gather(norm1_gain, ("dp", "tensor"), axis=0, tiled=True),
        lax.all_gather(norm1_shift, ("dp", "tensor"), axis=0, tiled=True),
        lax.all_gather(out_bias, ("dp", "tensor"), axis=0, tiled=True),
        lax.all_gather(norm2_gain, ("dp", "tensor"), axis=0, tiled=True),
        lax.all_gather(norm2_shift, ("dp", "tensor"), axis=0, tiled=True),
        lax.all_gather(down_bias, ("dp", "tensor"), axis=0, tiled=True),
    )
    gain_one, shift_one, out_vec, gain_two, shift_two, down_vec = [
        item.astype(jnp.float32) for item in small_full
    ]
    qkv_full, qv_full, out_full = (
        lax.all_gather(qkv_weight, "dp", axis=1, tiled=True),
        lax.all_gather(qv_bias, "dp", axis=2, tiled=True),
        lax.all_gather(out_weight, "dp", axis=1, tiled=True),
    )
    inputs = tokens.astype(jnp.float32)
    normed_one, inverse_one = normalize(inputs)
    h_one = gather_rows((normed_one * gain_one + shift_one).astype(jnp.bfloat16))
    projected = jnp.einsum("gd,tde->tge", h_one, qkv_full, preferred_element_type=jnp.float32)
    qv_rows = qv_full.astype(jnp.float32)
    queries = split_heads((projected[0] + qv_rows[0, 0]).astype(jnp.bfloat16))
    keys = split_heads(projected[1].astype(jnp.bfloat16))
    values = split_heads((projected[2] + qv_rows[1, 0]).astype(jnp.bfloat16))
    attended_heads, log_total = attend(queries, keys, values)
    group_rows = h_one.shape[0]
    attended = attended_heads.reshape(group_rows, qkv_full.shape[2])
    branch_one = sum_rows(jnp.dot(attended, out_full, preferred_element_type=jnp.float32)) + out_vec
    middle = inputs + branch_one
    up_full, up_vec, down_full = (
        lax.all_gather(up_weight, "dp", axis=0, tiled=True),
        lax.all_gather(up_bias, "dp", axis=1, tiled=True),
        lax.all_gather(down_weight, "dp", axis=1, tiled=True),
    )
    normed_two, inverse_two = normalize(middle)
    h_two = gather_rows((normed_two * gain_two + shift_two).astype(jnp.bfloat16))
    pre_act = jnp.dot(h_two, up_full, preferred_element_type=jnp.float32) + up_vec[0].astype(
        jnp.float32
    )
    hidden = jax.nn.gelu(pre_act, approximate=False).astype(jnp.bfloat16)
    branch_two = sum_rows(jnp.dot(hidden, down_full, preferred_element_type=jnp.float32)) + down_vec
    layer_out = (middle + branch_two).astype(jnp.bfloat16)
    grad_rows = cotangent.astype(jnp.float32)
    grad_down_bias = jnp.sum(grad_rows, axis=0)
    cot_all = gather_grads(cotangent)
    grad_down = jnp.einsum("gf,gd->fd", hidden, cot_all, preferred_element_type=jnp.float32)
    d_hidden = jnp.einsum("gd,fd->gf", cot_all, down_full, preferred_element_type=jnp.float32)
    gelu_out, gelu_back = jax.vjp(partial(jax.nn.gelu, approximate=False), pre_act)
    d_pre = gelu_back(d_hidden)[0].astype(jnp.bfloat16)
    grad_up_bias = jnp.sum(d_pre.astype(jnp.float32), axis=0)[None, :]
    grad_up = jnp.einsum("gd,gf->df", h_two, d_pre, preferred_element_type=jnp.float32)
    d_h_two = sum_grads(jnp.einsum("gf,df->gd", d_pre, up_full, preferred_element_type=jnp.float32))
    d_middle, grad_gain_two, grad_shift_two = norm_back(d_h_two, normed_two, inverse_two, gain_two)
    d_middle = d_middle + grad_rows
    d_branch = d_middle.astype(jnp.bfloat16)
    grad_out_bias = jnp.sum(d_branch.astype(jnp.float32), axis=0)
    branch_all = gather_grads(d_branch)
    grad_out = jnp.einsum("ge,gd->ed", attended, branch_all, preferred_element_type=jnp.float32)
    d_attended = jnp.einsum(
        "gd,ed->ge", branch_all, out_full, preferred_element_type=jnp.float32
    ).astype(jnp.bfloat16)
    grad_queries, grad_keys, grad_values = attend_back(
        queries, keys, values, log_total, split_heads(d_attended)
    )
    width = qkv_full.shape[2]
    grad_stack = jnp.stack(
        [
            grad_queries.reshape(group_rows, width),
            grad_keys.reshape(group_rows, width),
            grad_values.reshape(group_rows, width),
        ]
    )
    grad_qv = jnp.stack(
        [
            jnp.sum(grad_stack[0].astype(jnp.float32), axis=0),
            jnp.sum(grad_stack[2].astype(jnp.float32), axis=0),
        ]
    )[:, None, :]
    grad_qkv = jnp.einsum("gd,tge->tde", h_one, grad_stack, preferred_element_type=jnp.float32)
    d_h_one = sum_grads(
        jnp.einsum("tge,tde->gd", grad_stack, qkv_full, preferred_element_type=jnp.float32)
    )
    share_qkv, share_qv, share_out, share_up, share_up_bias, share_down = (
        lax.psum_scatter(grad_qkv, "dp", scatter_dimension=1, tiled=True),
        lax.psum_scatter(grad_qv, "dp", scatter_dimension=2, tiled=True),
        lax.psum_scatter(grad_out, "dp", scatter_dimension=1, tiled=True),
        lax.psum_scatter(grad_up, "dp", scatter_dimension=0, tiled=True),
        lax.psum_scatter(grad_up_bias, "dp", scatter_dimension=1, tiled=True),
        lax.psum_scatter(grad_down, "dp", scatter_dimension=1, tiled=True),
    )
    d_input, grad_gain_one, grad_shift_one = norm_back(d_h_one, normed_one, inverse_one, gain_one)
    input_grad = d_middle + d_input
    small_shares = (
        lax.psum_scatter(grad_gain_one, ("dp", "tensor"), scatter_dimension=0, tiled=True),
        lax.psum_scatter(grad_shift_one, ("dp", "tensor"), scatter_dimension=0, tiled=True),
        lax.psum_scatter(grad_out_bias, ("dp", "tensor"), scatter_dimension=0, tiled=True),
        lax.psum_scatter(grad_gain_two, ("dp", "tensor"), scatter_dimension=0, tiled=True),
        lax.psum_scatter(grad_shift_two, ("dp", "tensor"), scatter_dimension=0, tiled=True),
        lax.psum_scatter(grad_down_bias, ("dp", "tensor"), scatter_dimension=0, tiled=True),
    )
    return (
        layer_out,
        input_grad,
        small_shares[0],
        small_shares[1],
        share_qkv,
        share_qv,
        share_out,
        small_shares[2],
        small_shares[3],
        small_shares[4],
        share_up,
        share_up_bias,
        share_down,
        small_shares[5],
    )


def local_fused(zs, tokens, cotangent, norm1_gain, norm1_shift, qkv_weight, qv_bias, out_weight, out_bias,
                norm2_gain, norm2_shift, up_weight, up_bias, down_weight, down_bias):
    images = tokens.shape[0] // SEQ
    tiny = [v[None] for v in (norm1_gain, norm1_shift, out_bias, norm2_gain, norm2_shift, down_bias)]
    tiny += [qv_bias[:, 0], up_bias]
    saved = forward(
        qkv_weight, out_weight.T, up_weight, down_weight.T, tokens, cotangent, tiny, zs, images, FORWARD
    )
    dx, gq, go, gu, gd, gs = backward((saved[1],) + saved[3:], zs, images, BACKWARD)
    cell = norm1_gain.shape[0]
    return (
        saved[0], dx, gs[0, :cell], gs[1, :cell], gq, gs[6:8, None, :cell], go.T, gs[2, :cell],
        gs[3, :cell], gs[4, :cell], gu, gs[8:9, : up_bias.shape[1]], gd.T, gs[5, :cell],
    )


def solution(mesh):
    size = mesh.shape["dp"]
    zs = size // (X * Y)
    fused = size == zs * X * Y and mesh.shape["tensor"] == 2 and 768 // size == 48
    placed = (
        P(("dp", "tensor"), None),
        P(("dp", "tensor"), None),
        P(("dp", "tensor")),
        P(("dp", "tensor")),
        P(None, "dp", "tensor"),
        P(None, "tensor", "dp"),
        P("tensor", "dp"),
        P(("dp", "tensor")),
        P(("dp", "tensor")),
        P(("dp", "tensor")),
        P("dp", "tensor"),
        P("tensor", "dp"),
        P("tensor", "dp"),
        P(("dp", "tensor")),
    )
    return jax.shard_map(
        partial(local_fused, zs) if fused else local,
        mesh=mesh,
        in_specs=placed,
        out_specs=(
            P(("dp", "tensor"), None),
            P(("dp", "tensor"), None),
            P(("dp", "tensor")),
            P(("dp", "tensor")),
            P(None, "dp", "tensor"),
            P(None, "tensor", "dp"),
            P("tensor", "dp"),
            P(("dp", "tensor")),
            P(("dp", "tensor")),
            P(("dp", "tensor")),
            P("dp", "tensor"),
            P("tensor", "dp"),
            P("tensor", "dp"),
            P(("dp", "tensor")),
        ),
        check_vma=False,
    )
```

```python
import functools
from functools import partial
import jax
import jax.numpy as jnp
from jax import lax
from jax.experimental import pallas as pl
from jax.experimental.pallas import tpu as pltpu
from jax.sharding import PartitionSpec as P

MESH = pl.DeviceIdType.MESH
BF = jnp.bfloat16
F32 = jnp.float32
DMA = pltpu.SemaphoreType.DMA
HD = 64
SEQ = 197
SP = 208
QUAD = 256
EPS = 1e-06
X = Y = 2
ALL = slice(None)


def dot(a, b, ca=1, cb=0):
    return lax.dot_general(a, b, (((ca,), (cb,)), ((), ())), preferred_element_type=F32)


def remote(src, dst, send, recv, dev):
    return pltpu.make_async_remote_copy(
        src_ref=src, dst_ref=dst, send_sem=send, recv_sem=recv, device_id=dev, device_id_type=MESH
    )


def center(x):
    d = x - jnp.mean(x, axis=-1, keepdims=True)
    r = lax.rsqrt(jnp.mean(d * d, axis=-1, keepdims=True) + EPS)
    return d * r, r


def padded(v, images):
    gap = jnp.zeros((SP - SEQ, v.shape[1]), v.dtype)
    parts = []
    for i in range(images):
        parts += [v[i * SEQ : (i + 1) * SEQ], gap]
    return jnp.concatenate(parts, axis=0)


def unpadded(v, images):
    return jnp.concatenate([v[i * SP : i * SP + SEQ] for i in range(images)], axis=0)


class Place:
    def __init__(self, zs):
        dp = lax.axis_index("dp")
        self.c = c = lax.axis_index("tensor")
        self.zs = zs
        self.z = z = dp // (X * Y)
        self.y = y = (dp // X) % Y
        self.x = x = dp % X
        self.one_y, self.one_x = y + c * (1 - 2 * y), x + (1 - c) * (1 - 2 * x)
        self.two_y, self.two_x = y + (1 - c) * (1 - 2 * y), x + c * (1 - 2 * x)
        self.one = self.dev(z, self.one_y, self.one_x, c)
        self.two = self.dev(z, self.two_y, self.two_x, c)
        self.pair = self.dev(z, y, x, 1 - c)

    def dev(self, z, y, x, c):
        return {"dp": (z * Y + y) * X + x, "tensor": c}

    def zdev(self, k):
        return self.dev(lax.rem(self.z + k, self.zs), self.y, self.x, self.c)

    def greet(self):
        barrier = pltpu.get_barrier_semaphore()
        peers = [self.one, self.two, self.pair] + [self.zdev(k) for k in range(1, self.zs)]
        for peer in peers:
            pl.semaphore_signal(barrier, inc=1, device_id=peer, device_id_type=MESH)
        pl.semaphore_wait(barrier, len(peers))


def perform(plan, tasks, families, stage):
    for item in plan:
        if isinstance(item, str):
            tasks[item]()
        elif isinstance(item[0], int):
            stage(*item)
        else:
            name, first, end, marks = item

            @pl.loop(first, end)
            def _(step, name=name, marks=marks):
                families[name](step)
                for at, stages in marks:

                    @pl.when(step == at)
                    def _(stages=stages):
                        for k in stages:
                            stage(*k)


PIECES = (
    ("s", 0, 0, 128, False),
    ("a", 0, 0, 384, False),
    ("a", 1, 0, 384, False),
    ("a", 2, 0, 384, False),
    ("a", 3, 0, 384, False),
    ("b", 0, 0, 768, False),
    ("b", 0, 768, 768, False),
    ("b", 1, 0, 768, False),
    ("b", 1, 768, 768, False),
)
NP = len(PIECES)
HALF = {"a": 384, "b": 1536}


class Gather:
    def __init__(self, place, shards, fulls, sems):
        self.place, self.shards, self.fulls = place, shards, fulls
        self.send, self.recv, self.zs, self.zr, self.cs, self.cr, self.ls = sems

    def full(self, p, idx):
        name, m, col, width, _ = PIECES[p]
        ref = self.fulls[name]
        c = self.place.c
        if name == "s":
            return ref.at[(c,) + idx]
        cols = pl.ds(pl.multiple_of(c * HALF[name] + col, 128), width)
        return ref.at[(m,) + idx + (ALL, cols)]

    def own(self, p):
        name, m, col, width, _ = PIECES[p]
        return self.shards[name, m].at[:, pl.ds(col, width)]

    def mine(self, p):
        pp = self.place
        return self.full(p, (pp.z, pp.y, pp.x))

    def zcopy(self, p, k):
        pp = self.place
        if PIECES[p][4]:
            src = dst = self.full(p, (pp.z, ALL, ALL))
        else:
            src, dst = self.own(p), self.mine(p)
        return remote(src, dst, self.zs.at[p, k - 1], self.zr.at[p, k - 1], pp.zdev(k))

    def local(self, p):
        return pltpu.make_async_copy(self.own(p), self.mine(p), self.ls.at[p])

    def hop(self, p, kind, k):
        pp = self.place
        zz = lax.rem(pp.z - k + pp.zs, pp.zs)
        dst = self.full(p, (zz, pp.y, pp.x) if kind < 2 else (zz, pp.one_y, pp.one_x))
        src = self.own(p) if kind < 2 and k == 0 else dst
        return remote(src, dst, self.send.at[p, kind, k], self.recv.at[p, kind, k], pp.one if kind == 0 else pp.two)

    def pair(self, p):
        s = self.full(p, (ALL, ALL, ALL))
        return remote(s, s, self.cs.at[p], self.cr.at[p], self.place.pair)

    def stage(self, p, k):
        zs = self.place.zs
        plane_first = PIECES[p][4]
        if k == 0:
            if not plane_first:
                for j in range(1, zs):
                    self.zcopy(p, j).start()
            self.local(p).start()
        elif k == 5:
            self.hop(p, 0, 0).start()
            self.hop(p, 1, 0).start()
        elif plane_first:
            if k == 1:
                self.hop(p, 0, 0).wait_recv()
                self.hop(p, 2, 0).start()
            elif k == 2:
                self.local(p).wait()
                self.hop(p, 1, 0).wait_recv()
                self.hop(p, 2, 0).wait_recv()
                for j in range(1, zs):
                    self.zcopy(p, j).start()
            elif k == 3:
                for j in range(1, zs):
                    self.zcopy(p, j).wait_recv()
                self.pair(p).start()
            else:
                self.pair(p).wait_recv()
        elif k == 1:
            self.hop(p, 0, 0).wait_recv()
            self.hop(p, 2, 0).start()
            for j in range(1, zs):
                self.zcopy(p, j).wait_recv()
                self.hop(p, 0, j).start()
                self.hop(p, 1, j).start()
        elif k == 2:
            for j in range(1, zs):
                self.hop(p, 0, j).wait_recv()
                self.hop(p, 2, j).start()
        elif k == 3:
            self.local(p).wait()
            for j in range(zs):
                self.hop(p, 1, j).wait_recv()
                self.hop(p, 2, j).wait_recv()
            self.pair(p).start()
        else:
            self.pair(p).wait_recv()

    def finish(self):
        for p in range(NP):
            for k in range(1, self.place.zs):
                self.zcopy(p, k).wait_send()
            for kind in range(3):
                for k in range(1 if PIECES[p][4] else self.place.zs):
                    self.hop(p, kind, k).wait_send()
            self.pair(p).wait_send()


def forward_kernel(zs, images, plan, *refs):
    (qkv_w, out_w, up_w, dn_w, tok_r, cot_r), tiny = refs[:6], refs[6:14]
    (lo_o, vec, upb_o, wa_o, wb_o, h1t_o, qkv_o, p_o, att_o, mid_o, h2t_o, gp_o, tok_o, cot_o, gdn_o) = refs[14:29]
    (wa, wb, sv, s_sh, s_wide, h1, qkv, pbuf, att, mid, hid, gp, tok, cot, cott, h1t, gdn, psem, osem, gsem, gpsem) = refs[29:50]
    sems = refs[50:]
    place = Place(zs)
    c = place.c
    n = zs * Y * X
    saves = []
    early = pltpu.make_async_copy(h1t, h1t_o, osem.at[15])
    middle = pltpu.make_async_copy(mid, mid_o, osem.at[14])
    h2 = h1

    def save(src, dst):
        copy = pltpu.make_async_copy(src, dst, osem.at[len(saves)])
        copy.start()
        saves.append(copy)

    s_wide[...] = jnp.zeros_like(s_wide)
    row = 0
    for ref in tiny:
        value = ref[...].astype(F32)
        s_wide[row : row + value.shape[0], 0 : value.shape[1]] = value
        row += value.shape[0]
    s_sh[...] = s_wide[...].astype(BF)
    place.greet()
    shards = {("s", 0): s_sh, ("b", 0): up_w, ("b", 1): dn_w, ("a", 3): out_w}
    for t in range(3):
        shards["a", t] = qkv_w.at[t]
    g = Gather(place, shards, {"a": wa, "b": wb, "s": sv}, sems)

    def rows_of(i):
        return pl.ds(pl.multiple_of(i * SP, 16), SP)

    def cut(v):
        return v.reshape(zs, Y, X, 48, v.shape[1])

    def pad():
        tok[...] = padded(tok_r[...].astype(F32), images).astype(BF)
        cot_f = cot_r[...].astype(F32)
        cot[...] = padded(cot_f, images).astype(BF)
        vec[16:17, :] = jnp.sum(cot_f, axis=0, keepdims=True)
        save(tok, tok_o)
        save(cot, cot_o)

    def ct():
        cott[...] = cot[...].T

    def prep():
        flat = sv[...].reshape(2 * n * 16, 128)
        cell, cell_up = 768 // (2 * n), 1536 // n
        lane = lax.broadcasted_iota(jnp.int32, (128, 768), 0)
        col = lax.rem(lax.broadcasted_iota(jnp.int32, (128, 768), 1), cell)
        spread = dot(flat, (col == lane).astype(BF)).reshape(2 * n, 16, 768)
        who = lax.broadcasted_iota(jnp.int32, (2 * n, 16, 768), 0)
        kind = lax.broadcasted_iota(jnp.int32, (2 * n, 16, 768), 1)
        spot = lax.broadcasted_iota(jnp.int32, (2 * n, 16, 768), 2) // cell
        r_of, c_of = lax.rem(who, n), who // n
        mine = jnp.where(kind < 6, 2 * r_of + c_of, n * c_of + r_of)
        vec[0:16, :] = jnp.sum(jnp.where(mine == spot, spread, 0.0), axis=0)
        row = lax.broadcasted_iota(jnp.int32, (2 * n, 2 * n * 16), 0)
        col = lax.broadcasted_iota(jnp.int32, (2 * n, 2 * n * 16), 1)
        up_rows = dot((col == row * 16 + 8).astype(BF), flat).astype(BF)
        lane = lax.broadcasted_iota(jnp.int32, (128, 3072), 0)
        col = lax.rem(lax.broadcasted_iota(jnp.int32, (128, 3072), 1), cell_up)
        spread = dot(up_rows, (col == lane).astype(BF))
        who = lax.broadcasted_iota(jnp.int32, (2 * n, 3072), 0)
        spot = lax.broadcasted_iota(jnp.int32, (2 * n, 3072), 1) // cell_up
        upb_o[...] = jnp.sum(jnp.where(who == spot, spread, 0.0), axis=0, keepdims=True)

        @pl.loop(0, images)
        def _(i):
            v, _r = center(tok[rows_of(i), :].astype(F32))
            h1[rows_of(i), :] = (v * vec[0:1, :] + vec[1:2, :]).astype(BF)

    def project(t):
        r = dot(h1[...], wa[t].reshape(768, 768))
        if t == 0:
            r = (r + vec[6:7, :]).astype(BF) * jnp.asarray(HD**-0.5, BF)
        elif t == 2:
            r = r + vec[7:8, :]
        qkv[t] = r.astype(BF)
        if t == 2:
            save(qkv, qkv_o)
            h1t[...] = h1[...].T
            early.start()

    def pcopy(step):
        return pltpu.make_async_copy(pbuf.at[step % 2], p_o.at[step], psem.at[step % 2])

    def attention(step):
        @pl.when(step >= 2)
        def _():
            pcopy(step - 2).wait()

        for j in range(3):
            cols = slice(j * QUAD, (j + 1) * QUAD)
            head = lax.broadcasted_iota(jnp.int32, (SP, QUAD), 1) // HD
            q = qkv[0, rows_of(step), cols]
            zero = jnp.zeros_like(q)
            q4 = jnp.concatenate([jnp.where(head == h, q, zero) for h in range(4)], axis=0)
            s = dot(qkv[1, rows_of(step), cols], q4, 1, 1)
            key = lax.broadcasted_iota(jnp.int32, (SP, 1), 0)
            s = jnp.where(key < SEQ, s, -jnp.inf)
            e = jnp.exp(s - jnp.max(s, axis=0, keepdims=True))
            p = (e * (1.0 / jnp.sum(e, axis=0, keepdims=True))).astype(BF)
            pbuf[step % 2, j] = p
            o4 = dot(p, qkv[2, rows_of(step), cols], 0, 0)
            o = jnp.zeros((SP, QUAD), F32)
            for h in range(4):
                o = jnp.where(head == h, o4[h * SP : (h + 1) * SP], o)
            att[rows_of(step), cols] = o.astype(BF)
        pcopy(step).start()

    def out():
        for k in (images - 2, images - 1):
            pcopy(k).wait()
        save(att, att_o)
        for j in range(3):
            w = wa[3].reshape(768, 768)[j * 256 : (j + 1) * 256, :]
            cols = slice(j * 256, (j + 1) * 256)
            mid[:, cols] = tok[:, cols].astype(F32) + (dot(att[...], w, 1, 1) + vec[2:3, cols])

        @pl.loop(0, images)
        def _(i):
            v, _r = center(mid[rows_of(i), :])
            h2[rows_of(i), :] = (v * vec[3:4, :] + vec[4:5, :]).astype(BF)

        middle.start()
        save(wa, wa_o)

    def part(piece, half):
        return pl.ds(pl.multiple_of(half * 1536 + piece * 768, 256), 768)

    def expand(step):
        cols = part(step // 2, step % 2)
        pre = dot(h2[...], wb[0, :, :, :, :, cols].reshape(768, 768)) + upb_o[:, cols]
        cdf = 0.5 + 0.5 * lax.erf(pre * (0.5**0.5))
        pdf = jnp.exp(pre * pre * -0.5) * 0.3989422804014327
        hid[:, cols] = (pre * cdf).astype(BF)
        gp[:, cols] = (cdf + pre * pdf).astype(BF)
        gpcopy(step).start()

    def gpcopy(k):
        cols = part(k // 2, k % 2)
        return pltpu.make_async_copy(gp.at[:, cols], gp_o.at[:, cols], gpsem.at[k])

    def save_up():
        save(wb.at[0], wb_o.at[0])

    def save_down(piece):
        for half in range(2):
            cols = slice(half * 1536 + piece * 768, half * 1536 + piece * 768 + 768)
            save(wb.at[1, :, :, :, :, cols], wb_o.at[1, :, :, :, :, cols])

    def gcopy(piece, own):
        return pltpu.make_async_copy(gdn.at[piece, own], gdn_o.at[piece, own], gsem.at[piece, own])

    def grad_down(step):
        piece, own = step // 2, step % 2
        cols = part(piece, 1 - own - c + 2 * own * c)
        gdn[piece, own] = cut(dot(cott[...], hid[:, cols]).astype(BF))
        gcopy(piece, own).start()

    def contract(piece):
        if piece == 0:
            middle.wait()
        for j in range(3):
            cols = slice(j * 256, (j + 1) * 256)
            total = mid[:, cols] + vec[5:6, cols] if piece == 0 else mid[:, cols]
            for half in range(2):
                fc = slice(half * 1536 + piece * 768, half * 1536 + piece * 768 + 768)
                w = wb[1, :, :, :, :, fc].reshape(768, 768)[j * 256 : (j + 1) * 256, :]
                total = total + dot(hid[:, fc], w, 1, 1)
            if piece == 0:
                mid[:, cols] = total
            else:
                lo_o[:, cols] = unpadded(total, images).astype(BF)
        if piece == 0:
            early.wait()
            h1t[...] = h2[...].T
            save(h1t, h2t_o)

    tasks = {"pad": pad, "ct": ct, "prep": prep, "out": out}
    for t in range(3):
        tasks["qkv"[t]] = functools.partial(project, t)
    for k in range(2):
        tasks[f"ct{k}"] = functools.partial(contract, k)
        tasks[f"sd{k}"] = functools.partial(save_down, k)
    tasks["su"] = save_up
    perform(plan, tasks, {"at": attention, "ex": expand, "gd": grad_down}, g.stage)
    g.finish()
    for k in range(4):
        gcopy(k // 2, k % 2).wait()
        gpcopy(k).wait()
    for copy in saves:
        copy.wait()


def forward(qkv_w, out_w, up_w, dn_w, tok, cot, tiny, zs, images, plan):
    rows = images * SP
    S = jax.ShapeDtypeStruct
    V = pltpu.VMEM
    dims = (zs, Y, X)
    outs = (
        S((images * SEQ, 768), BF), S((24, 768), F32), S((1, 3072), F32),
        S((4,) + dims + (48, 768), BF), S((2,) + dims + (48, 3072), BF), S((768, rows), BF), S((3, rows, 768), BF),
        S((images, 3, SP, 4 * SP), BF), S((rows, 768), BF), S((rows, 768), F32), S((768, rows), BF),
        S((rows, 3072), BF), S((rows, 768), BF), S((rows, 768), BF), S((2, 2) + dims + (48, 768), BF),
    )
    anys = pl.BlockSpec(memory_space=pl.ANY)
    vm = pl.BlockSpec(memory_space=pltpu.VMEM)
    return pl.pallas_call(
        functools.partial(forward_kernel, zs, images, plan),
        out_shape=outs,
        in_specs=[vm] * 14,
        out_specs=[vm] * 3 + [anys] * 12,
        scratch_shapes=[
            V((4,) + dims + (48, 768), BF), V((2,) + dims + (48, 3072), BF), V((2,) + dims + (16, 128), BF), V((16, 128), BF), V((16, 128), F32),
            V((rows, 768), BF), V((3, rows, 768), BF), V((2, 3, SP, 4 * SP), BF), V((rows, 768), BF), V((rows, 768), F32),
            V((rows, 3072), BF), V((rows, 3072), BF),
            V((rows, 768), BF), V((rows, 768), BF), V((768, rows), BF), V((768, rows), BF), V((2, 2) + dims + (48, 768), BF),
            DMA((2,)), DMA((16,)), DMA((2, 2)), DMA((4,)),
            DMA((NP, 3, zs)), DMA((NP, 3, zs)), DMA((NP, zs - 1)), DMA((NP, zs - 1)), DMA((NP,)), DMA((NP,)), DMA((NP,)),
        ],
        compiler_params=pltpu.CompilerParams(collective_id=1, has_side_effects=True, vmem_limit_bytes=60 * 2**20),
        name="gather_forward",
    )(qkv_w, out_w, up_w, dn_w, tok, cot, *tiny)


FORWARD = (
    (1, 0), (1, 5), (2, 0), (3, 0), (0, 0), (5, 0), (5, 5), (4, 0), "pad", (3, 5), (0, 5), (6, 0), (7, 0), (2, 5),
    (6, 5), "ct", (7, 5), (4, 5), (1, 1), (2, 1), (0, 1), (1, 2), (3, 1), (2, 2), (3, 2), (0, 2), (1, 3), (5, 1),
    (2, 3), (4, 1), (0, 3), (3, 3), (6, 1), (2, 4), (0, 4), "prep", (1, 4), (4, 2), (5, 2), "q", (3, 4), "k", (8, 0),
    "v", (6, 2), (7, 1), ("at", 0, 4, ((0, ((4, 3),)), (2, ((4, 4), (8, 5), (5, 3))))), "out", (6, 3), (7, 2),
    (8, 1), (5, 4), ("ex", 0, 3, ((1, ((6, 4),)),)), ("gd", 0, 1, ()), "su", (7, 3), (8, 2), ("ex", 3, 4, ()),
    ("gd", 1, 3, ()), (7, 4), "sd0", (8, 3), ("gd", 3, 4, ()), "ct0", (8, 4), "sd1", "ct1",
)

BACKWARD = (
    "down", (0, 0), (1, 0), "rdy", ("pr", 0, 4, ((2, ((0, 1),)),)), "trn",
    ("up", 0, 4, ((0, ((2, 0), (1, 1))), (2, ((0, 2),)))), "ud", (3, 0), "dh2", "dh1", (2, 1), "dh0", (0, 3), (1, 2),
    "nm2", "og", "da", (2, 2),
    ("at", 0, 12, ((1, ((3, 1),)), (2, ((4, 0),)), (5, ((1, 3),)), (8, ((0, 4), (2, 3), (4, 1))), (9, ((3, 2),)))),
    "gq", (5, 0), "gk", (6, 0), (1, 4), (4, 2), "gv", (5, 1), (7, 0), (6, 1), (3, 3), "di0", (4, 3), "di1", (7, 1),
    (5, 2), "di2", "nm1", (6, 2), "sm", (8, 0), (5, 3), (8, 1), (7, 2), (2, 4), (6, 3), "fin", (8, 2), (3, 4),
    (7, 3), (8, 3), (4, 4), (6, 4), (5, 4), (7, 4), (8, 4),
)


SPIECES = (
    ("b", 1, 0, 768),
    ("b", 1, 768, 768),
    ("b", 0, 0, 768),
    ("b", 0, 768, 768),
    ("a", 3, 0, 384),
    ("a", 0, 0, 384),
    ("a", 1, 0, 384),
    ("a", 2, 0, 384),
    ("s", 0, 0, 128),
)
NS = len(SPIECES)


class Scatter:
    def __init__(self, place, gdn, gout, gs, wb, pb, pa, psm, rb, ra, rs, outs, sems):
        self.place = place
        self.gdn, self.gout, self.gs_, self.wb = gdn, gout, gs, wb
        self.pbuf = {"b": pb, "a": pa, "s": psm}
        self.rbuf = {"b": rb, "a": ra, "s": rs}
        self.outs = outs
        self.send, self.recv_, self.z_send, self.z_recv = sems

    def index(self, p):
        return p if p < 4 else (p - 4 if p < 8 else 0)

    def part(self, p, own):
        if p < 2:
            return self.gdn.at[p, own]
        if p < 4:
            cols = pl.ds(pl.multiple_of((p - 2) * 1536 + own * 768, 128), 768)
            return self.wb.at[1, :, :, :, :, cols]
        if p == 4:
            return self.gout.at[own]
        if p < 8:
            k = p - 5
            return self.gdn.at[k // 2, own, :, :, :, :, pl.ds((k % 2) * 384, 384)]
        return self.gs_.at[own]

    def precv(self, p):
        return self.pbuf[SPIECES[p][0]].at[self.index(p)]

    def recv(self, p, k):
        return self.rbuf[SPIECES[p][0]][k].at[self.index(p)]

    def pair(self, p):
        return remote(self.part(p, 0), self.precv(p), self.send.at[p, 0], self.recv_.at[p, 0], self.place.pair)

    def hop(self, p, k):
        pp, s = self.place, self.part(p, 1)
        y, x = ((1 - pp.y, 1 - pp.x), (pp.two_y, pp.two_x), (pp.one_y, pp.one_x))[k - 1]
        return remote(
            s.at[:, y, x], self.recv(p, k - 1), self.send.at[p, k], self.recv_.at[p, k], pp.one if k == 3 else pp.two
        )

    def three(self, p, k):
        pp, s = self.place, self.part(p, 1)
        to = lax.rem(pp.z + k, pp.zs)
        return remote(
            s.at[to, pp.y, pp.x], self.recv(p, 3).at[k - 1], self.z_send.at[p, k - 1], self.z_recv.at[p, k - 1], pp.zdev(k)
        )

    def stage(self, p, k):
        pp = self.place
        zs = pp.zs
        kind = F32 if p == 8 else BF
        s = self.part(p, 1)
        if k == 0:
            self.pair(p).start()
        elif k == 1:
            self.pair(p).wait_recv()
            r = self.precv(p)
            for zz in range(zs):
                s[zz] = (s[zz].astype(F32) + r[zz].astype(F32)).astype(kind)
            self.hop(p, 1).start()
            self.hop(p, 2).start()
        elif k == 2:
            self.hop(p, 1).wait_recv()
            r = self.recv(p, 0)
            for zz in range(zs):
                at = (zz, pp.one_y, pp.one_x)
                s[at] = (s[at].astype(F32) + r[zz].astype(F32)).astype(kind)
            self.hop(p, 3).start()
        elif k == 3:
            self.hop(p, 2).wait_recv()
            self.hop(p, 3).wait_recv()
            ra, rb = self.recv(p, 1), self.recv(p, 2)
            for zz in range(zs):
                at = (zz, pp.y, pp.x)
                s[at] = (s[at].astype(F32) + ra[zz].astype(F32) + rb[zz].astype(F32)).astype(kind)
            for k in range(1, zs):
                self.three(p, k).start()
        else:
            r = self.recv(p, 3)
            total = s[pp.z, pp.y, pp.x].astype(F32)
            for k in range(1, zs):
                self.three(p, k).wait_recv()
                total = total + r[k - 1].astype(F32)
            name, m, col, width = SPIECES[p]
            self.outs[name, m][:, pl.ds(col, width)] = total
            self.pair(p).wait_send()
            for k in range(1, 4):
                self.hop(p, k).wait_send()
            for k in range(1, zs):
                self.three(p, k).wait_send()


def backward_kernel(zs, images, plan, *refs):
    (vec, wa_i, wb_i, h1t_i, qkv_i, p_i, att_i, mid_i, h2t_i, gp_i, tok_i, cot_i, gdn_i) = refs[:13]
    dx_o, gq_o, go_o, gu_o, gd_o, gs_o = refs[13:19]
    (wa, wb, cot, qkv, att, mid, dh, dpre, db, pt, xt, yt, vg, ug, gdn, gout, gs) = refs[19:36]
    pb, pa, psm = refs[36:39]
    rb, ra, rs = refs[39:43], refs[43:47], refs[47:51]
    lsem, psem = refs[51:53]
    sems = refs[53:]
    n = zs * Y * X
    place = Place(zs)
    c = place.c
    outs = {("b", 0): gu_o, ("b", 1): gd_o, ("a", 3): go_o, ("s", 0): gs_o}
    for t in range(3):
        outs["a", t] = gq_o.at[t]
    sc = Scatter(place, gdn, gout, gs, wb, pb, pa, psm, rb, ra, rs, outs, sems)

    loads = {
        "gdn": (gdn_i, gdn), "cot": (cot_i, cot), "dn": (wb_i.at[1], wb.at[1]), "gp": (gp_i, dpre), "h2t": (h2t_i, yt),
        "up": (wb_i.at[0], wb.at[0]), "mid": (mid_i, mid), "att": (att_i, att), "wa": (wa_i, wa), "qkv": (qkv_i, qkv),
        "tok": (tok_i, cot), "h1t": (h1t_i, yt),
    }
    names = list(loads)

    def load(name):
        src, dst = loads[name]
        return pltpu.make_async_copy(src, dst, lsem.at[names.index(name)])

    for name in names[:-2]:
        load(name).start()
    place.greet()

    def rows_of(i):
        return pl.ds(pl.multiple_of(i * SP, 16), SP)

    def cut(v):
        return v.reshape(zs, Y, X, 48, v.shape[1])

    def ptile(step):
        return pltpu.make_async_copy(p_i.at[step // 3, step % 3], pt.at[step % 2], psem.at[step % 2])

    ptile(0).start()
    vg[...] = jnp.zeros_like(vg)
    vg[5:6, :] = vec[16:17, :]

    def down():
        load("gdn").wait()

    def ready():
        load("cot").wait()
        load("dn").wait()
        load("gp").wait()

    def pre(step):
        cols = pl.ds(pl.multiple_of(step * 768, 256), 768)
        w = wb[1, :, :, :, :, cols].reshape(768, 768)
        d = (dot(cot[...], w) * dpre[:, cols].astype(F32)).astype(BF)
        dpre[:, cols] = d
        ug[:, cols] = jnp.sum(d.astype(F32), axis=0, keepdims=True)

    def grad_up(step):
        piece, own = step // 2, step % 2
        half = 1 - own - c + 2 * own * c
        cols = pl.ds(pl.multiple_of(half * 1536 + piece * 768, 256), 768)
        dest = pl.ds(pl.multiple_of(step * 768, 256), 768)
        wb[1, :, :, :, :, dest] = cut(dot(yt[...], dpre[:, cols]).astype(BF))

    def turned():
        load("h2t").wait()

    def up_done():
        load("h1t").start()
        load("up").wait()

    def d_h2(j):
        w = wb[0].reshape(768, 3072)[j * 256 : (j + 1) * 256, :]
        dh[:, j * 256 : (j + 1) * 256] = dot(dpre[...], w, 1, 1)

    def norm2():
        load("mid").wait()

        @pl.loop(0, images)
        def _(i):
            v, r = center(mid[rows_of(i), :])
            g = dh[rows_of(i), :]
            vg[3:4, :] += jnp.sum(g * v, axis=0, keepdims=True)
            vg[4:5, :] += jnp.sum(g, axis=0, keepdims=True)
            dn = g * vec[3:4, :]
            d = cot[rows_of(i), :].astype(F32) + r * (
                dn - jnp.mean(dn, axis=-1, keepdims=True) - v * jnp.mean(dn * v, axis=-1, keepdims=True)
            )
            dh[rows_of(i), :] = d
            low = d.astype(BF)
            db[rows_of(i), :] = low
            vg[2:3, :] += jnp.sum(low.astype(F32), axis=0, keepdims=True)

        load("tok").start()

    def grad_out():
        xt[...] = db[...].T
        load("att").wait()
        for h in range(2):
            own = 1 - h - c + 2 * h * c
            gout[own] = cut(dot(xt[...], att[:, h * 384 : (h + 1) * 384]).astype(BF))

    def d_att():
        load("wa").wait()
        load("qkv").wait()

        @pl.loop(0, 3)
        def _(j):
            cols = pl.ds(pl.multiple_of(j * 256, 256), 256)
            att[:, cols] = dot(db[...], wa[3, :, :, :, :, cols].reshape(768, 256)).astype(BF)

    total = images * 3

    def attention(step):
        if True:
            i, j = step // 3, step % 3
            cols = pl.ds(pl.multiple_of(j * QUAD, QUAD), QUAD)
            ptile(step).wait()

            @pl.when(step + 1 < total)
            def _():
                ptile(step + 1).start()

            head = lax.broadcasted_iota(jnp.int32, (SP, QUAD), 1) // HD
            q, k, v, do = qkv[0, rows_of(i), cols], qkv[1, rows_of(i), cols], qkv[2, rows_of(i), cols], att[rows_of(i), cols]
            zero = jnp.zeros_like(q)
            q4 = jnp.concatenate([jnp.where(head == h, q, zero) for h in range(4)], axis=0)
            do4 = jnp.concatenate([jnp.where(head == h, do, zero) for h in range(4)], axis=0)
            p = pt[step % 2]
            dp = dot(v, do4, 1, 1)
            dv = dot(p, do4)
            pf = p.astype(F32)
            ds = (pf * (dp - jnp.sum(pf * dp, axis=0, keepdims=True))).astype(BF)
            dq4 = dot(ds, k, 0, 0)
            dk = dot(ds, q4)
            dq = jnp.zeros((SP, QUAD), F32)
            for h in range(4):
                dq = jnp.where(head == h, dq4[h * SP : (h + 1) * SP], dq)
            qkv[0, rows_of(i), cols] = (dq * HD**-0.5).astype(BF)
            qkv[1, rows_of(i), cols] = dk.astype(BF)
            qkv[2, rows_of(i), cols] = dv.astype(BF)

    def grad_qkv(t):
        if t == 0:
            load("h1t").wait()
        for h in range(2):
            own = 1 - h - c + 2 * h * c
            gdn[t // 2, own, :, :, :, :, (t % 2) * 384 : (t % 2) * 384 + 384] = cut(
                dot(yt[...], qkv[t, :, h * 384 : (h + 1) * 384]).astype(BF)
            )
        if t != 1:
            vg[6 + t // 2 : 7 + t // 2, :] = jnp.sum(qkv[t].astype(F32), axis=0, keepdims=True)

    def d_h1(j):
        cols = slice(j * 256, (j + 1) * 256)
        sum_ = None
        for t in range(3):
            w = wa[t].reshape(768, 768)[cols, :]
            r = dot(qkv[t], w, 1, 1)
            sum_ = r if sum_ is None else sum_ + r
        mid[:, cols] = sum_

    def norm1():
        load("tok").wait()

        @pl.loop(0, images)
        def _(i):
            v, r = center(cot[rows_of(i), :].astype(F32))
            g = mid[rows_of(i), :]
            vg[0:1, :] += jnp.sum(g * v, axis=0, keepdims=True)
            vg[1:2, :] += jnp.sum(g, axis=0, keepdims=True)
            dn = g * vec[0:1, :]
            mid[rows_of(i), :] = dh[rows_of(i), :] + r * (
                dn - jnp.mean(dn, axis=-1, keepdims=True) - v * jnp.mean(dn * v, axis=-1, keepdims=True)
            )

    def two_parts(v):
        hi = v.astype(BF)
        return hi, (v - hi.astype(F32)).astype(BF)

    def small_blocks():
        cell, cell_up = 768 // (2 * n), 1536 // n
        who = lax.broadcasted_iota(jnp.int32, (2 * n, 16, 768), 0)
        kind = lax.broadcasted_iota(jnp.int32, (2 * n, 16, 768), 1)
        spot = lax.broadcasted_iota(jnp.int32, (2 * n, 16, 768), 2) // cell
        r_of, c_of = lax.rem(who, n), who // n
        mine = jnp.where(kind < 6, 2 * r_of + c_of, n * c_of + r_of)
        mixed = jnp.where(mine == spot, vg[...][None], 0.0).reshape(2 * n * 16, 768)
        col = lax.rem(lax.broadcasted_iota(jnp.int32, (768, 128), 0), cell)
        pick = (col == lax.broadcasted_iota(jnp.int32, (768, 128), 1)).astype(BF)
        small = sum(dot(part, pick) for part in two_parts(mixed)).reshape(2 * n, 16, 128)
        who = lax.broadcasted_iota(jnp.int32, (2 * n, 3072), 0)
        spot = lax.broadcasted_iota(jnp.int32, (2 * n, 3072), 1) // cell_up
        mixed = jnp.where(who == spot, ug[...], 0.0)
        col = lax.rem(lax.broadcasted_iota(jnp.int32, (3072, 128), 0), cell_up)
        pick = (col == lax.broadcasted_iota(jnp.int32, (3072, 128), 1)).astype(BF)
        up_part = sum(dot(part, pick) for part in two_parts(mixed)).reshape(2 * n, 1, 128)
        kind = lax.broadcasted_iota(jnp.int32, (2 * n, 16, 128), 1)
        small = jnp.where(kind == 8, up_part, small).reshape(2, zs, Y, X, 16, 128)
        for h in range(2):
            gs[1 - h - c + 2 * h * c] = small[h]

    def finish():
        dx_o[...] = unpadded(mid[...], images)

    tasks = {
        "down": down, "nm2": norm2, "og": grad_out, "da": d_att, "nm1": norm1, "sm": small_blocks, "fin": finish,
        "rdy": ready, "trn": turned, "ud": up_done,
    }
    for j in range(3):
        tasks[f"dh{j}"] = functools.partial(d_h2, j)
        tasks["g" + "qkv"[j]] = functools.partial(grad_qkv, j)
        tasks[f"di{j}"] = functools.partial(d_h1, j)
    perform(plan, tasks, {"pr": pre, "up": grad_up, "at": attention}, sc.stage)


def backward(saved, zs, images, plan):
    rows = images * SP
    S = jax.ShapeDtypeStruct
    V = pltpu.VMEM
    dims = (zs, Y, X)
    anys = pl.BlockSpec(memory_space=pl.ANY)
    vm = pl.BlockSpec(memory_space=pltpu.VMEM)

    def inbox(count, rows_, width, kind):
        return [V((count, zs, rows_, width), kind)] * 3 + [V((count, zs - 1, rows_, width), kind)]

    return pl.pallas_call(
        functools.partial(backward_kernel, zs, images, plan),
        out_shape=(
            S((images * SEQ, 768), F32), S((3, 48, 384), F32), S((48, 384), F32), S((48, 1536), F32), S((48, 1536), F32), S((16, 128), F32),
        ),
        in_specs=[vm] + [anys] * 12,
        out_specs=[vm] * 6,
        scratch_shapes=[
            V((4,) + dims + (48, 768), BF), V((2,) + dims + (48, 3072), BF), V((rows, 768), BF),
            V((3, rows, 768), BF), V((rows, 768), BF), V((rows, 768), F32), V((rows, 768), F32), V((rows, 3072), BF),
            V((rows, 768), BF), V((2, SP, 4 * SP), BF), V((768, rows), BF), V((768, rows), BF),
            V((16, 768), F32), V((1, 3072), F32),
            V((2, 2) + dims + (48, 768), BF), V((2,) + dims + (48, 384), BF), V((2,) + dims + (16, 128), F32),
            V((4,) + dims + (48, 768), BF), V((4,) + dims + (48, 384), BF), V((1,) + dims + (16, 128), F32),
        ]
        + inbox(4, 48, 768, BF)
        + inbox(4, 48, 384, BF)
        + inbox(1, 16, 128, F32)
        + [
            DMA((12,)), DMA((2,)),
            DMA((NS, 4)), DMA((NS, 4)), DMA((NS, zs - 1)), DMA((NS, zs - 1)),
        ],
        compiler_params=pltpu.CompilerParams(collective_id=2, has_side_effects=True, vmem_limit_bytes=60 * 2**20),
        name="backward_scatter",
    )(*saved)


def normalize(values):
    centered = values - jnp.mean(values, axis=-1, keepdims=True)
    inverse = lax.rsqrt(jnp.mean(centered * centered, axis=-1, keepdims=True) + EPS)
    return (centered * inverse, inverse)


def norm_back(grad_out, normed, inverse, gain):
    d_normed = grad_out * gain
    grad_in = inverse * (
        d_normed
        - jnp.mean(d_normed, axis=-1, keepdims=True)
        - normed * jnp.mean(d_normed * normed, axis=-1, keepdims=True)
    )
    return (grad_in, jnp.sum(grad_out * normed, axis=0), jnp.sum(grad_out, axis=0))


def gather_rows(rows):
    return lax.all_gather(rows, "tensor", axis=0, tiled=True)


def sum_rows(terms):
    return lax.psum_scatter(
        terms.astype(jnp.bfloat16), "tensor", scatter_dimension=0, tiled=True
    ).astype(jnp.float32)


def gather_grads(rows):
    return lax.all_gather(rows, "tensor", axis=0, tiled=True)


def sum_grads(terms):
    return lax.psum_scatter(
        terms.astype(jnp.bfloat16), "tensor", scatter_dimension=0, tiled=True
    ).astype(jnp.float32)


def split_heads(matrix):
    return matrix.reshape(matrix.shape[0] // SEQ, SEQ, matrix.shape[1] // HD, HD)


def attend(queries, keys, values):
    scores = jnp.einsum(
        "iqhd,ikhd->ihqk", queries, keys, preferred_element_type=jnp.float32
    ) * HD ** (-0.5)
    row_top = jnp.max(scores, axis=-1, keepdims=True)
    shifted = jnp.exp(scores - row_top)
    row_total = jnp.sum(shifted, axis=-1, keepdims=True)
    probs = (shifted / row_total).astype(jnp.bfloat16)
    attended = jnp.einsum("ihqk,ikhd->iqhd", probs, values, preferred_element_type=jnp.float32)
    return (attended.astype(jnp.bfloat16), row_top + jnp.log(row_total))


def attend_back(queries, keys, values, log_total, d_attended):
    factor = HD ** (-0.5)
    scores = (
        jnp.einsum("iqhd,ikhd->ihqk", queries, keys, preferred_element_type=jnp.float32) * factor
    )
    probs = jnp.exp(scores - log_total)
    probs_low = probs.astype(jnp.bfloat16)
    grad_values = jnp.einsum(
        "ihqk,iqhd->ikhd", probs_low, d_attended, preferred_element_type=jnp.float32
    ).astype(jnp.bfloat16)
    d_probs = jnp.einsum("iqhd,ikhd->ihqk", d_attended, values, preferred_element_type=jnp.float32)
    d_scores = (probs * (d_probs - jnp.sum(probs * d_probs, axis=-1, keepdims=True))).astype(
        jnp.bfloat16
    )
    grad_queries = (
        jnp.einsum("ihqk,ikhd->iqhd", d_scores, keys, preferred_element_type=jnp.float32) * factor
    ).astype(jnp.bfloat16)
    grad_keys = (
        jnp.einsum("ihqk,iqhd->ikhd", d_scores, queries, preferred_element_type=jnp.float32)
        * factor
    ).astype(jnp.bfloat16)
    return (grad_queries, grad_keys, grad_values)


def local(
    tokens,
    cotangent,
    norm1_gain,
    norm1_shift,
    qkv_weight,
    qv_bias,
    out_weight,
    out_bias,
    norm2_gain,
    norm2_shift,
    up_weight,
    up_bias,
    down_weight,
    down_bias,
):
    small_full = (
        lax.all_gather(norm1_gain, ("dp", "tensor"), axis=0, tiled=True),
        lax.all_gather(norm1_shift, ("dp", "tensor"), axis=0, tiled=True),
        lax.all_gather(out_bias, ("dp", "tensor"), axis=0, tiled=True),
        lax.all_gather(norm2_gain, ("dp", "tensor"), axis=0, tiled=True),
        lax.all_gather(norm2_shift, ("dp", "tensor"), axis=0, tiled=True),
        lax.all_gather(down_bias, ("dp", "tensor"), axis=0, tiled=True),
    )
    gain_one, shift_one, out_vec, gain_two, shift_two, down_vec = [
        item.astype(jnp.float32) for item in small_full
    ]
    qkv_full, qv_full, out_full = (
        lax.all_gather(qkv_weight, "dp", axis=1, tiled=True),
        lax.all_gather(qv_bias, "dp", axis=2, tiled=True),
        lax.all_gather(out_weight, "dp", axis=1, tiled=True),
    )
    inputs = tokens.astype(jnp.float32)
    normed_one, inverse_one = normalize(inputs)
    h_one = gather_rows((normed_one * gain_one + shift_one).astype(jnp.bfloat16))
    projected = jnp.einsum("gd,tde->tge", h_one, qkv_full, preferred_element_type=jnp.float32)
    qv_rows = qv_full.astype(jnp.float32)
    queries = split_heads((projected[0] + qv_rows[0, 0]).astype(jnp.bfloat16))
    keys = split_heads(projected[1].astype(jnp.bfloat16))
    values = split_heads((projected[2] + qv_rows[1, 0]).astype(jnp.bfloat16))
    attended_heads, log_total = attend(queries, keys, values)
    group_rows = h_one.shape[0]
    attended = attended_heads.reshape(group_rows, qkv_full.shape[2])
    branch_one = sum_rows(jnp.dot(attended, out_full, preferred_element_type=jnp.float32)) + out_vec
    middle = inputs + branch_one
    up_full, up_vec, down_full = (
        lax.all_gather(up_weight, "dp", axis=0, tiled=True),
        lax.all_gather(up_bias, "dp", axis=1, tiled=True),
        lax.all_gather(down_weight, "dp", axis=1, tiled=True),
    )
    normed_two, inverse_two = normalize(middle)
    h_two = gather_rows((normed_two * gain_two + shift_two).astype(jnp.bfloat16))
    pre_act = jnp.dot(h_two, up_full, preferred_element_type=jnp.float32) + up_vec[0].astype(
        jnp.float32
    )
    hidden = jax.nn.gelu(pre_act, approximate=False).astype(jnp.bfloat16)
    branch_two = sum_rows(jnp.dot(hidden, down_full, preferred_element_type=jnp.float32)) + down_vec
    layer_out = (middle + branch_two).astype(jnp.bfloat16)
    grad_rows = cotangent.astype(jnp.float32)
    grad_down_bias = jnp.sum(grad_rows, axis=0)
    cot_all = gather_grads(cotangent)
    grad_down = jnp.einsum("gf,gd->fd", hidden, cot_all, preferred_element_type=jnp.float32)
    d_hidden = jnp.einsum("gd,fd->gf", cot_all, down_full, preferred_element_type=jnp.float32)
    gelu_out, gelu_back = jax.vjp(partial(jax.nn.gelu, approximate=False), pre_act)
    d_pre = gelu_back(d_hidden)[0].astype(jnp.bfloat16)
    grad_up_bias = jnp.sum(d_pre.astype(jnp.float32), axis=0)[None, :]
    grad_up = jnp.einsum("gd,gf->df", h_two, d_pre, preferred_element_type=jnp.float32)
    d_h_two = sum_grads(jnp.einsum("gf,df->gd", d_pre, up_full, preferred_element_type=jnp.float32))
    d_middle, grad_gain_two, grad_shift_two = norm_back(d_h_two, normed_two, inverse_two, gain_two)
    d_middle = d_middle + grad_rows
    d_branch = d_middle.astype(jnp.bfloat16)
    grad_out_bias = jnp.sum(d_branch.astype(jnp.float32), axis=0)
    branch_all = gather_grads(d_branch)
    grad_out = jnp.einsum("ge,gd->ed", attended, branch_all, preferred_element_type=jnp.float32)
    d_attended = jnp.einsum(
        "gd,ed->ge", branch_all, out_full, preferred_element_type=jnp.float32
    ).astype(jnp.bfloat16)
    grad_queries, grad_keys, grad_values = attend_back(
        queries, keys, values, log_total, split_heads(d_attended)
    )
    width = qkv_full.shape[2]
    grad_stack = jnp.stack(
        [
            grad_queries.reshape(group_rows, width),
            grad_keys.reshape(group_rows, width),
            grad_values.reshape(group_rows, width),
        ]
    )
    grad_qv = jnp.stack(
        [
            jnp.sum(grad_stack[0].astype(jnp.float32), axis=0),
            jnp.sum(grad_stack[2].astype(jnp.float32), axis=0),
        ]
    )[:, None, :]
    grad_qkv = jnp.einsum("gd,tge->tde", h_one, grad_stack, preferred_element_type=jnp.float32)
    d_h_one = sum_grads(
        jnp.einsum("tge,tde->gd", grad_stack, qkv_full, preferred_element_type=jnp.float32)
    )
    share_qkv, share_qv, share_out, share_up, share_up_bias, share_down = (
        lax.psum_scatter(grad_qkv, "dp", scatter_dimension=1, tiled=True),
        lax.psum_scatter(grad_qv, "dp", scatter_dimension=2, tiled=True),
        lax.psum_scatter(grad_out, "dp", scatter_dimension=1, tiled=True),
        lax.psum_scatter(grad_up, "dp", scatter_dimension=0, tiled=True),
        lax.psum_scatter(grad_up_bias, "dp", scatter_dimension=1, tiled=True),
        lax.psum_scatter(grad_down, "dp", scatter_dimension=1, tiled=True),
    )
    d_input, grad_gain_one, grad_shift_one = norm_back(d_h_one, normed_one, inverse_one, gain_one)
    input_grad = d_middle + d_input
    small_shares = (
        lax.psum_scatter(grad_gain_one, ("dp", "tensor"), scatter_dimension=0, tiled=True),
        lax.psum_scatter(grad_shift_one, ("dp", "tensor"), scatter_dimension=0, tiled=True),
        lax.psum_scatter(grad_out_bias, ("dp", "tensor"), scatter_dimension=0, tiled=True),
        lax.psum_scatter(grad_gain_two, ("dp", "tensor"), scatter_dimension=0, tiled=True),
        lax.psum_scatter(grad_shift_two, ("dp", "tensor"), scatter_dimension=0, tiled=True),
        lax.psum_scatter(grad_down_bias, ("dp", "tensor"), scatter_dimension=0, tiled=True),
    )
    return (
        layer_out,
        input_grad,
        small_shares[0],
        small_shares[1],
        share_qkv,
        share_qv,
        share_out,
        small_shares[2],
        small_shares[3],
        small_shares[4],
        share_up,
        share_up_bias,
        share_down,
        small_shares[5],
    )


def local_fused(zs, tokens, cotangent, norm1_gain, norm1_shift, qkv_weight, qv_bias, out_weight, out_bias,
                norm2_gain, norm2_shift, up_weight, up_bias, down_weight, down_bias):
    images = tokens.shape[0] // SEQ
    tiny = [v[None] for v in (norm1_gain, norm1_shift, out_bias, norm2_gain, norm2_shift, down_bias)]
    tiny += [qv_bias[:, 0], up_bias]
    saved = forward(
        qkv_weight, out_weight.T, up_weight, down_weight.T, tokens, cotangent, tiny, zs, images, FORWARD
    )
    dx, gq, go, gu, gd, gs = backward((saved[1],) + saved[3:], zs, images, BACKWARD)
    cell = norm1_gain.shape[0]
    return (
        saved[0], dx, gs[0, :cell], gs[1, :cell], gq, gs[6:8, None, :cell], go.T, gs[2, :cell],
        gs[3, :cell], gs[4, :cell], gu, gs[8:9, : up_bias.shape[1]], gd.T, gs[5, :cell],
    )


def solution(mesh):
    size = mesh.shape["dp"]
    zs = size // (X * Y)
    fused = size == zs * X * Y and mesh.shape["tensor"] == 2 and 768 // size == 48
    placed = (
        P(("dp", "tensor"), None),
        P(("dp", "tensor"), None),
        P(("dp", "tensor")),
        P(("dp", "tensor")),
        P(None, "dp", "tensor"),
        P(None, "tensor", "dp"),
        P("tensor", "dp"),
        P(("dp", "tensor")),
        P(("dp", "tensor")),
        P(("dp", "tensor")),
        P("dp", "tensor"),
        P("tensor", "dp"),
        P("tensor", "dp"),
        P(("dp", "tensor")),
    )
    return jax.shard_map(
        partial(local_fused, zs) if fused else local,
        mesh=mesh,
        in_specs=placed,
        out_specs=(
            P(("dp", "tensor"), None),
            P(("dp", "tensor"), None),
            P(("dp", "tensor")),
            P(("dp", "tensor")),
            P(None, "dp", "tensor"),
            P(None, "tensor", "dp"),
            P("tensor", "dp"),
            P(("dp", "tensor")),
            P(("dp", "tensor")),
            P(("dp", "tensor")),
            P("dp", "tensor"),
            P("tensor", "dp"),
            P("tensor", "dp"),
            P(("dp", "tensor")),
        ),
        check_vma=False,
    )
```

```python
import functools
from functools import partial
import jax
import jax.numpy as jnp
from jax import lax
from jax.experimental import pallas as pl
from jax.experimental.pallas import tpu as pltpu
from jax.sharding import PartitionSpec as P

MESH = pl.DeviceIdType.MESH
BF = jnp.bfloat16
F32 = jnp.float32
DMA = pltpu.SemaphoreType.DMA
HD = 64
SEQ = 197
SP = 208
QUAD = 256
EPS = 1e-06
X = Y = 2
ALL = slice(None)


def dot(a, b, ca=1, cb=0):
    return lax.dot_general(a, b, (((ca,), (cb,)), ((), ())), preferred_element_type=F32)


def remote(src, dst, send, recv, dev):
    return pltpu.make_async_remote_copy(
        src_ref=src, dst_ref=dst, send_sem=send, recv_sem=recv, device_id=dev, device_id_type=MESH
    )


def center(x):
    d = x - jnp.mean(x, axis=-1, keepdims=True)
    r = lax.rsqrt(jnp.mean(d * d, axis=-1, keepdims=True) + EPS)
    return d * r, r


def padded(v, images):
    gap = jnp.zeros((SP - SEQ, v.shape[1]), v.dtype)
    parts = []
    for i in range(images):
        parts += [v[i * SEQ : (i + 1) * SEQ], gap]
    return jnp.concatenate(parts, axis=0)


def unpadded(v, images):
    return jnp.concatenate([v[i * SP : i * SP + SEQ] for i in range(images)], axis=0)


class Place:
    def __init__(self, zs):
        dp = lax.axis_index("dp")
        self.c = c = lax.axis_index("tensor")
        self.zs = zs
        self.z = z = dp // (X * Y)
        self.y = y = (dp // X) % Y
        self.x = x = dp % X
        self.one_y, self.one_x = y + c * (1 - 2 * y), x + (1 - c) * (1 - 2 * x)
        self.two_y, self.two_x = y + (1 - c) * (1 - 2 * y), x + c * (1 - 2 * x)
        self.one = self.dev(z, self.one_y, self.one_x, c)
        self.two = self.dev(z, self.two_y, self.two_x, c)
        self.pair = self.dev(z, y, x, 1 - c)

    def dev(self, z, y, x, c):
        return {"dp": (z * Y + y) * X + x, "tensor": c}

    def zdev(self, k):
        return self.dev(lax.rem(self.z + k, self.zs), self.y, self.x, self.c)

    def greet(self):
        barrier = pltpu.get_barrier_semaphore()
        peers = [self.one, self.two, self.pair] + [self.zdev(k) for k in range(1, self.zs)]
        for peer in peers:
            pl.semaphore_signal(barrier, inc=1, device_id=peer, device_id_type=MESH)
        pl.semaphore_wait(barrier, len(peers))


def perform(plan, tasks, families, stage):
    for item in plan:
        if isinstance(item, str):
            tasks[item]()
        elif isinstance(item[0], int):
            stage(*item)
        else:
            name, first, end, marks = item

            @pl.loop(first, end)
            def _(step, name=name, marks=marks):
                families[name](step)
                for at, stages in marks:

                    @pl.when(step == at)
                    def _(stages=stages):
                        for k in stages:
                            stage(*k)


PIECES = (
    ("s", 0, 0, 128, False),
    ("a", 0, 0, 384, False),
    ("a", 1, 0, 384, False),
    ("a", 2, 0, 384, False),
    ("a", 3, 0, 384, False),
    ("b", 0, 0, 768, False),
    ("b", 0, 768, 768, False),
    ("b", 1, 0, 512, False),
    ("b", 1, 512, 512, False),
    ("b", 1, 1024, 512, True),
)
NP = len(PIECES)
HALF = {"a": 384, "b": 1536}


class Gather:
    def __init__(self, place, shards, fulls, sems):
        self.place, self.shards, self.fulls = place, shards, fulls
        self.send, self.recv, self.zs, self.zr, self.cs, self.cr, self.ls = sems

    def full(self, p, idx):
        name, m, col, width, _ = PIECES[p]
        ref = self.fulls[name]
        c = self.place.c
        if name == "s":
            return ref.at[(c,) + idx]
        cols = pl.ds(pl.multiple_of(c * HALF[name] + col, 128), width)
        return ref.at[(m,) + idx + (ALL, cols)]

    def own(self, p):
        name, m, col, width, _ = PIECES[p]
        return self.shards[name, m].at[:, pl.ds(col, width)]

    def mine(self, p):
        pp = self.place
        return self.full(p, (pp.z, pp.y, pp.x))

    def zcopy(self, p, k):
        pp = self.place
        if PIECES[p][4]:
            src = dst = self.full(p, (pp.z, ALL, ALL))
        else:
            src, dst = self.own(p), self.mine(p)
        return remote(src, dst, self.zs.at[p, k - 1], self.zr.at[p, k - 1], pp.zdev(k))

    def local(self, p):
        return pltpu.make_async_copy(self.own(p), self.mine(p), self.ls.at[p])

    def hop(self, p, kind, k):
        pp = self.place
        zz = lax.rem(pp.z - k + pp.zs, pp.zs)
        dst = self.full(p, (zz, pp.y, pp.x) if kind < 2 else (zz, pp.one_y, pp.one_x))
        src = self.own(p) if kind < 2 and k == 0 else dst
        return remote(src, dst, self.send.at[p, kind, k], self.recv.at[p, kind, k], pp.one if kind == 0 else pp.two)

    def pair(self, p):
        s = self.full(p, (ALL, ALL, ALL))
        return remote(s, s, self.cs.at[p], self.cr.at[p], self.place.pair)

    def stage(self, p, k):
        zs = self.place.zs
        plane_first = PIECES[p][4]
        if k == 0:
            if not plane_first:
                for j in range(1, zs):
                    self.zcopy(p, j).start()
            self.local(p).start()
        elif k == 5:
            self.hop(p, 0, 0).start()
            self.hop(p, 1, 0).start()
        elif plane_first:
            if k == 1:
                self.hop(p, 0, 0).wait_recv()
                self.hop(p, 2, 0).start()
            elif k == 2:
                self.local(p).wait()
                self.hop(p, 1, 0).wait_recv()
                self.hop(p, 2, 0).wait_recv()
                for j in range(1, zs):
                    self.zcopy(p, j).start()
            elif k == 3:
                for j in range(1, zs):
                    self.zcopy(p, j).wait_recv()
                self.pair(p).start()
            else:
                self.pair(p).wait_recv()
        elif k == 1:
            self.hop(p, 0, 0).wait_recv()
            self.hop(p, 2, 0).start()
            for j in range(1, zs):
                self.zcopy(p, j).wait_recv()
                self.hop(p, 0, j).start()
                self.hop(p, 1, j).start()
        elif k == 2:
            for j in range(1, zs):
                self.hop(p, 0, j).wait_recv()
                self.hop(p, 2, j).start()
        elif k == 3:
            self.local(p).wait()
            for j in range(zs):
                self.hop(p, 1, j).wait_recv()
                self.hop(p, 2, j).wait_recv()
            self.pair(p).start()
        else:
            self.pair(p).wait_recv()

    def finish(self):
        for p in range(NP):
            for k in range(1, self.place.zs):
                self.zcopy(p, k).wait_send()
            for kind in range(3):
                for k in range(1 if PIECES[p][4] else self.place.zs):
                    self.hop(p, kind, k).wait_send()
            self.pair(p).wait_send()


def forward_kernel(zs, images, plan, *refs):
    (qkv_w, out_w, up_w, dn_w, tok_r, cot_r), tiny = refs[:6], refs[6:14]
    (lo_o, vec, upb_o, wa_o, wb_o, h1t_o, qkv_o, p_o, att_o, mid_o, h2t_o, gp_o, tok_o, cot_o, gdn_o) = refs[14:29]
    (wa, wb, sv, s_sh, s_wide, h1, qkv, pbuf, att, mid, hid, gp, tok, cot, cott, h1t, gdn, psem, osem, gsem, gpsem, insem) = refs[29:51]
    sems = refs[51:]
    place = Place(zs)
    c = place.c
    n = zs * Y * X
    saves = []
    early = pltpu.make_async_copy(h1t, h1t_o, osem.at[15])
    middle = pltpu.make_async_copy(mid, mid_o, osem.at[14])
    h2 = h1

    def save(src, dst):
        copy = pltpu.make_async_copy(src, dst, osem.at[len(saves)])
        copy.start()
        saves.append(copy)

    raw = [pltpu.make_async_copy(ref, lo_o, insem.at[k]) for k, ref in enumerate((tok_r, cot_r))]
    raw[0].start()
    s_wide[...] = jnp.zeros_like(s_wide)
    row = 0
    for ref in tiny:
        value = ref[...].astype(F32)
        s_wide[row : row + value.shape[0], 0 : value.shape[1]] = value
        row += value.shape[0]
    s_sh[...] = s_wide[...].astype(BF)
    place.greet()
    shards = {("s", 0): s_sh, ("b", 0): up_w, ("b", 1): dn_w, ("a", 3): out_w}
    for t in range(3):
        shards["a", t] = qkv_w.at[t]
    g = Gather(place, shards, {"a": wa, "b": wb, "s": sv}, sems)

    def rows_of(i):
        return pl.ds(pl.multiple_of(i * SP, 16), SP)

    def cut(v):
        return v.reshape(zs, Y, X, 48, v.shape[1])

    def pad():
        raw[0].wait()
        tok[...] = padded(lo_o[...].astype(F32), images).astype(BF)
        raw[1].start()
        raw[1].wait()
        cot_f = lo_o[...].astype(F32)
        cot[...] = padded(cot_f, images).astype(BF)
        vec[16:17, :] = jnp.sum(cot_f, axis=0, keepdims=True)
        save(tok, tok_o)
        save(cot, cot_o)

    def ct():
        cott[...] = cot[...].T

    def prep():
        flat = sv[...].reshape(2 * n * 16, 128)
        cell, cell_up = 768 // (2 * n), 1536 // n
        lane = lax.broadcasted_iota(jnp.int32, (128, 768), 0)
        col = lax.rem(lax.broadcasted_iota(jnp.int32, (128, 768), 1), cell)
        spread = dot(flat, (col == lane).astype(BF)).reshape(2 * n, 16, 768)
        who = lax.broadcasted_iota(jnp.int32, (2 * n, 16, 768), 0)
        kind = lax.broadcasted_iota(jnp.int32, (2 * n, 16, 768), 1)
        spot = lax.broadcasted_iota(jnp.int32, (2 * n, 16, 768), 2) // cell
        r_of, c_of = lax.rem(who, n), who // n
        mine = jnp.where(kind < 6, 2 * r_of + c_of, n * c_of + r_of)
        vec[0:16, :] = jnp.sum(jnp.where(mine == spot, spread, 0.0), axis=0)
        row = lax.broadcasted_iota(jnp.int32, (2 * n, 2 * n * 16), 0)
        col = lax.broadcasted_iota(jnp.int32, (2 * n, 2 * n * 16), 1)
        up_rows = dot((col == row * 16 + 8).astype(BF), flat).astype(BF)
        lane = lax.broadcasted_iota(jnp.int32, (128, 3072), 0)
        col = lax.rem(lax.broadcasted_iota(jnp.int32, (128, 3072), 1), cell_up)
        spread = dot(up_rows, (col == lane).astype(BF))
        who = lax.broadcasted_iota(jnp.int32, (2 * n, 3072), 0)
        spot = lax.broadcasted_iota(jnp.int32, (2 * n, 3072), 1) // cell_up
        upb_o[...] = jnp.sum(jnp.where(who == spot, spread, 0.0), axis=0, keepdims=True)

        @pl.loop(0, images)
        def _(i):
            v, _r = center(tok[rows_of(i), :].astype(F32))
            h1[rows_of(i), :] = (v * vec[0:1, :] + vec[1:2, :]).astype(BF)

    def project(t):
        r = dot(h1[...], wa[t].reshape(768, 768))
        if t == 0:
            r = (r + vec[6:7, :]).astype(BF) * jnp.asarray(HD**-0.5, BF)
        elif t == 2:
            r = r + vec[7:8, :]
        qkv[t] = r.astype(BF)
        if t == 2:
            save(qkv, qkv_o)
            h1t[...] = h1[...].T
            early.start()

    def pcopy(step):
        return pltpu.make_async_copy(pbuf.at[step % 2], p_o.at[step], psem.at[step % 2])

    def attention(step):
        @pl.when(step >= 2)
        def _():
            pcopy(step - 2).wait()

        for j in range(3):
            cols = slice(j * QUAD, (j + 1) * QUAD)
            head = lax.broadcasted_iota(jnp.int32, (SP, QUAD), 1) // HD
            q = qkv[0, rows_of(step), cols]
            zero = jnp.zeros_like(q)
            q4 = jnp.concatenate([jnp.where(head == h, q, zero) for h in range(4)], axis=0)
            s = dot(qkv[1, rows_of(step), cols], q4, 1, 1)
            key = lax.broadcasted_iota(jnp.int32, (SP, 1), 0)
            s = jnp.where(key < SEQ, s, -jnp.inf)
            e = jnp.exp(s - jnp.max(s, axis=0, keepdims=True))
            p = (e * (1.0 / jnp.sum(e, axis=0, keepdims=True))).astype(BF)
            pbuf[step % 2, j] = p
            o4 = dot(p, qkv[2, rows_of(step), cols], 0, 0)
            o = jnp.zeros((SP, QUAD), F32)
            for h in range(4):
                o = jnp.where(head == h, o4[h * SP : (h + 1) * SP], o)
            att[rows_of(step), cols] = o.astype(BF)
        pcopy(step).start()

    def out():
        for k in (images - 2, images - 1):
            pcopy(k).wait()
        save(att, att_o)
        for j in range(3):
            w = wa[3].reshape(768, 768)[j * 256 : (j + 1) * 256, :]
            cols = slice(j * 256, (j + 1) * 256)
            mid[:, cols] = tok[:, cols].astype(F32) + (dot(att[...], w, 1, 1) + vec[2:3, cols])

        @pl.loop(0, images)
        def _(i):
            v, _r = center(mid[rows_of(i), :])
            h2[rows_of(i), :] = (v * vec[3:4, :] + vec[4:5, :]).astype(BF)

        middle.start()
        save(wa, wa_o)

    def part(piece, half):
        return pl.ds(pl.multiple_of(half * 1536 + piece * 768, 256), 768)

    def expand(step):
        cols = part(step // 2, step % 2)
        pre = dot(h2[...], wb[0, :, :, :, :, cols].reshape(768, 768)) + upb_o[:, cols]
        cdf = 0.5 + 0.5 * lax.erf(pre * (0.5**0.5))
        pdf = jnp.exp(pre * pre * -0.5) * 0.3989422804014327
        hid[:, cols] = (pre * cdf).astype(BF)
        gp[:, cols] = (cdf + pre * pdf).astype(BF)
        gpcopy(step).start()

    def gpcopy(k):
        cols = part(k // 2, k % 2)
        return pltpu.make_async_copy(gp.at[:, cols], gp_o.at[:, cols], gpsem.at[k])

    def save_up():
        save(wb.at[0], wb_o.at[0])

    def save_down(piece):
        for half in range(2):
            cols = slice(half * 1536 + piece * 512, half * 1536 + piece * 512 + 512)
            save(wb.at[1, :, :, :, :, cols], wb_o.at[1, :, :, :, :, cols])

    def gcopy(piece, own):
        return pltpu.make_async_copy(gdn.at[piece, own], gdn_o.at[piece, own], gsem.at[piece, own])

    def grad_down(step):
        piece, own = step // 2, step % 2
        cols = part(piece, 1 - own - c + 2 * own * c)
        gdn[piece, own] = cut(dot(cott[...], hid[:, cols]).astype(BF))
        gcopy(piece, own).start()

    def contract(piece):
        if piece == 0:
            middle.wait()
        for j in range(3):
            cols = slice(j * 256, (j + 1) * 256)
            total = mid[:, cols] + vec[5:6, cols] if piece == 0 else mid[:, cols]
            for half in range(2):
                fc = slice(half * 1536 + piece * 512, half * 1536 + piece * 512 + 512)
                w = wb[1, :, :, :, :, fc].reshape(768, 512)[j * 256 : (j + 1) * 256, :]
                total = total + dot(hid[:, fc], w, 1, 1)
            if piece < 2:
                mid[:, cols] = total
            else:
                lo_o[:, cols] = unpadded(total, images).astype(BF)
        if piece == 0:
            early.wait()
            h1t[...] = h2[...].T
            save(h1t, h2t_o)

    tasks = {"pad": pad, "ct": ct, "prep": prep, "out": out}
    for t in range(3):
        tasks["qkv"[t]] = functools.partial(project, t)
    for k in range(3):
        tasks[f"ct{k}"] = functools.partial(contract, k)
        tasks[f"sd{k}"] = functools.partial(save_down, k)
    tasks["su"] = save_up
    perform(plan, tasks, {"at": attention, "ex": expand, "gd": grad_down}, g.stage)
    g.finish()
    for k in range(4):
        gcopy(k // 2, k % 2).wait()
        gpcopy(k).wait()
    for copy in saves:
        copy.wait()


def forward(qkv_w, out_w, up_w, dn_w, tok, cot, tiny, zs, images, plan):
    rows = images * SP
    S = jax.ShapeDtypeStruct
    V = pltpu.VMEM
    dims = (zs, Y, X)
    outs = (
        S((images * SEQ, 768), BF), S((24, 768), F32), S((1, 3072), F32),
        S((4,) + dims + (48, 768), BF), S((2,) + dims + (48, 3072), BF), S((768, rows), BF), S((3, rows, 768), BF),
        S((images, 3, SP, 4 * SP), BF), S((rows, 768), BF), S((rows, 768), F32), S((768, rows), BF),
        S((rows, 3072), BF), S((rows, 768), BF), S((rows, 768), BF), S((2, 2) + dims + (48, 768), BF),
    )
    anys = pl.BlockSpec(memory_space=pl.ANY)
    vm = pl.BlockSpec(memory_space=pltpu.VMEM)
    return pl.pallas_call(
        functools.partial(forward_kernel, zs, images, plan),
        out_shape=outs,
        in_specs=[vm] * 4 + [anys] * 2 + [vm] * 8,
        out_specs=[vm] * 3 + [anys] * 12,
        scratch_shapes=[
            V((4,) + dims + (48, 768), BF), V((2,) + dims + (48, 3072), BF), V((2,) + dims + (16, 128), BF), V((16, 128), BF), V((16, 128), F32),
            V((rows, 768), BF), V((3, rows, 768), BF), V((2, 3, SP, 4 * SP), BF), V((rows, 768), BF), V((rows, 768), F32),
            V((rows, 3072), BF), V((rows, 3072), BF),
            V((rows, 768), BF), V((rows, 768), BF), V((768, rows), BF), V((768, rows), BF), V((2, 2) + dims + (48, 768), BF),
            DMA((2,)), DMA((16,)), DMA((2, 2)), DMA((4,)), DMA((2,)),
            DMA((NP, 3, zs)), DMA((NP, 3, zs)), DMA((NP, zs - 1)), DMA((NP, zs - 1)), DMA((NP,)), DMA((NP,)), DMA((NP,)),
        ],
        compiler_params=pltpu.CompilerParams(collective_id=1, has_side_effects=True, vmem_limit_bytes=60 * 2**20),
        name="gather_forward",
    )(qkv_w, out_w, up_w, dn_w, tok, cot, *tiny)


FORWARD = (
    (1, 0), (1, 5), (0, 0), (2, 0), (3, 0), (2, 5), (4, 0), (5, 0), (6, 0), (6, 5), (4, 5), (9, 0), (0, 5), (5, 5),
    (9, 5), "pad", (1, 1), (0, 1), (3, 5), (2, 1), "ct", (1, 2), (0, 2), (3, 1), (4, 1), (2, 2), (3, 2), (1, 3),
    (9, 1), (0, 3), (4, 2), (0, 4), (8, 0), (1, 4), (5, 1), (2, 3), (7, 0), "prep", (3, 3), (9, 2), "q", (7, 5),
    (2, 4), (4, 3), "k", (5, 2), (6, 1), (3, 4), "v", (4, 4),
    ("at", 0, 4, ((1, ((8, 5),)), (2, ((5, 3), (6, 2), (7, 1))))), "out", (5, 4),
    ("ex", 0, 2, ((0, ((7, 2), (8, 1))),)), (6, 3), ("gd", 0, 2, ()), (8, 2), (6, 4),
    ("ex", 2, 4, ((2, ((7, 3),)),)), (9, 3), ("gd", 2, 4, ((2, ((8, 3),)),)), (7, 4), "ct0", (9, 4), "sd0", "su",
    "sd2", (8, 4), "ct1", "ct2", "sd1",
)

BACKWARD = (
    "down", (0, 0), (1, 0), "rdy", ("pr", 0, 4, ((2, ((0, 1),)),)), "trn",
    ("up", 0, 4, ((0, ((2, 0), (1, 1))), (2, ((0, 2),)))), "ud", (3, 0), "dh2", "dh1", (2, 1), "dh0", (0, 3), (1, 2),
    "nm2", "og", "da", (2, 2),
    ("at", 0, 12, ((1, ((3, 1),)), (2, ((4, 0),)), (5, ((1, 3),)), (8, ((0, 4), (2, 3), (4, 1))), (9, ((3, 2),)))),
    "gq", (5, 0), "gk", (6, 0), (1, 4), (4, 2), "gv", (5, 1), (7, 0), (6, 1), (3, 3), "di0", (4, 3), "di1", (7, 1),
    (5, 2), "di2", "nm1", (6, 2), "sm", (8, 0), (5, 3), (8, 1), (7, 2), (2, 4), (6, 3), "fin", (8, 2), (3, 4),
    (7, 3), (8, 3), (4, 4), (6, 4), (5, 4), (7, 4), (8, 4),
)


SPIECES = (
    ("b", 1, 0, 768),
    ("b", 1, 768, 768),
    ("b", 0, 0, 768),
    ("b", 0, 768, 768),
    ("a", 3, 0, 384),
    ("a", 0, 0, 384),
    ("a", 1, 0, 384),
    ("a", 2, 0, 384),
    ("s", 0, 0, 128),
)
NS = len(SPIECES)


class Scatter:
    def __init__(self, place, gdn, gout, gs, wb, pb, pa, psm, rb, ra, rs, outs, sems):
        self.place = place
        self.gdn, self.gout, self.gs_, self.wb = gdn, gout, gs, wb
        self.pbuf = {"b": pb, "a": pa, "s": psm}
        self.rbuf = {"b": rb, "a": ra, "s": rs}
        self.outs = outs
        self.send, self.recv_, self.z_send, self.z_recv = sems

    def index(self, p):
        return p if p < 4 else (p - 4 if p < 8 else 0)

    def part(self, p, own):
        if p < 2:
            return self.gdn.at[p, own]
        if p < 4:
            cols = pl.ds(pl.multiple_of((p - 2) * 1536 + own * 768, 128), 768)
            return self.wb.at[1, :, :, :, :, cols]
        if p == 4:
            return self.gout.at[own]
        if p < 8:
            k = p - 5
            return self.gdn.at[k // 2, own, :, :, :, :, pl.ds((k % 2) * 384, 384)]
        return self.gs_.at[own]

    def precv(self, p):
        return self.pbuf[SPIECES[p][0]].at[self.index(p)]

    def recv(self, p, k):
        return self.rbuf[SPIECES[p][0]][k].at[self.index(p)]

    def pair(self, p):
        return remote(self.part(p, 0), self.precv(p), self.send.at[p, 0], self.recv_.at[p, 0], self.place.pair)

    def hop(self, p, k):
        pp, s = self.place, self.part(p, 1)
        y, x = ((1 - pp.y, 1 - pp.x), (pp.two_y, pp.two_x), (pp.one_y, pp.one_x))[k - 1]
        return remote(
            s.at[:, y, x], self.recv(p, k - 1), self.send.at[p, k], self.recv_.at[p, k], pp.one if k == 3 else pp.two
        )

    def three(self, p, k):
        pp, s = self.place, self.part(p, 1)
        to = lax.rem(pp.z + k, pp.zs)
        return remote(
            s.at[to, pp.y, pp.x], self.recv(p, 3).at[k - 1], self.z_send.at[p, k - 1], self.z_recv.at[p, k - 1], pp.zdev(k)
        )

    def stage(self, p, k):
        pp = self.place
        zs = pp.zs
        kind = F32 if p == 8 else BF
        s = self.part(p, 1)
        if k == 0:
            self.pair(p).start()
        elif k == 1:
            self.pair(p).wait_recv()
            r = self.precv(p)
            for zz in range(zs):
                s[zz] = (s[zz].astype(F32) + r[zz].astype(F32)).astype(kind)
            self.hop(p, 1).start()
            self.hop(p, 2).start()
        elif k == 2:
            self.hop(p, 1).wait_recv()
            r = self.recv(p, 0)
            for zz in range(zs):
                at = (zz, pp.one_y, pp.one_x)
                s[at] = (s[at].astype(F32) + r[zz].astype(F32)).astype(kind)
            self.hop(p, 3).start()
        elif k == 3:
            self.hop(p, 2).wait_recv()
            self.hop(p, 3).wait_recv()
            ra, rb = self.recv(p, 1), self.recv(p, 2)
            for zz in range(zs):
                at = (zz, pp.y, pp.x)
                s[at] = (s[at].astype(F32) + ra[zz].astype(F32) + rb[zz].astype(F32)).astype(kind)
            for k in range(1, zs):
                self.three(p, k).start()
        else:
            r = self.recv(p, 3)
            total = s[pp.z, pp.y, pp.x].astype(F32)
            for k in range(1, zs):
                self.three(p, k).wait_recv()
                total = total + r[k - 1].astype(F32)
            name, m, col, width = SPIECES[p]
            self.outs[name, m][:, pl.ds(col, width)] = total
            self.pair(p).wait_send()
            for k in range(1, 4):
                self.hop(p, k).wait_send()
            for k in range(1, zs):
                self.three(p, k).wait_send()


def backward_kernel(zs, images, plan, *refs):
    (vec, wa_i, wb_i, h1t_i, qkv_i, p_i, att_i, mid_i, h2t_i, gp_i, tok_i, cot_i, gdn_i) = refs[:13]
    dx_o, gq_o, go_o, gu_o, gd_o, gs_o = refs[13:19]
    (wa, wb, cot, qkv, att, mid, dh, dpre, db, pt, xt, yt, vg, ug, gdn, gout, gs) = refs[19:36]
    pb, pa, psm = refs[36:39]
    rb, ra, rs = refs[39:43], refs[43:47], refs[47:51]
    lsem, psem = refs[51:53]
    sems = refs[53:]
    n = zs * Y * X
    place = Place(zs)
    c = place.c
    outs = {("b", 0): gu_o, ("b", 1): gd_o, ("a", 3): go_o, ("s", 0): gs_o}
    for t in range(3):
        outs["a", t] = gq_o.at[t]
    sc = Scatter(place, gdn, gout, gs, wb, pb, pa, psm, rb, ra, rs, outs, sems)

    loads = {
        "gdn": (gdn_i, gdn), "cot": (cot_i, cot), "dn": (wb_i.at[1], wb.at[1]), "gp": (gp_i, dpre), "h2t": (h2t_i, yt),
        "up": (wb_i.at[0], wb.at[0]), "mid": (mid_i, mid), "att": (att_i, att), "wa": (wa_i, wa), "qkv": (qkv_i, qkv),
        "tok": (tok_i, cot), "h1t": (h1t_i, yt),
    }
    names = list(loads)

    def load(name):
        src, dst = loads[name]
        return pltpu.make_async_copy(src, dst, lsem.at[names.index(name)])

    for name in names[:-2]:
        load(name).start()
    place.greet()

    def rows_of(i):
        return pl.ds(pl.multiple_of(i * SP, 16), SP)

    def cut(v):
        return v.reshape(zs, Y, X, 48, v.shape[1])

    def ptile(step):
        return pltpu.make_async_copy(p_i.at[step // 3, step % 3], pt.at[step % 2], psem.at[step % 2])

    ptile(0).start()
    vg[...] = jnp.zeros_like(vg)
    vg[5:6, :] = vec[16:17, :]

    def down():
        load("gdn").wait()

    def ready():
        load("cot").wait()
        load("dn").wait()
        load("gp").wait()

    def pre(step):
        cols = pl.ds(pl.multiple_of(step * 768, 256), 768)
        w = wb[1, :, :, :, :, cols].reshape(768, 768)
        d = (dot(cot[...], w) * dpre[:, cols].astype(F32)).astype(BF)
        dpre[:, cols] = d
        ug[:, cols] = jnp.sum(d.astype(F32), axis=0, keepdims=True)

    def grad_up(step):
        piece, own = step // 2, step % 2
        half = 1 - own - c + 2 * own * c
        cols = pl.ds(pl.multiple_of(half * 1536 + piece * 768, 256), 768)
        dest = pl.ds(pl.multiple_of(step * 768, 256), 768)
        wb[1, :, :, :, :, dest] = cut(dot(yt[...], dpre[:, cols]).astype(BF))

    def turned():
        load("h2t").wait()

    def up_done():
        load("h1t").start()
        load("up").wait()

    def d_h2(j):
        w = wb[0].reshape(768, 3072)[j * 256 : (j + 1) * 256, :]
        dh[:, j * 256 : (j + 1) * 256] = dot(dpre[...], w, 1, 1)

    def norm2():
        load("mid").wait()

        @pl.loop(0, images)
        def _(i):
            v, r = center(mid[rows_of(i), :])
            g = dh[rows_of(i), :]
            vg[3:4, :] += jnp.sum(g * v, axis=0, keepdims=True)
            vg[4:5, :] += jnp.sum(g, axis=0, keepdims=True)
            dn = g * vec[3:4, :]
            d = cot[rows_of(i), :].astype(F32) + r * (
                dn - jnp.mean(dn, axis=-1, keepdims=True) - v * jnp.mean(dn * v, axis=-1, keepdims=True)
            )
            dh[rows_of(i), :] = d
            low = d.astype(BF)
            db[rows_of(i), :] = low
            vg[2:3, :] += jnp.sum(low.astype(F32), axis=0, keepdims=True)

        load("tok").start()

    def grad_out():
        xt[...] = db[...].T
        load("att").wait()
        for h in range(2):
            own = 1 - h - c + 2 * h * c
            gout[own] = cut(dot(xt[...], att[:, h * 384 : (h + 1) * 384]).astype(BF))

    def d_att():
        load("wa").wait()
        load("qkv").wait()

        @pl.loop(0, 3)
        def _(j):
            cols = pl.ds(pl.multiple_of(j * 256, 256), 256)
            att[:, cols] = dot(db[...], wa[3, :, :, :, :, cols].reshape(768, 256)).astype(BF)

    total = images * 3

    def attention(step):
        if True:
            i, j = step // 3, step % 3
            cols = pl.ds(pl.multiple_of(j * QUAD, QUAD), QUAD)
            ptile(step).wait()

            @pl.when(step + 1 < total)
            def _():
                ptile(step + 1).start()

            head = lax.broadcasted_iota(jnp.int32, (SP, QUAD), 1) // HD
            q, k, v, do = qkv[0, rows_of(i), cols], qkv[1, rows_of(i), cols], qkv[2, rows_of(i), cols], att[rows_of(i), cols]
            zero = jnp.zeros_like(q)
            q4 = jnp.concatenate([jnp.where(head == h, q, zero) for h in range(4)], axis=0)
            do4 = jnp.concatenate([jnp.where(head == h, do, zero) for h in range(4)], axis=0)
            p = pt[step % 2]
            dp = dot(v, do4, 1, 1)
            dv = dot(p, do4)
            pf = p.astype(F32)
            ds = (pf * (dp - jnp.sum(pf * dp, axis=0, keepdims=True))).astype(BF)
            dq4 = dot(ds, k, 0, 0)
            dk = dot(ds, q4)
            dq = jnp.zeros((SP, QUAD), F32)
            for h in range(4):
                dq = jnp.where(head == h, dq4[h * SP : (h + 1) * SP], dq)
            qkv[0, rows_of(i), cols] = (dq * HD**-0.5).astype(BF)
            qkv[1, rows_of(i), cols] = dk.astype(BF)
            qkv[2, rows_of(i), cols] = dv.astype(BF)

    def grad_qkv(t):
        if t == 0:
            load("h1t").wait()
        for h in range(2):
            own = 1 - h - c + 2 * h * c
            gdn[t // 2, own, :, :, :, :, (t % 2) * 384 : (t % 2) * 384 + 384] = cut(
                dot(yt[...], qkv[t, :, h * 384 : (h + 1) * 384]).astype(BF)
            )
        if t != 1:
            vg[6 + t // 2 : 7 + t // 2, :] = jnp.sum(qkv[t].astype(F32), axis=0, keepdims=True)

    def d_h1(j):
        cols = slice(j * 256, (j + 1) * 256)
        sum_ = None
        for t in range(3):
            w = wa[t].reshape(768, 768)[cols, :]
            r = dot(qkv[t], w, 1, 1)
            sum_ = r if sum_ is None else sum_ + r
        mid[:, cols] = sum_

    def norm1():
        load("tok").wait()

        @pl.loop(0, images)
        def _(i):
            v, r = center(cot[rows_of(i), :].astype(F32))
            g = mid[rows_of(i), :]
            vg[0:1, :] += jnp.sum(g * v, axis=0, keepdims=True)
            vg[1:2, :] += jnp.sum(g, axis=0, keepdims=True)
            dn = g * vec[0:1, :]
            mid[rows_of(i), :] = dh[rows_of(i), :] + r * (
                dn - jnp.mean(dn, axis=-1, keepdims=True) - v * jnp.mean(dn * v, axis=-1, keepdims=True)
            )

    def two_parts(v):
        hi = v.astype(BF)
        return hi, (v - hi.astype(F32)).astype(BF)

    def small_blocks():
        cell, cell_up = 768 // (2 * n), 1536 // n
        who = lax.broadcasted_iota(jnp.int32, (2 * n, 16, 768), 0)
        kind = lax.broadcasted_iota(jnp.int32, (2 * n, 16, 768), 1)
        spot = lax.broadcasted_iota(jnp.int32, (2 * n, 16, 768), 2) // cell
        r_of, c_of = lax.rem(who, n), who // n
        mine = jnp.where(kind < 6, 2 * r_of + c_of, n * c_of + r_of)
        mixed = jnp.where(mine == spot, vg[...][None], 0.0).reshape(2 * n * 16, 768)
        col = lax.rem(lax.broadcasted_iota(jnp.int32, (768, 128), 0), cell)
        pick = (col == lax.broadcasted_iota(jnp.int32, (768, 128), 1)).astype(BF)
        small = sum(dot(part, pick) for part in two_parts(mixed)).reshape(2 * n, 16, 128)
        who = lax.broadcasted_iota(jnp.int32, (2 * n, 3072), 0)
        spot = lax.broadcasted_iota(jnp.int32, (2 * n, 3072), 1) // cell_up
        mixed = jnp.where(who == spot, ug[...], 0.0)
        col = lax.rem(lax.broadcasted_iota(jnp.int32, (3072, 128), 0), cell_up)
        pick = (col == lax.broadcasted_iota(jnp.int32, (3072, 128), 1)).astype(BF)
        up_part = sum(dot(part, pick) for part in two_parts(mixed)).reshape(2 * n, 1, 128)
        kind = lax.broadcasted_iota(jnp.int32, (2 * n, 16, 128), 1)
        small = jnp.where(kind == 8, up_part, small).reshape(2, zs, Y, X, 16, 128)
        for h in range(2):
            gs[1 - h - c + 2 * h * c] = small[h]

    def finish():
        dx_o[...] = unpadded(mid[...], images)

    tasks = {
        "down": down, "nm2": norm2, "og": grad_out, "da": d_att, "nm1": norm1, "sm": small_blocks, "fin": finish,
        "rdy": ready, "trn": turned, "ud": up_done,
    }
    for j in range(3):
        tasks[f"dh{j}"] = functools.partial(d_h2, j)
        tasks["g" + "qkv"[j]] = functools.partial(grad_qkv, j)
        tasks[f"di{j}"] = functools.partial(d_h1, j)
    perform(plan, tasks, {"pr": pre, "up": grad_up, "at": attention}, sc.stage)


def backward(saved, zs, images, plan):
    rows = images * SP
    S = jax.ShapeDtypeStruct
    V = pltpu.VMEM
    dims = (zs, Y, X)
    anys = pl.BlockSpec(memory_space=pl.ANY)
    vm = pl.BlockSpec(memory_space=pltpu.VMEM)

    def inbox(count, rows_, width, kind):
        return [V((count, zs, rows_, width), kind)] * 3 + [V((count, zs - 1, rows_, width), kind)]

    return pl.pallas_call(
        functools.partial(backward_kernel, zs, images, plan),
        out_shape=(
            S((images * SEQ, 768), F32), S((3, 48, 384), F32), S((48, 384), F32), S((48, 1536), F32), S((48, 1536), F32), S((16, 128), F32),
        ),
        in_specs=[vm] + [anys] * 12,
        out_specs=[vm] * 6,
        scratch_shapes=[
            V((4,) + dims + (48, 768), BF), V((2,) + dims + (48, 3072), BF), V((rows, 768), BF),
            V((3, rows, 768), BF), V((rows, 768), BF), V((rows, 768), F32), V((rows, 768), F32), V((rows, 3072), BF),
            V((rows, 768), BF), V((2, SP, 4 * SP), BF), V((768, rows), BF), V((768, rows), BF),
            V((16, 768), F32), V((1, 3072), F32),
            V((2, 2) + dims + (48, 768), BF), V((2,) + dims + (48, 384), BF), V((2,) + dims + (16, 128), F32),
            V((4,) + dims + (48, 768), BF), V((4,) + dims + (48, 384), BF), V((1,) + dims + (16, 128), F32),
        ]
        + inbox(4, 48, 768, BF)
        + inbox(4, 48, 384, BF)
        + inbox(1, 16, 128, F32)
        + [
            DMA((12,)), DMA((2,)),
            DMA((NS, 4)), DMA((NS, 4)), DMA((NS, zs - 1)), DMA((NS, zs - 1)),
        ],
        compiler_params=pltpu.CompilerParams(collective_id=2, has_side_effects=True, vmem_limit_bytes=60 * 2**20),
        name="backward_scatter",
    )(*saved)


def normalize(values):
    centered = values - jnp.mean(values, axis=-1, keepdims=True)
    inverse = lax.rsqrt(jnp.mean(centered * centered, axis=-1, keepdims=True) + EPS)
    return (centered * inverse, inverse)


def norm_back(grad_out, normed, inverse, gain):
    d_normed = grad_out * gain
    grad_in = inverse * (
        d_normed
        - jnp.mean(d_normed, axis=-1, keepdims=True)
        - normed * jnp.mean(d_normed * normed, axis=-1, keepdims=True)
    )
    return (grad_in, jnp.sum(grad_out * normed, axis=0), jnp.sum(grad_out, axis=0))


def gather_rows(rows):
    return lax.all_gather(rows, "tensor", axis=0, tiled=True)


def sum_rows(terms):
    return lax.psum_scatter(
        terms.astype(jnp.bfloat16), "tensor", scatter_dimension=0, tiled=True
    ).astype(jnp.float32)


def gather_grads(rows):
    return lax.all_gather(rows, "tensor", axis=0, tiled=True)


def sum_grads(terms):
    return lax.psum_scatter(
        terms.astype(jnp.bfloat16), "tensor", scatter_dimension=0, tiled=True
    ).astype(jnp.float32)


def split_heads(matrix):
    return matrix.reshape(matrix.shape[0] // SEQ, SEQ, matrix.shape[1] // HD, HD)


def attend(queries, keys, values):
    scores = jnp.einsum(
        "iqhd,ikhd->ihqk", queries, keys, preferred_element_type=jnp.float32
    ) * HD ** (-0.5)
    row_top = jnp.max(scores, axis=-1, keepdims=True)
    shifted = jnp.exp(scores - row_top)
    row_total = jnp.sum(shifted, axis=-1, keepdims=True)
    probs = (shifted / row_total).astype(jnp.bfloat16)
    attended = jnp.einsum("ihqk,ikhd->iqhd", probs, values, preferred_element_type=jnp.float32)
    return (attended.astype(jnp.bfloat16), row_top + jnp.log(row_total))


def attend_back(queries, keys, values, log_total, d_attended):
    factor = HD ** (-0.5)
    scores = (
        jnp.einsum("iqhd,ikhd->ihqk", queries, keys, preferred_element_type=jnp.float32) * factor
    )
    probs = jnp.exp(scores - log_total)
    probs_low = probs.astype(jnp.bfloat16)
    grad_values = jnp.einsum(
        "ihqk,iqhd->ikhd", probs_low, d_attended, preferred_element_type=jnp.float32
    ).astype(jnp.bfloat16)
    d_probs = jnp.einsum("iqhd,ikhd->ihqk", d_attended, values, preferred_element_type=jnp.float32)
    d_scores = (probs * (d_probs - jnp.sum(probs * d_probs, axis=-1, keepdims=True))).astype(
        jnp.bfloat16
    )
    grad_queries = (
        jnp.einsum("ihqk,ikhd->iqhd", d_scores, keys, preferred_element_type=jnp.float32) * factor
    ).astype(jnp.bfloat16)
    grad_keys = (
        jnp.einsum("ihqk,iqhd->ikhd", d_scores, queries, preferred_element_type=jnp.float32)
        * factor
    ).astype(jnp.bfloat16)
    return (grad_queries, grad_keys, grad_values)


def local(
    tokens,
    cotangent,
    norm1_gain,
    norm1_shift,
    qkv_weight,
    qv_bias,
    out_weight,
    out_bias,
    norm2_gain,
    norm2_shift,
    up_weight,
    up_bias,
    down_weight,
    down_bias,
):
    small_full = (
        lax.all_gather(norm1_gain, ("dp", "tensor"), axis=0, tiled=True),
        lax.all_gather(norm1_shift, ("dp", "tensor"), axis=0, tiled=True),
        lax.all_gather(out_bias, ("dp", "tensor"), axis=0, tiled=True),
        lax.all_gather(norm2_gain, ("dp", "tensor"), axis=0, tiled=True),
        lax.all_gather(norm2_shift, ("dp", "tensor"), axis=0, tiled=True),
        lax.all_gather(down_bias, ("dp", "tensor"), axis=0, tiled=True),
    )
    gain_one, shift_one, out_vec, gain_two, shift_two, down_vec = [
        item.astype(jnp.float32) for item in small_full
    ]
    qkv_full, qv_full, out_full = (
        lax.all_gather(qkv_weight, "dp", axis=1, tiled=True),
        lax.all_gather(qv_bias, "dp", axis=2, tiled=True),
        lax.all_gather(out_weight, "dp", axis=1, tiled=True),
    )
    inputs = tokens.astype(jnp.float32)
    normed_one, inverse_one = normalize(inputs)
    h_one = gather_rows((normed_one * gain_one + shift_one).astype(jnp.bfloat16))
    projected = jnp.einsum("gd,tde->tge", h_one, qkv_full, preferred_element_type=jnp.float32)
    qv_rows = qv_full.astype(jnp.float32)
    queries = split_heads((projected[0] + qv_rows[0, 0]).astype(jnp.bfloat16))
    keys = split_heads(projected[1].astype(jnp.bfloat16))
    values = split_heads((projected[2] + qv_rows[1, 0]).astype(jnp.bfloat16))
    attended_heads, log_total = attend(queries, keys, values)
    group_rows = h_one.shape[0]
    attended = attended_heads.reshape(group_rows, qkv_full.shape[2])
    branch_one = sum_rows(jnp.dot(attended, out_full, preferred_element_type=jnp.float32)) + out_vec
    middle = inputs + branch_one
    up_full, up_vec, down_full = (
        lax.all_gather(up_weight, "dp", axis=0, tiled=True),
        lax.all_gather(up_bias, "dp", axis=1, tiled=True),
        lax.all_gather(down_weight, "dp", axis=1, tiled=True),
    )
    normed_two, inverse_two = normalize(middle)
    h_two = gather_rows((normed_two * gain_two + shift_two).astype(jnp.bfloat16))
    pre_act = jnp.dot(h_two, up_full, preferred_element_type=jnp.float32) + up_vec[0].astype(
        jnp.float32
    )
    hidden = jax.nn.gelu(pre_act, approximate=False).astype(jnp.bfloat16)
    branch_two = sum_rows(jnp.dot(hidden, down_full, preferred_element_type=jnp.float32)) + down_vec
    layer_out = (middle + branch_two).astype(jnp.bfloat16)
    grad_rows = cotangent.astype(jnp.float32)
    grad_down_bias = jnp.sum(grad_rows, axis=0)
    cot_all = gather_grads(cotangent)
    grad_down = jnp.einsum("gf,gd->fd", hidden, cot_all, preferred_element_type=jnp.float32)
    d_hidden = jnp.einsum("gd,fd->gf", cot_all, down_full, preferred_element_type=jnp.float32)
    gelu_out, gelu_back = jax.vjp(partial(jax.nn.gelu, approximate=False), pre_act)
    d_pre = gelu_back(d_hidden)[0].astype(jnp.bfloat16)
    grad_up_bias = jnp.sum(d_pre.astype(jnp.float32), axis=0)[None, :]
    grad_up = jnp.einsum("gd,gf->df", h_two, d_pre, preferred_element_type=jnp.float32)
    d_h_two = sum_grads(jnp.einsum("gf,df->gd", d_pre, up_full, preferred_element_type=jnp.float32))
    d_middle, grad_gain_two, grad_shift_two = norm_back(d_h_two, normed_two, inverse_two, gain_two)
    d_middle = d_middle + grad_rows
    d_branch = d_middle.astype(jnp.bfloat16)
    grad_out_bias = jnp.sum(d_branch.astype(jnp.float32), axis=0)
    branch_all = gather_grads(d_branch)
    grad_out = jnp.einsum("ge,gd->ed", attended, branch_all, preferred_element_type=jnp.float32)
    d_attended = jnp.einsum(
        "gd,ed->ge", branch_all, out_full, preferred_element_type=jnp.float32
    ).astype(jnp.bfloat16)
    grad_queries, grad_keys, grad_values = attend_back(
        queries, keys, values, log_total, split_heads(d_attended)
    )
    width = qkv_full.shape[2]
    grad_stack = jnp.stack(
        [
            grad_queries.reshape(group_rows, width),
            grad_keys.reshape(group_rows, width),
            grad_values.reshape(group_rows, width),
        ]
    )
    grad_qv = jnp.stack(
        [
            jnp.sum(grad_stack[0].astype(jnp.float32), axis=0),
            jnp.sum(grad_stack[2].astype(jnp.float32), axis=0),
        ]
    )[:, None, :]
    grad_qkv = jnp.einsum("gd,tge->tde", h_one, grad_stack, preferred_element_type=jnp.float32)
    d_h_one = sum_grads(
        jnp.einsum("tge,tde->gd", grad_stack, qkv_full, preferred_element_type=jnp.float32)
    )
    share_qkv, share_qv, share_out, share_up, share_up_bias, share_down = (
        lax.psum_scatter(grad_qkv, "dp", scatter_dimension=1, tiled=True),
        lax.psum_scatter(grad_qv, "dp", scatter_dimension=2, tiled=True),
        lax.psum_scatter(grad_out, "dp", scatter_dimension=1, tiled=True),
        lax.psum_scatter(grad_up, "dp", scatter_dimension=0, tiled=True),
        lax.psum_scatter(grad_up_bias, "dp", scatter_dimension=1, tiled=True),
        lax.psum_scatter(grad_down, "dp", scatter_dimension=1, tiled=True),
    )
    d_input, grad_gain_one, grad_shift_one = norm_back(d_h_one, normed_one, inverse_one, gain_one)
    input_grad = d_middle + d_input
    small_shares = (
        lax.psum_scatter(grad_gain_one, ("dp", "tensor"), scatter_dimension=0, tiled=True),
        lax.psum_scatter(grad_shift_one, ("dp", "tensor"), scatter_dimension=0, tiled=True),
        lax.psum_scatter(grad_out_bias, ("dp", "tensor"), scatter_dimension=0, tiled=True),
        lax.psum_scatter(grad_gain_two, ("dp", "tensor"), scatter_dimension=0, tiled=True),
        lax.psum_scatter(grad_shift_two, ("dp", "tensor"), scatter_dimension=0, tiled=True),
        lax.psum_scatter(grad_down_bias, ("dp", "tensor"), scatter_dimension=0, tiled=True),
    )
    return (
        layer_out,
        input_grad,
        small_shares[0],
        small_shares[1],
        share_qkv,
        share_qv,
        share_out,
        small_shares[2],
        small_shares[3],
        small_shares[4],
        share_up,
        share_up_bias,
        share_down,
        small_shares[5],
    )


def deliver_kernel(count, cell, cell_up, *refs):
    src, small = refs[:count], refs[count]
    dst, outs = refs[count + 1 : 2 * count + 1], refs[2 * count + 1 : 2 * count + 9]
    held, sem = refs[2 * count + 9 : -1], refs[-1]
    reads = [pltpu.make_async_copy(a, b, sem.at[0, k]) for k, (a, b) in enumerate(zip(src, held))]
    writes = [pltpu.make_async_copy(a, b, sem.at[1, k]) for k, (a, b) in enumerate(zip(held, dst))]
    for copy in reads:
        copy.start()
    for read, write in zip(reads, writes):
        read.wait()
        write.start()
    for k in range(6):
        outs[k][...] = small[k : k + 1, :cell]
    outs[6][...] = small[6:8, :cell]
    outs[7][...] = small[8:9, :cell_up]
    for write in writes:
        write.wait()


def deliver(large, small, cell, cell_up):
    S = jax.ShapeDtypeStruct
    anys = [pl.BlockSpec(memory_space=pl.ANY)] * len(large)
    vm = pl.BlockSpec(memory_space=pltpu.VMEM)
    return pl.pallas_call(
        partial(deliver_kernel, len(large), cell, cell_up),
        out_shape=[S(v.shape, v.dtype) for v in large] + [S((1, cell), F32)] * 6 + [S((2, cell), F32), S((1, cell_up), F32)],
        in_specs=anys + [vm],
        out_specs=anys + [vm] * 8,
        scratch_shapes=[pltpu.VMEM(v.shape, v.dtype) for v in large] + [DMA((2, len(large)))],
        compiler_params=pltpu.CompilerParams(vmem_limit_bytes=60 * 2**20),
        name="deliver",
    )(*large, small)


def local_fused(zs, tokens, cotangent, norm1_gain, norm1_shift, qkv_weight, qv_bias, out_weight, out_bias,
                norm2_gain, norm2_shift, up_weight, up_bias, down_weight, down_bias):
    images = tokens.shape[0] // SEQ
    tiny = [v[None] for v in (norm1_gain, norm1_shift, out_bias, norm2_gain, norm2_shift, down_bias)]
    tiny += [qv_bias[:, 0], up_bias]
    saved = forward(
        qkv_weight, out_weight.T, up_weight, down_weight.T, tokens, cotangent, tiny, zs, images, FORWARD
    )
    dx, gq, go, gu, gd, gs = backward((saved[1],) + saved[3:], zs, images, BACKWARD)
    cell = norm1_gain.shape[0]
    lo, dx, gq, go, gu, gd, *rows, gqv, gub = deliver((saved[0], dx, gq, go, gu, gd), gs, cell, up_bias.shape[1])
    small = [row[0] for row in rows]
    return (
        lo, dx, small[0], small[1], gq, gqv[:, None], go.T, small[2], small[3], small[4], gu, gub, gd.T, small[5],
    )


def solution(mesh):
    size = mesh.shape["dp"]
    zs = size // (X * Y)
    fused = size == zs * X * Y and mesh.shape["tensor"] == 2 and 768 // size == 48
    placed = (
        P(("dp", "tensor"), None),
        P(("dp", "tensor"), None),
        P(("dp", "tensor")),
        P(("dp", "tensor")),
        P(None, "dp", "tensor"),
        P(None, "tensor", "dp"),
        P("tensor", "dp"),
        P(("dp", "tensor")),
        P(("dp", "tensor")),
        P(("dp", "tensor")),
        P("dp", "tensor"),
        P("tensor", "dp"),
        P("tensor", "dp"),
        P(("dp", "tensor")),
    )
    return jax.shard_map(
        partial(local_fused, zs) if fused else local,
        mesh=mesh,
        in_specs=placed,
        out_specs=(
            P(("dp", "tensor"), None),
            P(("dp", "tensor"), None),
            P(("dp", "tensor")),
            P(("dp", "tensor")),
            P(None, "dp", "tensor"),
            P(None, "tensor", "dp"),
            P("tensor", "dp"),
            P(("dp", "tensor")),
            P(("dp", "tensor")),
            P(("dp", "tensor")),
            P("dp", "tensor"),
            P("tensor", "dp"),
            P("tensor", "dp"),
            P(("dp", "tensor")),
        ),
        check_vma=False,
    )
```

```python
import functools
from functools import partial
import jax
import jax.numpy as jnp
from jax import lax
from jax.experimental import pallas as pl
from jax.experimental.pallas import tpu as pltpu
from jax.sharding import PartitionSpec as P

MESH = pl.DeviceIdType.MESH
BF = jnp.bfloat16
F32 = jnp.float32
DMA = pltpu.SemaphoreType.DMA
HD = 64
SEQ = 197
SP = 208
QUAD = 256
EPS = 1e-06
X = Y = 2
ALL = slice(None)


def dot(a, b, ca=1, cb=0):
    return lax.dot_general(a, b, (((ca,), (cb,)), ((), ())), preferred_element_type=F32)


def remote(src, dst, send, recv, dev):
    return pltpu.make_async_remote_copy(
        src_ref=src, dst_ref=dst, send_sem=send, recv_sem=recv, device_id=dev, device_id_type=MESH
    )


def center(x):
    d = x - jnp.mean(x, axis=-1, keepdims=True)
    r = lax.rsqrt(jnp.mean(d * d, axis=-1, keepdims=True) + EPS)
    return d * r, r


def padded(v, images):
    gap = jnp.zeros((SP - SEQ, v.shape[1]), v.dtype)
    parts = []
    for i in range(images):
        parts += [v[i * SEQ : (i + 1) * SEQ], gap]
    return jnp.concatenate(parts, axis=0)


def unpadded(v, images):
    return jnp.concatenate([v[i * SP : i * SP + SEQ] for i in range(images)], axis=0)


class Place:
    def __init__(self, zs):
        dp = lax.axis_index("dp")
        self.c = c = lax.axis_index("tensor")
        self.zs = zs
        self.z = z = dp // (X * Y)
        self.y = y = (dp // X) % Y
        self.x = x = dp % X
        self.one_y, self.one_x = y + c * (1 - 2 * y), x + (1 - c) * (1 - 2 * x)
        self.two_y, self.two_x = y + (1 - c) * (1 - 2 * y), x + c * (1 - 2 * x)
        self.one = self.dev(z, self.one_y, self.one_x, c)
        self.two = self.dev(z, self.two_y, self.two_x, c)
        self.pair = self.dev(z, y, x, 1 - c)

    def dev(self, z, y, x, c):
        return {"dp": (z * Y + y) * X + x, "tensor": c}

    def zdev(self, k):
        return self.dev(lax.rem(self.z + k, self.zs), self.y, self.x, self.c)

    def greet(self):
        barrier = pltpu.get_barrier_semaphore()
        peers = [self.one, self.two, self.pair] + [self.zdev(k) for k in range(1, self.zs)]
        for peer in peers:
            pl.semaphore_signal(barrier, inc=1, device_id=peer, device_id_type=MESH)
        pl.semaphore_wait(barrier, len(peers))


def perform(plan, tasks, families, stage):
    for item in plan:
        if isinstance(item, str):
            tasks[item]()
        elif isinstance(item[0], int):
            stage(*item)
        else:
            name, first, end, marks = item

            @pl.loop(first, end)
            def _(step, name=name, marks=marks):
                families[name](step)
                for at, stages in marks:

                    @pl.when(step == at)
                    def _(stages=stages):
                        for k in stages:
                            stage(*k)


PIECES = (
    ("s", 0, 0, 128, False),
    ("a", 0, 0, 384, False),
    ("a", 1, 0, 384, False),
    ("a", 2, 0, 384, False),
    ("a", 3, 0, 384, False),
    ("b", 0, 0, 768, False),
    ("b", 0, 768, 768, False),
    ("b", 1, 0, 512, False),
    ("b", 1, 512, 512, False),
    ("b", 1, 1024, 512, True),
)
NP = len(PIECES)
HALF = {"a": 384, "b": 1536}


class Gather:
    def __init__(self, place, shards, fulls, sems):
        self.place, self.shards, self.fulls = place, shards, fulls
        self.send, self.recv, self.zs, self.zr, self.cs, self.cr, self.ls = sems

    def full(self, p, idx):
        name, m, col, width, _ = PIECES[p]
        ref = self.fulls[name]
        c = self.place.c
        if name == "s":
            return ref.at[(c,) + idx]
        cols = pl.ds(pl.multiple_of(c * HALF[name] + col, 128), width)
        return ref.at[(m,) + idx + (ALL, cols)]

    def own(self, p):
        name, m, col, width, _ = PIECES[p]
        return self.shards[name, m].at[:, pl.ds(col, width)]

    def mine(self, p):
        pp = self.place
        return self.full(p, (pp.z, pp.y, pp.x))

    def zcopy(self, p, k):
        pp = self.place
        if PIECES[p][4]:
            src = dst = self.full(p, (pp.z, ALL, ALL))
        else:
            src, dst = self.own(p), self.mine(p)
        return remote(src, dst, self.zs.at[p, k - 1], self.zr.at[p, k - 1], pp.zdev(k))

    def local(self, p):
        return pltpu.make_async_copy(self.own(p), self.mine(p), self.ls.at[p])

    def hop(self, p, kind, k):
        pp = self.place
        zz = lax.rem(pp.z - k + pp.zs, pp.zs)
        dst = self.full(p, (zz, pp.y, pp.x) if kind < 2 else (zz, pp.one_y, pp.one_x))
        src = self.own(p) if kind < 2 and k == 0 else dst
        return remote(src, dst, self.send.at[p, kind, k], self.recv.at[p, kind, k], pp.one if kind == 0 else pp.two)

    def pair(self, p):
        s = self.full(p, (ALL, ALL, ALL))
        return remote(s, s, self.cs.at[p], self.cr.at[p], self.place.pair)

    def stage(self, p, k):
        zs = self.place.zs
        plane_first = PIECES[p][4]
        if k == 0:
            if not plane_first:
                for j in range(1, zs):
                    self.zcopy(p, j).start()
            self.local(p).start()
        elif k == 5:
            self.hop(p, 0, 0).start()
            self.hop(p, 1, 0).start()
        elif plane_first:
            if k == 1:
                self.hop(p, 0, 0).wait_recv()
                self.hop(p, 2, 0).start()
            elif k == 2:
                self.local(p).wait()
                self.hop(p, 1, 0).wait_recv()
                self.hop(p, 2, 0).wait_recv()
                for j in range(1, zs):
                    self.zcopy(p, j).start()
            elif k == 3:
                for j in range(1, zs):
                    self.zcopy(p, j).wait_recv()
                self.pair(p).start()
            else:
                self.pair(p).wait_recv()
        elif k == 1:
            self.hop(p, 0, 0).wait_recv()
            self.hop(p, 2, 0).start()
            for j in range(1, zs):
                self.zcopy(p, j).wait_recv()
                self.hop(p, 0, j).start()
                self.hop(p, 1, j).start()
        elif k == 2:
            for j in range(1, zs):
                self.hop(p, 0, j).wait_recv()
                self.hop(p, 2, j).start()
        elif k == 3:
            self.local(p).wait()
            for j in range(zs):
                self.hop(p, 1, j).wait_recv()
                self.hop(p, 2, j).wait_recv()
            self.pair(p).start()
        else:
            self.pair(p).wait_recv()

    def finish(self):
        for p in range(NP):
            for k in range(1, self.place.zs):
                self.zcopy(p, k).wait_send()
            for kind in range(3):
                for k in range(1 if PIECES[p][4] else self.place.zs):
                    self.hop(p, kind, k).wait_send()
            self.pair(p).wait_send()


def forward_kernel(zs, images, plan, *refs):
    (qkv_w, out_w, up_w, dn_w, tok_r, cot_r), tiny = refs[:6], refs[6:14]
    (lo_o, vec, upb_o, wa_o, wb_o, h1t_o, qkv_o, p_o, att_o, mid_o, h2t_o, gp_o, tok_o, cot_o, gdn_o) = refs[14:29]
    (wa, wb, sv, s_sh, s_wide, h1, qkv, pbuf, att, mid, hid, gp, tok, cot, cott, h1t, gdn, psem, osem, gsem, gpsem, insem) = refs[29:51]
    sems = refs[51:]
    place = Place(zs)
    c = place.c
    n = zs * Y * X
    saves = []
    early = pltpu.make_async_copy(h1t, h1t_o, osem.at[15])
    middle = pltpu.make_async_copy(mid, mid_o, osem.at[14])
    h2 = h1

    def save(src, dst):
        copy = pltpu.make_async_copy(src, dst, osem.at[len(saves)])
        copy.start()
        saves.append(copy)

    raw = [pltpu.make_async_copy(ref, lo_o, insem.at[k]) for k, ref in enumerate((tok_r, cot_r))]
    raw[0].start()
    s_wide[...] = jnp.zeros_like(s_wide)
    row = 0
    for ref in tiny:
        value = ref[...].astype(F32)
        s_wide[row : row + value.shape[0], 0 : value.shape[1]] = value
        row += value.shape[0]
    s_sh[...] = s_wide[...].astype(BF)
    place.greet()
    shards = {("s", 0): s_sh, ("b", 0): up_w, ("b", 1): dn_w, ("a", 3): out_w}
    for t in range(3):
        shards["a", t] = qkv_w.at[t]
    g = Gather(place, shards, {"a": wa, "b": wb, "s": sv}, sems)

    def rows_of(i):
        return pl.ds(pl.multiple_of(i * SP, 16), SP)

    def cut(v):
        return v.reshape(zs, Y, X, 48, v.shape[1])

    def pad():
        raw[0].wait()
        tok[...] = padded(lo_o[...].astype(F32), images).astype(BF)
        raw[1].start()
        raw[1].wait()
        cot_f = lo_o[...].astype(F32)
        cot[...] = padded(cot_f, images).astype(BF)
        vec[16:17, :] = jnp.sum(cot_f, axis=0, keepdims=True)
        save(tok, tok_o)
        save(cot, cot_o)

    def ct():
        cott[...] = cot[...].T

    def prep():
        flat = sv[...].reshape(2 * n * 16, 128)
        cell, cell_up = 768 // (2 * n), 1536 // n
        lane = lax.broadcasted_iota(jnp.int32, (128, 768), 0)
        col = lax.rem(lax.broadcasted_iota(jnp.int32, (128, 768), 1), cell)
        spread = dot(flat, (col == lane).astype(BF)).reshape(2 * n, 16, 768)
        who = lax.broadcasted_iota(jnp.int32, (2 * n, 16, 768), 0)
        kind = lax.broadcasted_iota(jnp.int32, (2 * n, 16, 768), 1)
        spot = lax.broadcasted_iota(jnp.int32, (2 * n, 16, 768), 2) // cell
        r_of, c_of = lax.rem(who, n), who // n
        mine = jnp.where(kind < 6, 2 * r_of + c_of, n * c_of + r_of)
        vec[0:16, :] = jnp.sum(jnp.where(mine == spot, spread, 0.0), axis=0)
        row = lax.broadcasted_iota(jnp.int32, (2 * n, 2 * n * 16), 0)
        col = lax.broadcasted_iota(jnp.int32, (2 * n, 2 * n * 16), 1)
        up_rows = dot((col == row * 16 + 8).astype(BF), flat).astype(BF)
        lane = lax.broadcasted_iota(jnp.int32, (128, 3072), 0)
        col = lax.rem(lax.broadcasted_iota(jnp.int32, (128, 3072), 1), cell_up)
        spread = dot(up_rows, (col == lane).astype(BF))
        who = lax.broadcasted_iota(jnp.int32, (2 * n, 3072), 0)
        spot = lax.broadcasted_iota(jnp.int32, (2 * n, 3072), 1) // cell_up
        upb_o[...] = jnp.sum(jnp.where(who == spot, spread, 0.0), axis=0, keepdims=True)

        @pl.loop(0, images)
        def _(i):
            v, _r = center(tok[rows_of(i), :].astype(F32))
            h1[rows_of(i), :] = (v * vec[0:1, :] + vec[1:2, :]).astype(BF)

    def project(t):
        r = dot(h1[...], wa[t].reshape(768, 768))
        if t == 0:
            r = (r + vec[6:7, :]).astype(BF) * jnp.asarray(HD**-0.5, BF)
        elif t == 2:
            r = r + vec[7:8, :]
        qkv[t] = r.astype(BF)
        if t == 2:
            save(qkv, qkv_o)
            h1t[...] = h1[...].T
            early.start()

    def pcopy(step):
        return pltpu.make_async_copy(pbuf.at[step % 2], p_o.at[step], psem.at[step % 2])

    def attention(step):
        @pl.when(step >= 2)
        def _():
            pcopy(step - 2).wait()

        for j in range(3):
            cols = slice(j * QUAD, (j + 1) * QUAD)
            head = lax.broadcasted_iota(jnp.int32, (SP, QUAD), 1) // HD
            q = qkv[0, rows_of(step), cols]
            zero = jnp.zeros_like(q)
            q4 = jnp.concatenate([jnp.where(head == h, q, zero) for h in range(4)], axis=0)
            s = dot(qkv[1, rows_of(step), cols], q4, 1, 1)
            key = lax.broadcasted_iota(jnp.int32, (SP, 1), 0)
            s = jnp.where(key < SEQ, s, -jnp.inf)
            e = jnp.exp(s - jnp.max(s, axis=0, keepdims=True))
            p = (e * (1.0 / jnp.sum(e, axis=0, keepdims=True))).astype(BF)
            pbuf[step % 2, j] = p
            o4 = dot(p, qkv[2, rows_of(step), cols], 0, 0)
            o = jnp.zeros((SP, QUAD), F32)
            for h in range(4):
                o = jnp.where(head == h, o4[h * SP : (h + 1) * SP], o)
            att[rows_of(step), cols] = o.astype(BF)
        pcopy(step).start()

    def out():
        for k in (images - 2, images - 1):
            pcopy(k).wait()
        save(att, att_o)
        for j in range(3):
            w = wa[3].reshape(768, 768)[j * 256 : (j + 1) * 256, :]
            cols = slice(j * 256, (j + 1) * 256)
            mid[:, cols] = tok[:, cols].astype(F32) + (dot(att[...], w, 1, 1) + vec[2:3, cols])

        @pl.loop(0, images)
        def _(i):
            v, _r = center(mid[rows_of(i), :])
            h2[rows_of(i), :] = (v * vec[3:4, :] + vec[4:5, :]).astype(BF)

        middle.start()
        save(wa, wa_o)

    def part(piece, half):
        return pl.ds(pl.multiple_of(half * 1536 + piece * 768, 256), 768)

    def expand(step):
        cols = part(step // 2, step % 2)
        pre = dot(h2[...], wb[0, :, :, :, :, cols].reshape(768, 768)) + upb_o[:, cols]
        cdf = 0.5 + 0.5 * lax.erf(pre * (0.5**0.5))
        pdf = jnp.exp(pre * pre * -0.5) * 0.3989422804014327
        hid[:, cols] = (pre * cdf).astype(BF)
        gp[:, cols] = (cdf + pre * pdf).astype(BF)
        gpcopy(step).start()

    def gpcopy(k):
        cols = part(k // 2, k % 2)
        return pltpu.make_async_copy(gp.at[:, cols], gp_o.at[:, cols], gpsem.at[k])

    def save_up():
        save(wb.at[0], wb_o.at[0])

    def save_down(piece):
        for half in range(2):
            cols = slice(half * 1536 + piece * 512, half * 1536 + piece * 512 + 512)
            save(wb.at[1, :, :, :, :, cols], wb_o.at[1, :, :, :, :, cols])

    def gcopy(piece, own):
        return pltpu.make_async_copy(gdn.at[piece, own], gdn_o.at[piece, own], gsem.at[piece, own])

    def grad_down(step):
        piece, own = step // 2, step % 2
        cols = part(piece, 1 - own - c + 2 * own * c)
        gdn[piece, own] = cut(dot(cott[...], hid[:, cols]).astype(BF))
        gcopy(piece, own).start()

    def contract(piece):
        if piece == 0:
            middle.wait()
        for j in range(3):
            cols = slice(j * 256, (j + 1) * 256)
            total = mid[:, cols] + vec[5:6, cols] if piece == 0 else mid[:, cols]
            for half in range(2):
                fc = slice(half * 1536 + piece * 512, half * 1536 + piece * 512 + 512)
                w = wb[1, :, :, :, :, fc].reshape(768, 512)[j * 256 : (j + 1) * 256, :]
                total = total + dot(hid[:, fc], w, 1, 1)
            if piece < 2:
                mid[:, cols] = total
            else:
                lo_o[:, cols] = unpadded(total, images).astype(BF)
        if piece == 0:
            early.wait()
            h1t[...] = h2[...].T
            save(h1t, h2t_o)

    tasks = {"pad": pad, "ct": ct, "prep": prep, "out": out}
    for t in range(3):
        tasks["qkv"[t]] = functools.partial(project, t)
    for k in range(3):
        tasks[f"ct{k}"] = functools.partial(contract, k)
        tasks[f"sd{k}"] = functools.partial(save_down, k)
    tasks["su"] = save_up
    perform(plan, tasks, {"at": attention, "ex": expand, "gd": grad_down}, g.stage)
    g.finish()
    for k in range(4):
        gcopy(k // 2, k % 2).wait()
        gpcopy(k).wait()
    for copy in saves:
        copy.wait()


def forward(qkv_w, out_w, up_w, dn_w, tok, cot, tiny, zs, images, plan):
    rows = images * SP
    S = jax.ShapeDtypeStruct
    V = pltpu.VMEM
    dims = (zs, Y, X)
    outs = (
        S((images * SEQ, 768), BF), S((24, 768), F32), S((1, 3072), F32),
        S((4,) + dims + (48, 768), BF), S((2,) + dims + (48, 3072), BF), S((768, rows), BF), S((3, rows, 768), BF),
        S((images, 3, SP, 4 * SP), BF), S((rows, 768), BF), S((rows, 768), F32), S((768, rows), BF),
        S((rows, 3072), BF), S((rows, 768), BF), S((rows, 768), BF), S((2, 2) + dims + (48, 768), BF),
    )
    anys = pl.BlockSpec(memory_space=pl.ANY)
    vm = pl.BlockSpec(memory_space=pltpu.VMEM)
    return pl.pallas_call(
        functools.partial(forward_kernel, zs, images, plan),
        out_shape=outs,
        in_specs=[vm] * 4 + [anys] * 2 + [vm] * 8,
        out_specs=[vm] * 3 + [anys] * 12,
        scratch_shapes=[
            V((4,) + dims + (48, 768), BF), V((2,) + dims + (48, 3072), BF), V((2,) + dims + (16, 128), BF), V((16, 128), BF), V((16, 128), F32),
            V((rows, 768), BF), V((3, rows, 768), BF), V((2, 3, SP, 4 * SP), BF), V((rows, 768), BF), V((rows, 768), F32),
            V((rows, 3072), BF), V((rows, 3072), BF),
            V((rows, 768), BF), V((rows, 768), BF), V((768, rows), BF), V((768, rows), BF), V((2, 2) + dims + (48, 768), BF),
            DMA((2,)), DMA((16,)), DMA((2, 2)), DMA((4,)), DMA((2,)),
            DMA((NP, 3, zs)), DMA((NP, 3, zs)), DMA((NP, zs - 1)), DMA((NP, zs - 1)), DMA((NP,)), DMA((NP,)), DMA((NP,)),
        ],
        compiler_params=pltpu.CompilerParams(collective_id=1, has_side_effects=True, vmem_limit_bytes=60 * 2**20),
        name="gather_forward",
    )(qkv_w, out_w, up_w, dn_w, tok, cot, *tiny)


FORWARD = (
    (1, 0), (1, 5), (0, 0), (2, 0), (2, 5), (3, 0), (4, 0), (9, 0), (5, 0), (0, 5), (9, 5), (5, 5), (3, 5), (4, 5),
    (9, 1), (0, 1), (1, 1), (2, 1), (6, 0), (0, 2), "pad", (1, 2), (8, 0), (3, 1), (2, 2), (4, 1), (0, 3), (3, 2),
    "ct", (7, 0), (6, 5), (1, 3), (4, 2), (2, 3), (0, 4), (5, 1), "prep", (3, 3), (1, 4), (2, 4), (9, 2), "q", "k",
    (4, 3), (5, 2), (6, 1), (3, 4), "v", (4, 4), ("at", 0, 4, ((2, ((6, 2), (7, 5), (5, 3))),)), (8, 5), "out",
    (7, 1), (5, 4), ("ex", 0, 2, ((0, ((6, 3), (8, 1))),)), ("gd", 0, 2, ((0, ((7, 2),)),)), (6, 4),
    ("ex", 2, 3, ()), "su", (8, 2), ("ex", 3, 4, ()), (7, 3), (9, 3), ("gd", 2, 4, ((2, ((8, 3),)),)), (7, 4), "sd0",
    "ct0", (9, 4), "sd2", (8, 4), "ct1", "ct2", "sd1",
)

BACKWARD = (
    "down", (1, 0), (0, 0), "rdy", ("pr", 0, 4, ((2, ((1, 1),)),)), "dh0", "trn", (0, 1), "dh1", "dh2", (1, 2),
    "nm2", ("up", 0, 2, ((0, ((2, 0),)),)), (0, 2), "og", (2, 1), (4, 0), ("up", 2, 3, ()), "da",
    ("at", 0, 5, ((0, ((0, 3), (3, 0), (4, 1))), (1, ((1, 3), (2, 2))))), ("up", 3, 4, ()), "ud",
    ("at", 5, 12, ((5, ((3, 1),)), (6, ((0, 4),)), (10, ((4, 2), (2, 3))))), "gq", (5, 0), (3, 2), "gk", (6, 0),
    (1, 4), "gv", (5, 1), (4, 3), (6, 1), (7, 0), "di0", (3, 3), "di1", (5, 2), "di2", (7, 1), "nm1", (6, 2), "sm",
    (8, 0), "fin", (5, 3), (8, 1), (7, 2), (2, 4), (6, 3), (8, 2), (3, 4), (7, 3), (6, 4), (8, 3), (5, 4), (7, 4),
    (4, 4), (8, 4),
)


SPIECES = (
    ("b", 1, 0, 768),
    ("b", 1, 768, 768),
    ("b", 0, 0, 768),
    ("b", 0, 768, 768),
    ("a", 3, 0, 384),
    ("a", 0, 0, 384),
    ("a", 1, 0, 384),
    ("a", 2, 0, 384),
    ("s", 0, 0, 128),
)
NS = len(SPIECES)


class Scatter:
    def __init__(self, place, gdn, gout, gs, wb, pb, pa, psm, rb, ra, rs, outs, sems):
        self.place = place
        self.gdn, self.gout, self.gs_, self.wb = gdn, gout, gs, wb
        self.pbuf = {"b": pb, "a": pa, "s": psm}
        self.rbuf = {"b": rb, "a": ra, "s": rs}
        self.outs = outs
        self.send, self.recv_, self.z_send, self.z_recv = sems

    def index(self, p):
        return p if p < 4 else (p - 4 if p < 8 else 0)

    def part(self, p, own):
        if p < 2:
            return self.gdn.at[p, own]
        if p < 4:
            cols = pl.ds(pl.multiple_of((p - 2) * 1536 + own * 768, 128), 768)
            return self.wb.at[1, :, :, :, :, cols]
        if p == 4:
            return self.gout.at[own]
        if p < 8:
            k = p - 5
            return self.gdn.at[k // 2, own, :, :, :, :, pl.ds((k % 2) * 384, 384)]
        return self.gs_.at[own]

    def precv(self, p):
        return self.pbuf[SPIECES[p][0]].at[self.index(p)]

    def recv(self, p, k):
        return self.rbuf[SPIECES[p][0]][k].at[self.index(p)]

    def pair(self, p):
        return remote(self.part(p, 0), self.precv(p), self.send.at[p, 0], self.recv_.at[p, 0], self.place.pair)

    def hop(self, p, k):
        pp, s = self.place, self.part(p, 1)
        y, x = ((1 - pp.y, 1 - pp.x), (pp.two_y, pp.two_x), (pp.one_y, pp.one_x))[k - 1]
        return remote(
            s.at[:, y, x], self.recv(p, k - 1), self.send.at[p, k], self.recv_.at[p, k], pp.one if k == 3 else pp.two
        )

    def three(self, p, k):
        pp, s = self.place, self.part(p, 1)
        to = lax.rem(pp.z + k, pp.zs)
        return remote(
            s.at[to, pp.y, pp.x], self.recv(p, 3).at[k - 1], self.z_send.at[p, k - 1], self.z_recv.at[p, k - 1], pp.zdev(k)
        )

    def stage(self, p, k):
        pp = self.place
        zs = pp.zs
        kind = F32 if p == 8 else BF
        s = self.part(p, 1)
        if k == 0:
            self.pair(p).start()
        elif k == 1:
            self.pair(p).wait_recv()
            r = self.precv(p)
            for zz in range(zs):
                s[zz] = (s[zz].astype(F32) + r[zz].astype(F32)).astype(kind)
            self.hop(p, 1).start()
            self.hop(p, 2).start()
        elif k == 2:
            self.hop(p, 1).wait_recv()
            r = self.recv(p, 0)
            for zz in range(zs):
                at = (zz, pp.one_y, pp.one_x)
                s[at] = (s[at].astype(F32) + r[zz].astype(F32)).astype(kind)
            self.hop(p, 3).start()
        elif k == 3:
            self.hop(p, 2).wait_recv()
            self.hop(p, 3).wait_recv()
            ra, rb = self.recv(p, 1), self.recv(p, 2)
            for zz in range(zs):
                at = (zz, pp.y, pp.x)
                s[at] = (s[at].astype(F32) + ra[zz].astype(F32) + rb[zz].astype(F32)).astype(kind)
            for k in range(1, zs):
                self.three(p, k).start()
        else:
            r = self.recv(p, 3)
            total = s[pp.z, pp.y, pp.x].astype(F32)
            for k in range(1, zs):
                self.three(p, k).wait_recv()
                total = total + r[k - 1].astype(F32)
            name, m, col, width = SPIECES[p]
            self.outs[name, m][:, pl.ds(col, width)] = total
            self.pair(p).wait_send()
            for k in range(1, 4):
                self.hop(p, k).wait_send()
            for k in range(1, zs):
                self.three(p, k).wait_send()


def backward_kernel(zs, images, plan, *refs):
    (vec, wa_i, wb_i, h1t_i, qkv_i, p_i, att_i, mid_i, h2t_i, gp_i, tok_i, cot_i, gdn_i) = refs[:13]
    dx_o, gq_o, go_o, gu_o, gd_o, gs_o = refs[13:19]
    (wa, wb, cot, qkv, att, mid, dh, dpre, db, pt, xt, yt, vg, ug, gdn, gout, gs) = refs[19:36]
    pb, pa, psm = refs[36:39]
    rb, ra, rs = refs[39:43], refs[43:47], refs[47:51]
    lsem, psem = refs[51:53]
    sems = refs[53:]
    n = zs * Y * X
    place = Place(zs)
    c = place.c
    outs = {("b", 0): gu_o, ("b", 1): gd_o, ("a", 3): go_o, ("s", 0): gs_o}
    for t in range(3):
        outs["a", t] = gq_o.at[t]
    sc = Scatter(place, gdn, gout, gs, wb, pb, pa, psm, rb, ra, rs, outs, sems)

    loads = {
        "gdn": (gdn_i, gdn), "cot": (cot_i, cot), "dn": (wb_i.at[1], wb.at[1]), "gp": (gp_i, dpre), "h2t": (h2t_i, yt),
        "up": (wb_i.at[0], wb.at[0]), "mid": (mid_i, mid), "att": (att_i, att), "wa": (wa_i, wa), "qkv": (qkv_i, qkv),
        "tok": (tok_i, cot), "h1t": (h1t_i, yt),
    }
    names = list(loads)

    def load(name):
        src, dst = loads[name]
        return pltpu.make_async_copy(src, dst, lsem.at[names.index(name)])

    for name in names[:-2]:
        load(name).start()
    place.greet()

    def rows_of(i):
        return pl.ds(pl.multiple_of(i * SP, 16), SP)

    def cut(v):
        return v.reshape(zs, Y, X, 48, v.shape[1])

    def ptile(step):
        return pltpu.make_async_copy(p_i.at[step // 3, step % 3], pt.at[step % 2], psem.at[step % 2])

    ptile(0).start()
    vg[...] = jnp.zeros_like(vg)
    vg[5:6, :] = vec[16:17, :]

    def down():
        load("gdn").wait()

    def ready():
        load("cot").wait()
        load("dn").wait()
        load("gp").wait()

    def pre(step):
        cols = pl.ds(pl.multiple_of(step * 768, 256), 768)
        w = wb[1, :, :, :, :, cols].reshape(768, 768)
        d = (dot(cot[...], w) * dpre[:, cols].astype(F32)).astype(BF)
        dpre[:, cols] = d
        ug[:, cols] = jnp.sum(d.astype(F32), axis=0, keepdims=True)

    def grad_up(step):
        piece, own = step // 2, step % 2
        half = 1 - own - c + 2 * own * c
        cols = pl.ds(pl.multiple_of(half * 1536 + piece * 768, 256), 768)
        dest = pl.ds(pl.multiple_of(step * 768, 256), 768)
        wb[1, :, :, :, :, dest] = cut(dot(yt[...], dpre[:, cols]).astype(BF))

    def turned():
        load("h2t").wait()

    def up_done():
        load("h1t").start()

    def d_h2(j):
        if j == 0:
            load("up").wait()
        w = wb[0].reshape(768, 3072)[j * 256 : (j + 1) * 256, :]
        dh[:, j * 256 : (j + 1) * 256] = dot(dpre[...], w, 1, 1)

    def norm2():
        load("mid").wait()

        @pl.loop(0, images)
        def _(i):
            v, r = center(mid[rows_of(i), :])
            g = dh[rows_of(i), :]
            vg[3:4, :] += jnp.sum(g * v, axis=0, keepdims=True)
            vg[4:5, :] += jnp.sum(g, axis=0, keepdims=True)
            dn = g * vec[3:4, :]
            d = cot[rows_of(i), :].astype(F32) + r * (
                dn - jnp.mean(dn, axis=-1, keepdims=True) - v * jnp.mean(dn * v, axis=-1, keepdims=True)
            )
            dh[rows_of(i), :] = d
            low = d.astype(BF)
            db[rows_of(i), :] = low
            vg[2:3, :] += jnp.sum(low.astype(F32), axis=0, keepdims=True)

        load("tok").start()

    def grad_out():
        xt[...] = db[...].T
        load("att").wait()
        both = dot(xt[...], att[...]).astype(BF)
        for h in range(2):
            gout[1 - h - c + 2 * h * c] = cut(both[:, h * 384 : (h + 1) * 384])

    def d_att():
        load("wa").wait()
        load("qkv").wait()

        att[...] = dot(db[...], wa[3].reshape(768, 768)).astype(BF)

    total = images * 3

    def attention(step):
        if True:
            i, j = step // 3, step % 3
            cols = pl.ds(pl.multiple_of(j * QUAD, QUAD), QUAD)
            ptile(step).wait()

            @pl.when(step + 1 < total)
            def _():
                ptile(step + 1).start()

            head = lax.broadcasted_iota(jnp.int32, (SP, QUAD), 1) // HD
            q, k, v, do = qkv[0, rows_of(i), cols], qkv[1, rows_of(i), cols], qkv[2, rows_of(i), cols], att[rows_of(i), cols]
            zero = jnp.zeros_like(q)
            q4 = jnp.concatenate([jnp.where(head == h, q, zero) for h in range(4)], axis=0)
            do4 = jnp.concatenate([jnp.where(head == h, do, zero) for h in range(4)], axis=0)
            p = pt[step % 2]
            dp = dot(v, do4, 1, 1)
            dv = dot(p, do4)
            pf = p.astype(F32)
            ds = (pf * (dp - jnp.sum(pf * dp, axis=0, keepdims=True))).astype(BF)
            dq4 = dot(ds, k, 0, 0)
            dk = dot(ds, q4)
            dq = jnp.zeros((SP, QUAD), F32)
            for h in range(4):
                dq = jnp.where(head == h, dq4[h * SP : (h + 1) * SP], dq)
            qkv[0, rows_of(i), cols] = (dq * HD**-0.5).astype(BF)
            qkv[1, rows_of(i), cols] = dk.astype(BF)
            qkv[2, rows_of(i), cols] = dv.astype(BF)

    def grad_qkv(t):
        if t == 0:
            load("h1t").wait()
        both = dot(yt[...], qkv[t]).astype(BF)
        for h in range(2):
            cols = slice((t % 2) * 384, (t % 2) * 384 + 384)
            gdn[t // 2, 1 - h - c + 2 * h * c, :, :, :, :, cols] = cut(both[:, h * 384 : (h + 1) * 384])
        if t != 1:
            vg[6 + t // 2 : 7 + t // 2, :] = jnp.sum(qkv[t].astype(F32), axis=0, keepdims=True)

    def d_h1(j):
        cols = slice(j * 256, (j + 1) * 256)
        sum_ = None
        for t in range(3):
            w = wa[t].reshape(768, 768)[cols, :]
            r = dot(qkv[t], w, 1, 1)
            sum_ = r if sum_ is None else sum_ + r
        mid[:, cols] = sum_

    def norm1():
        load("tok").wait()

        @pl.loop(0, images)
        def _(i):
            v, r = center(cot[rows_of(i), :].astype(F32))
            g = mid[rows_of(i), :]
            vg[0:1, :] += jnp.sum(g * v, axis=0, keepdims=True)
            vg[1:2, :] += jnp.sum(g, axis=0, keepdims=True)
            dn = g * vec[0:1, :]
            mid[rows_of(i), :] = dh[rows_of(i), :] + r * (
                dn - jnp.mean(dn, axis=-1, keepdims=True) - v * jnp.mean(dn * v, axis=-1, keepdims=True)
            )

    def two_parts(v):
        hi = v.astype(BF)
        return hi, (v - hi.astype(F32)).astype(BF)

    def small_blocks():
        cell, cell_up = 768 // (2 * n), 1536 // n
        who = lax.broadcasted_iota(jnp.int32, (2 * n, 16, 768), 0)
        kind = lax.broadcasted_iota(jnp.int32, (2 * n, 16, 768), 1)
        spot = lax.broadcasted_iota(jnp.int32, (2 * n, 16, 768), 2) // cell
        r_of, c_of = lax.rem(who, n), who // n
        mine = jnp.where(kind < 6, 2 * r_of + c_of, n * c_of + r_of)
        mixed = jnp.where(mine == spot, vg[...][None], 0.0).reshape(2 * n * 16, 768)
        col = lax.rem(lax.broadcasted_iota(jnp.int32, (768, 128), 0), cell)
        pick = (col == lax.broadcasted_iota(jnp.int32, (768, 128), 1)).astype(BF)
        small = sum(dot(part, pick) for part in two_parts(mixed)).reshape(2 * n, 16, 128)
        who = lax.broadcasted_iota(jnp.int32, (2 * n, 3072), 0)
        spot = lax.broadcasted_iota(jnp.int32, (2 * n, 3072), 1) // cell_up
        mixed = jnp.where(who == spot, ug[...], 0.0)
        col = lax.rem(lax.broadcasted_iota(jnp.int32, (3072, 128), 0), cell_up)
        pick = (col == lax.broadcasted_iota(jnp.int32, (3072, 128), 1)).astype(BF)
        up_part = sum(dot(part, pick) for part in two_parts(mixed)).reshape(2 * n, 1, 128)
        kind = lax.broadcasted_iota(jnp.int32, (2 * n, 16, 128), 1)
        small = jnp.where(kind == 8, up_part, small).reshape(2, zs, Y, X, 16, 128)
        for h in range(2):
            gs[1 - h - c + 2 * h * c] = small[h]

    def finish():
        dx_o[...] = unpadded(mid[...], images)

    tasks = {
        "down": down, "nm2": norm2, "og": grad_out, "da": d_att, "nm1": norm1, "sm": small_blocks, "fin": finish,
        "rdy": ready, "trn": turned, "ud": up_done,
    }
    for j in range(3):
        tasks[f"dh{j}"] = functools.partial(d_h2, j)
        tasks["g" + "qkv"[j]] = functools.partial(grad_qkv, j)
        tasks[f"di{j}"] = functools.partial(d_h1, j)
    perform(plan, tasks, {"pr": pre, "up": grad_up, "at": attention}, sc.stage)


def backward(saved, zs, images, plan):
    rows = images * SP
    S = jax.ShapeDtypeStruct
    V = pltpu.VMEM
    dims = (zs, Y, X)
    anys = pl.BlockSpec(memory_space=pl.ANY)
    vm = pl.BlockSpec(memory_space=pltpu.VMEM)

    def inbox(count, rows_, width, kind):
        return [V((count, zs, rows_, width), kind)] * 3 + [V((count, zs - 1, rows_, width), kind)]

    return pl.pallas_call(
        functools.partial(backward_kernel, zs, images, plan),
        out_shape=(
            S((images * SEQ, 768), F32), S((3, 48, 384), F32), S((48, 384), F32), S((48, 1536), F32), S((48, 1536), F32), S((16, 128), F32),
        ),
        in_specs=[vm] + [anys] * 12,
        out_specs=[vm] * 6,
        scratch_shapes=[
            V((4,) + dims + (48, 768), BF), V((2,) + dims + (48, 3072), BF), V((rows, 768), BF),
            V((3, rows, 768), BF), V((rows, 768), BF), V((rows, 768), F32), V((rows, 768), F32), V((rows, 3072), BF),
            V((rows, 768), BF), V((2, SP, 4 * SP), BF), V((768, rows), BF), V((768, rows), BF),
            V((16, 768), F32), V((1, 3072), F32),
            V((2, 2) + dims + (48, 768), BF), V((2,) + dims + (48, 384), BF), V((2,) + dims + (16, 128), F32),
            V((4,) + dims + (48, 768), BF), V((4,) + dims + (48, 384), BF), V((1,) + dims + (16, 128), F32),
        ]
        + inbox(4, 48, 768, BF)
        + inbox(4, 48, 384, BF)
        + inbox(1, 16, 128, F32)
        + [
            DMA((12,)), DMA((2,)),
            DMA((NS, 4)), DMA((NS, 4)), DMA((NS, zs - 1)), DMA((NS, zs - 1)),
        ],
        compiler_params=pltpu.CompilerParams(collective_id=2, has_side_effects=True, vmem_limit_bytes=60 * 2**20),
        name="backward_scatter",
    )(*saved)


def normalize(values):
    centered = values - jnp.mean(values, axis=-1, keepdims=True)
    inverse = lax.rsqrt(jnp.mean(centered * centered, axis=-1, keepdims=True) + EPS)
    return (centered * inverse, inverse)


def norm_back(grad_out, normed, inverse, gain):
    d_normed = grad_out * gain
    grad_in = inverse * (
        d_normed
        - jnp.mean(d_normed, axis=-1, keepdims=True)
        - normed * jnp.mean(d_normed * normed, axis=-1, keepdims=True)
    )
    return (grad_in, jnp.sum(grad_out * normed, axis=0), jnp.sum(grad_out, axis=0))


def gather_rows(rows):
    return lax.all_gather(rows, "tensor", axis=0, tiled=True)


def sum_rows(terms):
    return lax.psum_scatter(
        terms.astype(jnp.bfloat16), "tensor", scatter_dimension=0, tiled=True
    ).astype(jnp.float32)


def gather_grads(rows):
    return lax.all_gather(rows, "tensor", axis=0, tiled=True)


def sum_grads(terms):
    return lax.psum_scatter(
        terms.astype(jnp.bfloat16), "tensor", scatter_dimension=0, tiled=True
    ).astype(jnp.float32)


def split_heads(matrix):
    return matrix.reshape(matrix.shape[0] // SEQ, SEQ, matrix.shape[1] // HD, HD)


def attend(queries, keys, values):
    scores = jnp.einsum(
        "iqhd,ikhd->ihqk", queries, keys, preferred_element_type=jnp.float32
    ) * HD ** (-0.5)
    row_top = jnp.max(scores, axis=-1, keepdims=True)
    shifted = jnp.exp(scores - row_top)
    row_total = jnp.sum(shifted, axis=-1, keepdims=True)
    probs = (shifted / row_total).astype(jnp.bfloat16)
    attended = jnp.einsum("ihqk,ikhd->iqhd", probs, values, preferred_element_type=jnp.float32)
    return (attended.astype(jnp.bfloat16), row_top + jnp.log(row_total))


def attend_back(queries, keys, values, log_total, d_attended):
    factor = HD ** (-0.5)
    scores = (
        jnp.einsum("iqhd,ikhd->ihqk", queries, keys, preferred_element_type=jnp.float32) * factor
    )
    probs = jnp.exp(scores - log_total)
    probs_low = probs.astype(jnp.bfloat16)
    grad_values = jnp.einsum(
        "ihqk,iqhd->ikhd", probs_low, d_attended, preferred_element_type=jnp.float32
    ).astype(jnp.bfloat16)
    d_probs = jnp.einsum("iqhd,ikhd->ihqk", d_attended, values, preferred_element_type=jnp.float32)
    d_scores = (probs * (d_probs - jnp.sum(probs * d_probs, axis=-1, keepdims=True))).astype(
        jnp.bfloat16
    )
    grad_queries = (
        jnp.einsum("ihqk,ikhd->iqhd", d_scores, keys, preferred_element_type=jnp.float32) * factor
    ).astype(jnp.bfloat16)
    grad_keys = (
        jnp.einsum("ihqk,iqhd->ikhd", d_scores, queries, preferred_element_type=jnp.float32)
        * factor
    ).astype(jnp.bfloat16)
    return (grad_queries, grad_keys, grad_values)


def local(
    tokens,
    cotangent,
    norm1_gain,
    norm1_shift,
    qkv_weight,
    qv_bias,
    out_weight,
    out_bias,
    norm2_gain,
    norm2_shift,
    up_weight,
    up_bias,
    down_weight,
    down_bias,
):
    small_full = (
        lax.all_gather(norm1_gain, ("dp", "tensor"), axis=0, tiled=True),
        lax.all_gather(norm1_shift, ("dp", "tensor"), axis=0, tiled=True),
        lax.all_gather(out_bias, ("dp", "tensor"), axis=0, tiled=True),
        lax.all_gather(norm2_gain, ("dp", "tensor"), axis=0, tiled=True),
        lax.all_gather(norm2_shift, ("dp", "tensor"), axis=0, tiled=True),
        lax.all_gather(down_bias, ("dp", "tensor"), axis=0, tiled=True),
    )
    gain_one, shift_one, out_vec, gain_two, shift_two, down_vec = [
        item.astype(jnp.float32) for item in small_full
    ]
    qkv_full, qv_full, out_full = (
        lax.all_gather(qkv_weight, "dp", axis=1, tiled=True),
        lax.all_gather(qv_bias, "dp", axis=2, tiled=True),
        lax.all_gather(out_weight, "dp", axis=1, tiled=True),
    )
    inputs = tokens.astype(jnp.float32)
    normed_one, inverse_one = normalize(inputs)
    h_one = gather_rows((normed_one * gain_one + shift_one).astype(jnp.bfloat16))
    projected = jnp.einsum("gd,tde->tge", h_one, qkv_full, preferred_element_type=jnp.float32)
    qv_rows = qv_full.astype(jnp.float32)
    queries = split_heads((projected[0] + qv_rows[0, 0]).astype(jnp.bfloat16))
    keys = split_heads(projected[1].astype(jnp.bfloat16))
    values = split_heads((projected[2] + qv_rows[1, 0]).astype(jnp.bfloat16))
    attended_heads, log_total = attend(queries, keys, values)
    group_rows = h_one.shape[0]
    attended = attended_heads.reshape(group_rows, qkv_full.shape[2])
    branch_one = sum_rows(jnp.dot(attended, out_full, preferred_element_type=jnp.float32)) + out_vec
    middle = inputs + branch_one
    up_full, up_vec, down_full = (
        lax.all_gather(up_weight, "dp", axis=0, tiled=True),
        lax.all_gather(up_bias, "dp", axis=1, tiled=True),
        lax.all_gather(down_weight, "dp", axis=1, tiled=True),
    )
    normed_two, inverse_two = normalize(middle)
    h_two = gather_rows((normed_two * gain_two + shift_two).astype(jnp.bfloat16))
    pre_act = jnp.dot(h_two, up_full, preferred_element_type=jnp.float32) + up_vec[0].astype(
        jnp.float32
    )
    hidden = jax.nn.gelu(pre_act, approximate=False).astype(jnp.bfloat16)
    branch_two = sum_rows(jnp.dot(hidden, down_full, preferred_element_type=jnp.float32)) + down_vec
    layer_out = (middle + branch_two).astype(jnp.bfloat16)
    grad_rows = cotangent.astype(jnp.float32)
    grad_down_bias = jnp.sum(grad_rows, axis=0)
    cot_all = gather_grads(cotangent)
    grad_down = jnp.einsum("gf,gd->fd", hidden, cot_all, preferred_element_type=jnp.float32)
    d_hidden = jnp.einsum("gd,fd->gf", cot_all, down_full, preferred_element_type=jnp.float32)
    gelu_out, gelu_back = jax.vjp(partial(jax.nn.gelu, approximate=False), pre_act)
    d_pre = gelu_back(d_hidden)[0].astype(jnp.bfloat16)
    grad_up_bias = jnp.sum(d_pre.astype(jnp.float32), axis=0)[None, :]
    grad_up = jnp.einsum("gd,gf->df", h_two, d_pre, preferred_element_type=jnp.float32)
    d_h_two = sum_grads(jnp.einsum("gf,df->gd", d_pre, up_full, preferred_element_type=jnp.float32))
    d_middle, grad_gain_two, grad_shift_two = norm_back(d_h_two, normed_two, inverse_two, gain_two)
    d_middle = d_middle + grad_rows
    d_branch = d_middle.astype(jnp.bfloat16)
    grad_out_bias = jnp.sum(d_branch.astype(jnp.float32), axis=0)
    branch_all = gather_grads(d_branch)
    grad_out = jnp.einsum("ge,gd->ed", attended, branch_all, preferred_element_type=jnp.float32)
    d_attended = jnp.einsum(
        "gd,ed->ge", branch_all, out_full, preferred_element_type=jnp.float32
    ).astype(jnp.bfloat16)
    grad_queries, grad_keys, grad_values = attend_back(
        queries, keys, values, log_total, split_heads(d_attended)
    )
    width = qkv_full.shape[2]
    grad_stack = jnp.stack(
        [
            grad_queries.reshape(group_rows, width),
            grad_keys.reshape(group_rows, width),
            grad_values.reshape(group_rows, width),
        ]
    )
    grad_qv = jnp.stack(
        [
            jnp.sum(grad_stack[0].astype(jnp.float32), axis=0),
            jnp.sum(grad_stack[2].astype(jnp.float32), axis=0),
        ]
    )[:, None, :]
    grad_qkv = jnp.einsum("gd,tge->tde", h_one, grad_stack, preferred_element_type=jnp.float32)
    d_h_one = sum_grads(
        jnp.einsum("tge,tde->gd", grad_stack, qkv_full, preferred_element_type=jnp.float32)
    )
    share_qkv, share_qv, share_out, share_up, share_up_bias, share_down = (
        lax.psum_scatter(grad_qkv, "dp", scatter_dimension=1, tiled=True),
        lax.psum_scatter(grad_qv, "dp", scatter_dimension=2, tiled=True),
        lax.psum_scatter(grad_out, "dp", scatter_dimension=1, tiled=True),
        lax.psum_scatter(grad_up, "dp", scatter_dimension=0, tiled=True),
        lax.psum_scatter(grad_up_bias, "dp", scatter_dimension=1, tiled=True),
        lax.psum_scatter(grad_down, "dp", scatter_dimension=1, tiled=True),
    )
    d_input, grad_gain_one, grad_shift_one = norm_back(d_h_one, normed_one, inverse_one, gain_one)
    input_grad = d_middle + d_input
    small_shares = (
        lax.psum_scatter(grad_gain_one, ("dp", "tensor"), scatter_dimension=0, tiled=True),
        lax.psum_scatter(grad_shift_one, ("dp", "tensor"), scatter_dimension=0, tiled=True),
        lax.psum_scatter(grad_out_bias, ("dp", "tensor"), scatter_dimension=0, tiled=True),
        lax.psum_scatter(grad_gain_two, ("dp", "tensor"), scatter_dimension=0, tiled=True),
        lax.psum_scatter(grad_shift_two, ("dp", "tensor"), scatter_dimension=0, tiled=True),
        lax.psum_scatter(grad_down_bias, ("dp", "tensor"), scatter_dimension=0, tiled=True),
    )
    return (
        layer_out,
        input_grad,
        small_shares[0],
        small_shares[1],
        share_qkv,
        share_qv,
        share_out,
        small_shares[2],
        small_shares[3],
        small_shares[4],
        share_up,
        share_up_bias,
        share_down,
        small_shares[5],
    )


def deliver_kernel(count, cell, cell_up, *refs):
    src, small = refs[:count], refs[count]
    dst, outs = refs[count + 1 : 2 * count + 1], refs[2 * count + 1 : 2 * count + 9]
    held, sem = refs[2 * count + 9 : -1], refs[-1]
    reads = [pltpu.make_async_copy(a, b, sem.at[0, k]) for k, (a, b) in enumerate(zip(src, held))]
    writes = [pltpu.make_async_copy(a, b, sem.at[1, k]) for k, (a, b) in enumerate(zip(held, dst))]
    for copy in reads:
        copy.start()
    for read, write in zip(reads, writes):
        read.wait()
        write.start()
    for k in range(6):
        outs[k][...] = small[k : k + 1, :cell]
    outs[6][...] = small[6:8, :cell]
    outs[7][...] = small[8:9, :cell_up]
    for write in writes:
        write.wait()


def deliver(large, small, cell, cell_up):
    S = jax.ShapeDtypeStruct
    anys = [pl.BlockSpec(memory_space=pl.ANY)] * len(large)
    vm = pl.BlockSpec(memory_space=pltpu.VMEM)
    return pl.pallas_call(
        partial(deliver_kernel, len(large), cell, cell_up),
        out_shape=[S(v.shape, v.dtype) for v in large] + [S((1, cell), F32)] * 6 + [S((2, cell), F32), S((1, cell_up), F32)],
        in_specs=anys + [vm],
        out_specs=anys + [vm] * 8,
        scratch_shapes=[pltpu.VMEM(v.shape, v.dtype) for v in large] + [DMA((2, len(large)))],
        compiler_params=pltpu.CompilerParams(vmem_limit_bytes=60 * 2**20),
        name="deliver",
    )(*large, small)


def local_fused(zs, tokens, cotangent, norm1_gain, norm1_shift, qkv_weight, qv_bias, out_weight, out_bias,
                norm2_gain, norm2_shift, up_weight, up_bias, down_weight, down_bias):
    images = tokens.shape[0] // SEQ
    tiny = [v[None] for v in (norm1_gain, norm1_shift, out_bias, norm2_gain, norm2_shift, down_bias)]
    tiny += [qv_bias[:, 0], up_bias]
    saved = forward(
        qkv_weight, out_weight.T, up_weight, down_weight.T, tokens, cotangent, tiny, zs, images, FORWARD
    )
    dx, gq, go, gu, gd, gs = backward((saved[1],) + saved[3:], zs, images, BACKWARD)
    cell = norm1_gain.shape[0]
    lo, dx, gq, go, gu, gd, *rows, gqv, gub = deliver((saved[0], dx, gq, go, gu, gd), gs, cell, up_bias.shape[1])
    small = [row[0] for row in rows]
    return (
        lo, dx, small[0], small[1], gq, gqv[:, None], go.T, small[2], small[3], small[4], gu, gub, gd.T, small[5],
    )


def solution(mesh):
    size = mesh.shape["dp"]
    zs = size // (X * Y)
    fused = size == zs * X * Y and mesh.shape["tensor"] == 2 and 768 // size == 48
    placed = (
        P(("dp", "tensor"), None),
        P(("dp", "tensor"), None),
        P(("dp", "tensor")),
        P(("dp", "tensor")),
        P(None, "dp", "tensor"),
        P(None, "tensor", "dp"),
        P("tensor", "dp"),
        P(("dp", "tensor")),
        P(("dp", "tensor")),
        P(("dp", "tensor")),
        P("dp", "tensor"),
        P("tensor", "dp"),
        P("tensor", "dp"),
        P(("dp", "tensor")),
    )
    return jax.shard_map(
        partial(local_fused, zs) if fused else local,
        mesh=mesh,
        in_specs=placed,
        out_specs=(
            P(("dp", "tensor"), None),
            P(("dp", "tensor"), None),
            P(("dp", "tensor")),
            P(("dp", "tensor")),
            P(None, "dp", "tensor"),
            P(None, "tensor", "dp"),
            P("tensor", "dp"),
            P(("dp", "tensor")),
            P(("dp", "tensor")),
            P(("dp", "tensor")),
            P("dp", "tensor"),
            P("tensor", "dp"),
            P("tensor", "dp"),
            P(("dp", "tensor")),
        ),
        check_vma=False,
    )
```
